32 devices in a mesh: expert: 2 (over y), context: 4 (over x, core), dp: 4 (over z).
Axes of the slice: x: 2, y: 2, z: 4, core: 2. Of those that a mesh axis runs over, the one named last changes fastest.
Arguments:
- tokens: bfloat16 [8, 512, 2048], P(('expert', 'dp'), 'context'), may hold values from -6 to 6
- cotangent: float32 [8, 512, 2048], P(('expert', 'dp'), 'context'), may hold values from -6 to 6
- w_attn: float32 [2048, 8192], P(('expert', 'context', 'dp'))
- w_router: float32 [2048, 16], P(('expert', 'context', 'dp')), may hold values from -0.0625 to 0.0625
- norm_gains: float32 [4, 2048], P(None, ('expert', 'context', 'dp')), may hold values from 0.5 to 1.5
- w_experts: float32 [2048, 16, 3072], P('dp', ('expert', 'context'))
- lengths: int32 [8, 4], P(('expert', 'dp')), may hold values from 1 to 480, 512 in all within a row
- block_order: int32 [8, 8], P(('expert', 'dp')), may hold values from 0 to 7, each once within a row
- routes: int32 [8, 512, 8], P(('expert', 'dp'), 'context'), may hold values from 0 to 15, all different within a row; in each aligned block of 128 rows (0 to 127, 128 to 255, ..., all dimensions but the last counted through in order) at most 72 rows name the same one
Outputs:
- output: float32 [8, 512, 2048], P(('expert', 'dp'), 'context')
- grad_tokens: float32 [8, 512, 2048], P(('expert', 'dp'), 'context')
- grad_attn: float32 [2048, 8192], P(('expert', 'context', 'dp'))
- grad_router: float32 [2048, 16], P(('expert', 'context', 'dp'))
- grad_gains: float32 [4, 2048], P(None, ('expert', 'context', 'dp'))
- grad_experts: float32 [2048, 16, 3072], P('dp', ('expert', 'context'))
The draws below stay inside these ranges and needn't reach their ends.
Inputs may be any that keep to these rules, and one draw needn't show every extreme that they name: `routes`: each row names 8 different experts; among the rows of one device no expert is named more than 72 times, a bound that some block reaches. A pack's lengths sum to 512; its longest document has exactly 480 positions. `block_order`: each pack's row is a permutation.
All inputs are finite; a program needn't handle non-finite values.
Results may differ from the reference program's by a relative error of at most 0.018.
Values may be sent and summed in bfloat16 or wider, within the bound.
No kernel may reach another device: no remote copies, remote signals or barrier semaphores. Data moves between devices by JAX's collectives and lax.ppermute only.
A program may use at most 384 MiB of HBM per device.

```python
import math
import jax
import jax.numpy as jnp
import numpy as np
from jax import lax

D = 2048
HEADS = 16
FF = 1024
TOP = 8
DOCS = 4
TOK_DEV = 128
HEAD_DIM = 128
EXPERTS = 16
PACK = 512
PACKS = 8
BLK = 64
LONGEST = 480
CAP = 72
N_CONTEXT = 4


def draw_w_attn(key, part):
    key = jax.random.fold_in(key, 11)
    column = jnp.arange(4 * D)
    column_std = jnp.where(column < 3 * D, 1.0, 6.0) * D ** (-0.5)
    base_draw = jax.random.normal(key, (D, 4 * D), jnp.float32)
    return base_draw * column_std[None, :]


def draw_w_experts(key, part):
    key = jax.random.fold_in(key, 23)
    column = jnp.arange(3 * FF)
    down_std = EXPERTS / (0.6 * (TOP * FF) ** 0.5)
    column_std = jnp.where(column < 2 * FF, D ** (-0.5), down_std)
    base_draw = jax.random.normal(key, (D, EXPERTS, 3 * FF), jnp.float32)
    return base_draw * column_std[None, None, :]


def block_levels(stream_key, extent, cuts, least, largest):
    level, own = 1.0, jax.random.fold_in(stream_key, 6)
    for dim, parts in cuts:
        steps = jnp.exp(jax.random.uniform(jax.random.fold_in(own, dim), (parts,), jnp.float32, least / len(cuts), largest / len(cuts)))
        level = level * jnp.repeat(steps, extent[dim] // parts).reshape([-1 if axis == dim else 1 for axis in range(len(extent))])
    return level


def split_up(count, total, bound, skew):
    weights = [(1 << 20) // math.isqrt(grade ** skew) + 1 for grade in range(2, count + 1)]
    surplus, given = total - bound - (count - 1), [1] * (count - 1)
    while surplus > 0:
        free = [i for i in range(count - 1) if given[i] < bound]
        mass, budget = sum([weights[i] for i in free]), surplus
        for i in free:
            extra = min(bound - given[i], max(1, budget * weights[i] // mass), surplus)
            given[i] = given[i] + extra
            surplus = surplus - extra
    return np.array([bound] + given)


def ragged_sizes(key, number_of, total, bound, slope):
    if number_of == 2:
        one = jax.random.randint(key, (), max(1, total - bound), min(bound, total - 1) + 1)
        return jnp.stack([one, total - one])
    sizes = jnp.asarray(split_up(number_of, total, bound, slope), jnp.int32)
    couples = (number_of - 1) // 2
    donor, taker = sizes[1:1 + 2 * couples:2], sizes[2:2 + 2 * couples:2]
    margin = jnp.minimum(donor - 1, bound - taker)
    shifted = jax.random.randint(jax.random.fold_in(key, 1), (couples,), 0, 1 << 20) % (margin + 1)
    sizes = sizes.at[1:1 + 2 * couples:2].set(donor - shifted).at[2:2 + 2 * couples:2].set(taker + shifted)
    return sizes[jax.random.permutation(jax.random.fold_in(key, 2), number_of)]


def assign_block(stream_key, own, number, rows, amount, top, reach, slope):
    ranking = jax.random.permutation(stream_key, amount)
    packed, common = portions_of(amount, rows * top, reach, slope, True), portions_of(amount, rows * top, reach, slope, False)
    places = jnp.arange(amount)

    def named(sizes, offset_by):
        used = int((sizes > 0).sum())
        fixed = max(1, used // 4)
        shifted = fixed + (places - fixed + offset_by * (used - fixed)) % max(1, amount - fixed)
        return jnp.zeros((amount,), jnp.int32).at[ranking[jnp.where(places < fixed, places, shifted)]].set(jnp.asarray(sizes, jnp.int32))

    sizes = jnp.where(number % 4 == 0, named(packed, number // 4), named(common, number - number // 4 - 1))
    mixed = jax.random.permutation(jax.random.fold_in(own, 3), amount)
    donor, taker = mixed[0:amount // 2 * 2:2], mixed[1:amount // 2 * 2:2]
    slack = jnp.minimum(sizes[donor] - 1, reach - sizes[taker]) // 2
    slack = jnp.where((donor == ranking[0]) | (taker == ranking[0]) | (sizes[taker] == 0), 0, jnp.maximum(slack, 0))
    shifted = jax.random.randint(jax.random.fold_in(own, 4), (amount // 2,), 0, 1 << 20) % (slack + 1)
    sizes = sizes.at[donor].add(-shifted).at[taker].add(shifted)
    items = jnp.searchsorted(jnp.cumsum(sizes), jnp.arange(rows * top), side="right").astype(jnp.int32)
    listing = items.reshape(top, rows).T
    listing = listing[jax.random.permutation(jax.random.fold_in(own, 1), rows)]
    offset_by = jax.random.randint(jax.random.fold_in(own, 2), (rows, 1), 0, top)
    return jnp.take_along_axis(listing, (jnp.arange(top)[None, :] + offset_by) % top, axis=1)


def portions_of(count, total, reach, skew, full):
    weights = [(1 << 20) // math.isqrt(standing ** skew) + 1 for standing in range(1, count + 1)]
    largest = reach if full else min(reach, max(-(-total // count), total * weights[0] // sum(weights)))
    least = 1 if total - largest >= count - 1 else 0
    holding, surplus = [largest] + [least] * (count - 1), total - largest - least * (count - 1)
    while surplus > 0:
        candidates = [i for i in range(1, count) if holding[i] < largest] or [i for i in range(1, count) if holding[i] < reach]
        pool, budget = sum([weights[i] for i in candidates]), surplus
        for i in candidates:
            extra = min(reach - holding[i], max(1, budget * weights[i] // pool), surplus)
            holding[i] = holding[i] + extra
            surplus = surplus - extra
    return np.array(holding)


def gaussian(key, extent, spread, reach, split=(), held_as=jnp.bfloat16):
    loudness = block_levels(key, extent, split, -0.22, 0.18) if split else 1.0
    values = jax.random.normal(key, extent, jnp.float32) * spread * loudness
    return jnp.minimum(jnp.maximum(values, -reach), reach).astype(held_as)


def setup_inputs(seed: int = 0) -> dict:
    splits = jax.random.split(jax.random.key(seed), 10)
    tokens = gaussian(splits[0], (PACKS, PACK, D), 1.0, 6.0, ((0, 8), (1, 4)))
    cotangent = gaussian(splits[1], (PACKS, PACK, D), 1.0, 6.0, ((0, 8), (1, 4)), jnp.float32)
    w_attn = draw_w_attn(jax.random.fold_in(splits[9], 71), 0)
    w_router = gaussian(splits[3], (D, EXPERTS), (4 * D) ** -0.5, 0.0625, ((0, 32),), jnp.float32)
    norm_gains = jnp.clip(1.0 + 0.1 * jax.random.normal(splits[4], (4, D), jnp.float32), 0.5, 1.5)
    w_experts = draw_w_experts(jax.random.fold_in(splits[9], 71), 0)
    lengths = jax.vmap(lambda own: ragged_sizes(own, DOCS, PACK, LONGEST, 1))(jax.random.split(splits[6], PACKS)).reshape((PACKS, DOCS)).astype(jnp.int32)
    block_order = jax.vmap(lambda own: jax.random.permutation(own, 2 * N_CONTEXT))(jax.random.split(splits[7], PACKS)).reshape((PACKS, 2 * N_CONTEXT)).astype(jnp.int32)
    routes_keys = jax.random.split(jax.random.fold_in(splits[8], 1), PACKS * PACK // TOK_DEV)
    routes_turns = jax.random.permutation(jax.random.fold_in(splits[8], 3), PACKS * PACK // TOK_DEV)
    routes = jax.vmap(lambda own, number: assign_block(jax.random.fold_in(splits[8], 2), own, number, TOK_DEV, EXPERTS, TOP, CAP, 1))(routes_keys, routes_turns).reshape((PACKS, PACK, TOP))
    return dict(tokens=tokens, cotangent=cotangent, w_attn=w_attn, w_router=w_router, norm_gains=norm_gains, w_experts=w_experts, lengths=lengths, block_order=block_order, routes=routes)


epsilon = 1e-05
rope_base = 10000.0
masked_score = -1e+30
top_precision = lax.Precision.HIGHEST

@jax.custom_vjp
def low(v):
    return lax.optimization_barrier(v.astype(jnp.bfloat16)).astype(jnp.float32)

@jax.custom_vjp
def low_back(v):
    return v

def low_keep(v):
    return (low(v), None)

def low_pass(kept, grad):
    return (grad,)

def back_keep(v):
    return (v, None)

def back_low(kept, grad):
    return (low(grad),)
low.defvjp(low_keep, low_pass)
low_back.defvjp(back_keep, back_low)

def rms_scale(values, gain_row):
    return values * lax.rsqrt(lax.optimization_barrier(jnp.mean(values * values, axis=-1, keepdims=True)) + epsilon) * gain_row

def rotate(values, offset):
    row_count = values.shape[0]
    half_width = HEAD_DIM // 2
    freq_table = rope_base ** (-2.0 * jnp.arange(half_width, dtype=jnp.float32) / HEAD_DIM)
    angle_table = offset.astype(jnp.float32)[:, None] * freq_table[None, :]
    cos_table = jnp.cos(angle_table)[:, None, :]
    sin_table = jnp.sin(angle_table)[:, None, :]
    split_heads = values.reshape(row_count, HEADS, HEAD_DIM)
    first_half = split_heads[..., :half_width]
    second_half = split_heads[..., half_width:]
    turned = jnp.concatenate([first_half * cos_table - second_half * sin_table, second_half * cos_table + first_half * sin_table], axis=-1)
    return turned.reshape(row_count, D)

def locate(stored_rows, doc_lens, blk_order, blk_rows):
    block_ids = stored_rows // blk_rows
    block_hits = block_ids[:, None] == jnp.arange(blk_order.shape[0], dtype=jnp.int32)[None, :]
    placed_at = lax.optimization_barrier(jnp.sum(jnp.where(block_hits, blk_order[None, :], 0), axis=1)).astype(jnp.int32) * blk_rows + stored_rows % blk_rows
    doc_ends = jnp.cumsum(doc_lens).astype(jnp.int32)
    doc_ids = lax.optimization_barrier(jnp.sum((placed_at[:, None] >= doc_ends[None, :]).astype(jnp.int32), axis=1)).astype(jnp.int32)
    doc_hits = doc_ids[:, None] == jnp.arange(doc_lens.shape[0], dtype=jnp.int32)[None, :]
    doc_starts = doc_ends - doc_lens
    offset = placed_at - lax.optimization_barrier(jnp.sum(jnp.where(doc_hits, doc_starts[None, :], 0), axis=1)).astype(jnp.int32)
    return (placed_at, doc_ids, offset)

def forward(inputs, w_attn, w_router, norm_gains, w_experts, lengths, block_order, routes):
    attn_w = low(w_attn)
    router_w = low(w_router)
    gains = low(norm_gains)
    expert_w = low(w_experts)

    def attend(pack_item):
        pack_x, doc_lens, blk_order = pack_item
        stored_rows = jnp.arange(PACK, dtype=jnp.int32)
        placed_at, doc_ids, offset = locate(stored_rows, doc_lens, blk_order, BLK)
        normed = low(rms_scale(pack_x, gains[0]))
        qkv_all = low_back(jnp.dot(normed, attn_w[:, :3 * D], precision=top_precision))
        query_f = low(rotate(rms_scale(qkv_all[:, :D], gains[2]), offset))
        key_f = low(rotate(rms_scale(qkv_all[:, D:2 * D], gains[3]), offset))
        value_f = low(qkv_all[:, 2 * D:])
        head_q = query_f.reshape(PACK, HEADS, HEAD_DIM)
        head_k = key_f.reshape(PACK, HEADS, HEAD_DIM)
        head_v = value_f.reshape(PACK, HEADS, HEAD_DIM)
        scores = low_back(jnp.einsum('qhd,khd->hqk', head_q, head_k, precision=top_precision) * HEAD_DIM ** (-0.5))
        allowed = (doc_ids[:, None] == doc_ids[None, :]) & (placed_at[None, :] <= placed_at[:, None])
        weights = low(jax.nn.softmax(jnp.where(allowed[None], scores, masked_score), axis=-1))
        mixed = jnp.einsum('hqk,khd->qhd', weights, head_v, precision=top_precision).reshape(PACK, D)
        mixed = low_back(low(mixed))
        return pack_x + low_back(jnp.dot(mixed, attn_w[:, 3 * D:], precision=top_precision))
    hidden = lax.map(jax.checkpoint(attend), (inputs, lengths, block_order))
    total_rows = PACKS * PACK
    flat_hidden = hidden.reshape(total_rows, D)
    normed_two = low(rms_scale(flat_hidden, gains[1]))
    logits = low_back(jnp.dot(normed_two, router_w, precision=top_precision))
    probs = jax.nn.softmax(logits, axis=-1)
    pick_rows = routes.reshape(total_rows, TOP)
    gates = jnp.take_along_axis(probs, pick_rows, axis=1)
    unit_count = total_rows // TOK_DEV
    unit_picks = pick_rows.reshape(unit_count, TOK_DEV * TOP)
    expert_hits = (unit_picks[:, :, None] == jnp.arange(EXPERTS, dtype=jnp.int32)[None, None, :]).astype(jnp.int32)
    slot_rank = lax.optimization_barrier(jnp.sum((jnp.cumsum(expert_hits, axis=1) - 1) * expert_hits, axis=2)).astype(jnp.int32)
    expert_slots = unit_count * CAP
    unit_base = (jnp.arange(unit_count, dtype=jnp.int32) * CAP)[:, None]
    slot_dest = (unit_picks * expert_slots + unit_base + slot_rank).astype(jnp.int32)
    flat_dest = slot_dest.reshape(-1)
    pair_token = (jnp.arange(total_rows * TOP, dtype=jnp.int32) // TOP).astype(jnp.int32)
    slot_token = jnp.zeros((EXPERTS * expert_slots,), jnp.int32).at[flat_dest].set(pair_token)
    filled = jnp.zeros((EXPERTS * expert_slots,), jnp.float32).at[flat_dest].set(1.0)
    buffer = low_back(normed_two[slot_token] * filled[:, None]).reshape(EXPERTS, expert_slots, D)

    def run_expert(expert_item):
        slot_rows, weight_block = expert_item
        gate_up = low_back(jnp.dot(slot_rows, weight_block[:, :2 * FF], precision=top_precision))
        activ = low(jax.nn.silu(gate_up[:, :FF]) * gate_up[:, FF:])
        produced = jnp.dot(activ, weight_block[:, 2 * FF:].T, precision=top_precision)
        return low_back(low(produced))
    expert_out = lax.map(jax.checkpoint(run_expert), (buffer, jnp.moveaxis(expert_w, 1, 0)))
    out_flat = expert_out.reshape(EXPERTS * expert_slots, D)

    def combine(unit_item):
        unit_dest, unit_gates = unit_item
        picked = out_flat[unit_dest].reshape(TOK_DEV, TOP, D)
        return lax.optimization_barrier(jnp.sum(picked * unit_gates[:, :, None], axis=1))
    mixture = lax.map(jax.checkpoint(combine), (slot_dest, gates.reshape(unit_count, TOK_DEV, TOP)))
    result = flat_hidden + mixture.reshape(total_rows, D)
    return result.reshape(PACKS, PACK, D)

def reference(tokens, cotangent, w_attn, w_router, norm_gains, w_experts, lengths, block_order, routes):

    def run_layer(inputs, attn_arg, router_arg, gain_arg, expert_arg):
        return forward(inputs, attn_arg, router_arg, gain_arg, expert_arg, lengths, block_order, routes)
    output, pull_back = jax.vjp(run_layer, tokens.astype(jnp.float32), w_attn, w_router, norm_gains, w_experts)
    grad_tokens, grad_attn, grad_router, grad_gains, grad_experts = pull_back(cotangent)
    return (output, grad_tokens, grad_attn, grad_router, grad_gains, grad_experts)
```

```python
import jax
import jax.numpy as jnp
from jax import lax
from jax.sharding import PartitionSpec as P

HEADS = 16
epsilon = 1e-05
rope_base = 10000.0
masked_score = -1e30
bf16 = jnp.bfloat16
f32 = jnp.float32
EVERY = ("expert", "context", "dp")


def mm(a, b):
    return jnp.dot(a, b, preferred_element_type=f32)


def mm_nt(a, b):
    return lax.dot_general(a, b, (((1,), (1,)), ((), ())), preferred_element_type=f32)


def mm_tn(a, b):
    return lax.dot_general(a, b, (((0,), (0,)), ((), ())), preferred_element_type=f32)


def swap(value, axis, bit):
    count = lax.axis_size(axis)
    return lax.ppermute(value, axis, [(i, i ^ bit) for i in range(count)])


def shift(value, axis, step):
    count = lax.axis_size(axis)
    return lax.ppermute(value, axis, [(i, (i + step) % count) for i in range(count)])


def bits_of(axis):
    count = lax.axis_size(axis)
    return [1 << i for i in range(count.bit_length() - 1)]


def spread(value):
    total = lax.axis_size(EVERY)
    return lax.all_to_all(value, EVERY, 0, 0, tiled=True) if value.shape[0] == total else None


def locate(stored_rows, doc_lens, blk_order, blk_rows):
    block_ids = stored_rows // blk_rows
    block_hits = block_ids[:, None] == jnp.arange(blk_order.shape[0], dtype=jnp.int32)[None, :]
    placed_at = (
        jnp.sum(jnp.where(block_hits, blk_order[None, :], 0), axis=1) * blk_rows
        + stored_rows % blk_rows
    )
    doc_count = doc_lens.shape[0]
    upto = jnp.arange(doc_count)[:, None] >= jnp.arange(doc_count)[None, :]
    doc_ends = jnp.sum(jnp.where(upto, doc_lens[None, :], 0), axis=1)
    doc_ids = jnp.sum((placed_at[:, None] >= doc_ends[None, :]).astype(jnp.int32), axis=1)
    doc_hits = doc_ids[:, None] == jnp.arange(doc_count, dtype=jnp.int32)[None, :]
    doc_starts = doc_ends - doc_lens
    offset = placed_at - jnp.sum(jnp.where(doc_hits, doc_starts[None, :], 0), axis=1)
    return placed_at, doc_ids, offset


def context_gather(value):
    me = lax.axis_index("context")
    parts = [value]
    for bit in reversed(bits_of("context")):
        parts = parts + [swap(part, "context", bit) for part in parts]
    count = len(parts)
    order = []
    for r in range(count):
        source = 0
        for i, bit in enumerate(reversed(bits_of("context"))):
            if r >> i & 1:
                source |= bit
        order.append(source)
    stack = [None] * count
    for r in range(count):
        stack[order[r]] = parts[r]
    rows = []
    for target in range(count):
        rows.append(
            sum(
                jnp.where(me == target ^ m, stack[m], jnp.zeros_like(stack[m])) for m in range(count)
            )
        )
    return jnp.concatenate(rows, axis=0)


def half_step(value, axis, bit, dim):
    mine = (lax.axis_index(axis) // bit) % 2
    keep = lax.dynamic_index_in_dim(value, mine, dim, keepdims=False)
    send = lax.dynamic_index_in_dim(value, 1 - mine, dim, keepdims=False).astype(bf16)
    return keep.astype(f32) + swap(send, axis, bit).astype(f32)


def context_scatter(value):
    bits = bits_of("context")
    rows = value.shape[0] >> len(bits)
    value = value.reshape((2,) * len(bits) + (rows, value.shape[1]))
    left = list(reversed(bits))
    for bit in bits:
        dim = left.index(bit)
        value = half_step(value, "context", bit, dim)
        left.remove(bit)
    return value


def token_scatter(value):
    steps_e = [("expert", b) for b in bits_of("expert")]
    steps_c = [("context", b) for b in bits_of("context")]
    z_count = lax.axis_size("dp")
    rows, width = value.shape[1:]
    dims = list(reversed(steps_e)) + list(reversed(steps_c))
    value = value.reshape((2,) * len(dims) + (z_count, rows, width))
    first, rest = steps_c[0], steps_c[1:] + steps_e
    dim = dims.index(first)
    value = half_step(value, first[0], first[1], dim).astype(bf16)
    dims = dims[:dim] + dims[dim + 1 :]
    half = width // 2
    outs = []
    for part, order in ((value[..., :half], rest), (value[..., half:], rest[::-1])):
        left = list(dims)
        for step in order:
            dim = left.index(step)
            part = half_step(part, step[0], step[1], dim).astype(bf16)
            left.remove(step)
        got = lax.all_to_all(part, "dp", 0, 0, tiled=True)
        outs.append(jnp.sum(got.astype(f32), axis=0))
    return jnp.concatenate(outs, axis=1)


def relative_gather(piece):
    around = [piece]
    for _ in range(lax.axis_size("dp") - 1):
        around.append(shift(around[-1], "dp", 1))
    held = [around]
    for bit in bits_of("expert"):
        held = held + [[swap(part, "expert", bit) for part in row] for row in held]
    return held


def relative_scatter(value):
    for bit in reversed(bits_of("expert")):
        half = value.shape[0] // 2
        value = value[:half].astype(f32) + swap(value[half:].astype(bf16), "expert", bit).astype(f32)
    value = value[0]
    total = value[0].astype(f32)
    for k in range(1, lax.axis_size("dp")):
        total = total + shift(value[k].astype(bf16), "dp", -k).astype(f32)
    return total


def on_device(
    tokens, cotangent, w_attn, w_router, norm_gains, w_experts, lengths, block_order, routes
):
    tok_rows, width = tokens.shape[1:]
    blk_rows = tok_rows // 2
    e_count, c_count, z_count = (lax.axis_size(a) for a in EVERY)
    total = e_count * c_count * z_count
    me_e, me_c, me_z = (lax.axis_index(a) for a in EVERY)
    pack_rows = tok_rows * c_count
    pick_rows = routes[0]
    top_count = pick_rows.shape[1]
    local_experts = w_experts.shape[1]
    expert_count = local_experts * e_count * c_count
    slot_cap = tok_rows * top_count * 9 // (8 * expert_count)
    ffn = w_experts.shape[2] // 3
    halves = z_count // local_experts
    ffh = ffn // halves
    head_width = width // HEADS
    local_heads = HEADS // c_count
    cols = local_heads * head_width
    w_rows = w_attn.shape[0]
    score_scale = head_width ** (-0.5)
    block_rows = z_count * w_rows
    aligned = block_rows % head_width == 0
    head_run = block_rows // head_width if aligned else local_heads
    runs = local_heads // head_run
    run_cols = head_run * head_width

    expert_ids = jnp.arange(expert_count, dtype=jnp.int32)
    pick_hits = (pick_rows[:, :, None] == expert_ids[None, None, :]).astype(f32)
    named = jnp.sum(pick_hits, axis=1)
    earlier = jnp.arange(tok_rows)[:, None] > jnp.arange(tok_rows)[None, :]
    ranks = mm(earlier.astype(bf16), named.astype(bf16))
    rank_rows = jnp.repeat(jnp.where(named > 0, ranks, -1.0).T, halves, axis=0)
    own_row = jnp.concatenate(
        [w_router.astype(bf16).reshape(-1), norm_gains.astype(bf16).reshape(-1)]
    )
    small_sent = jnp.concatenate(
        [jnp.broadcast_to(own_row[None], (total, own_row.shape[0])), rank_rows.astype(bf16)], axis=1
    )
    small = lax.all_to_all(small_sent, EVERY, 0, 0, tiled=True)
    n_router = w_router.size
    router_w = small[:, :n_router].reshape(width, expert_count)
    gains = (
        small[:, n_router : n_router + norm_gains.size]
        .reshape(total, 4, norm_gains.shape[1])
        .transpose(1, 0, 2)
        .reshape(4, width)
        .astype(f32)
    )
    slot_of = small[:, n_router + norm_gains.size :].astype(jnp.int32)

    wqkv = (
        w_attn[:, : 3 * width]
        .astype(bf16)
        .reshape(w_rows, 3, runs, c_count, run_cols)
        .transpose(3, 0, 1, 2, 4)
        .reshape(c_count, w_rows, 3 * cols)
    )
    wqkv = lax.all_to_all(wqkv, "context", 0, 0, tiled=True).reshape(c_count * w_rows, 3 * cols)
    held = relative_gather(wqkv)
    wqkv_all = jnp.concatenate([part for row in held for part in row], axis=0)
    wo_own = w_attn[:, 3 * width :].astype(bf16)
    if aligned:
        wo_all = jnp.concatenate([part for row in relative_gather(wo_own) for part in row], axis=0)
    else:
        wo_full = lax.all_gather(wo_own, EVERY, axis=0, tiled=True)
        wo_all = lax.dynamic_slice_in_dim(wo_full, me_c * cols, cols, axis=0)

    def place_of(r_e, r_z, c, row):
        return (((me_e ^ r_e) * c_count + c) * z_count + (me_z - r_z) % z_count) * w_rows + row

    spots = jnp.arange(width, dtype=jnp.int32)
    per_e = z_count * c_count * w_rows
    feature_of = place_of(
        spots // per_e,
        spots // (c_count * w_rows) % z_count,
        spots // w_rows % c_count,
        spots % w_rows,
    )
    order_n = (spots[:, None] == feature_of[None, :]).astype(bf16)
    if aligned:
        near = jnp.arange(cols, dtype=jnp.int32)
        local_of = (
            (me_e ^ (near // block_rows)) * block_rows
            + (me_z - near // w_rows % z_count) % z_count * w_rows
            + near % w_rows
        )
        order_o = (near[:, None] == local_of[None, :]).astype(bf16)

    wx = (
        w_experts.astype(bf16)
        .reshape(w_experts.shape[0], local_experts, 3, halves, ffh)
        .transpose(1, 3, 0, 2, 4)
        .reshape(z_count, w_experts.shape[0], 3 * ffh)
    )
    wx = lax.all_to_all(wx, "dp", 0, 0, tiled=True).reshape(width, 3 * ffh)
    w_gu, w_down = wx[:, : 2 * ffh], wx[:, 2 * ffh :]

    grad_out = cotangent[0]
    inputs = tokens[0].astype(f32)
    pack_x = context_gather(tokens[0]).astype(f32)
    scale_one = lax.rsqrt(jnp.mean(pack_x * pack_x, axis=-1, keepdims=True) + epsilon)
    normed_one = (pack_x * scale_one * gains[0]).astype(bf16)
    normed_one_r = mm(normed_one, order_n).astype(bf16)
    qkv = mm(normed_one_r, wqkv_all)
    place, doc, offset = locate(
        jnp.arange(pack_rows, dtype=jnp.int32), lengths[0], block_order[0], blk_rows
    )
    half_width = head_width // 2
    freq = rope_base ** (-2.0 * jnp.arange(half_width, dtype=f32) / head_width)
    angle = offset.astype(f32)[:, None] * freq[None, :]
    cos_t, sin_t = jnp.cos(angle), jnp.sin(angle)
    cos_all = jnp.concatenate([cos_t, cos_t], axis=1)[:, None, :]
    sin_all = jnp.concatenate([-sin_t, sin_t], axis=1)[:, None, :]

    def turn(v):
        v = v.reshape(pack_rows, local_heads, head_width)
        return v * cos_all + jnp.roll(v, half_width, axis=2) * sin_all

    def turn_back(v):
        return (v * cos_all + jnp.roll(v * sin_all, half_width, axis=2)).reshape(pack_rows, cols)

    my_gains = lax.dynamic_index_in_dim(
        gains[2:].reshape(2, runs, c_count, run_cols), me_c, 2, keepdims=False
    ).reshape(2, cols)
    raw_q, raw_k = qkv[:, :cols], qkv[:, cols : 2 * cols]
    value = qkv[:, 2 * cols :].astype(bf16).reshape(pack_rows, local_heads, head_width)
    squares = jnp.stack([jnp.sum(raw_q * raw_q, axis=1), jnp.sum(raw_k * raw_k, axis=1)])
    scale_qk = lax.rsqrt(lax.psum(squares, "context") / width + epsilon)[:, :, None]
    unit_q, unit_k = raw_q * scale_qk[0], raw_k * scale_qk[1]
    query = turn(unit_q * my_gains[0]).astype(bf16)
    key = turn(unit_k * my_gains[1]).astype(bf16)
    scores = jnp.einsum("qhd,khd->hqk", query, key, preferred_element_type=f32) * score_scale
    allowed = (doc[:, None] == doc[None, :]) & (place[None, :] <= place[:, None])
    scores = jnp.where(allowed[None], scores, masked_score)
    top = jnp.max(scores, axis=2, keepdims=True)
    raised = jnp.exp(scores - top)
    soft = raised / jnp.sum(raised, axis=2, keepdims=True)
    soft_b = soft.astype(bf16)
    mixed = (
        jnp.einsum("hqk,khd->qhd", soft_b, value, preferred_element_type=f32)
        .reshape(pack_rows, cols)
        .astype(bf16)
    )
    mixed_r = mm(mixed, order_o).astype(bf16) if aligned else mixed
    hidden = inputs + context_scatter(mm(mixed_r, wo_all))
    scale_two = lax.rsqrt(jnp.mean(hidden * hidden, axis=-1, keepdims=True) + epsilon)
    normed_two = (hidden * scale_two * gains[1]).astype(bf16)
    logits = mm(normed_two, router_w)
    probs = jax.nn.softmax(logits, axis=-1)

    all_grad = lax.all_gather(grad_out.astype(bf16), EVERY, axis=0, tiled=True)
    all_grad = all_grad.reshape(total, tok_rows, width)
    all_normed = lax.all_gather(normed_two, EVERY, axis=0, tiled=True)
    all_normed = all_normed.reshape(total, tok_rows, width)
    gate_rows = lax.all_to_all(jnp.repeat(probs.T, halves, axis=0), EVERY, 0, 0, tiled=True)
    slots = jnp.arange(slot_cap, dtype=jnp.int32)
    pick = (slot_of[:, None, :] == slots[None, :, None]).astype(bf16)
    put = (slot_of[:, :, None] == slots[None, None, :]).astype(bf16)

    def take_rows(rows):
        got = jnp.einsum("sct,std->scd", pick, rows, preferred_element_type=f32)
        return got.astype(bf16).reshape(total * slot_cap, width)

    def put_rows(rows):
        rows = rows.astype(bf16).reshape(total, slot_cap, width)
        return jnp.einsum("stc,scd->std", put, rows, preferred_element_type=f32).astype(bf16)

    gate = jnp.sum(
        jnp.where(slot_of[:, None, :] == slots[None, :, None], gate_rows[:, None, :], 0.0), axis=2
    ).reshape(total * slot_cap, 1)
    g_rows = take_rows(all_grad)
    back = mm(g_rows, w_down)
    n_rows = take_rows(all_normed)
    gate_up = mm(n_rows, w_gu)
    gate_part, up_part = gate_up[:, :ffh], gate_up[:, ffh:]
    sig = jax.nn.sigmoid(gate_part)
    silu = gate_part * sig
    act = (silu * up_part).astype(bf16)
    act_f = act.astype(f32)
    grad_gate_slot = jnp.sum(act_f * back, axis=1).reshape(total, slot_cap)
    grad_act = back * gate
    grad_gu = jnp.concatenate(
        [grad_act * up_part * sig * (1.0 + gate_part * (1.0 - sig)), grad_act * silu], axis=1
    ).astype(bf16)
    grad_rows = mm_nt(grad_gu, w_gu)
    grad_n2 = token_scatter(put_rows(grad_rows))
    sent_gates = jnp.sum(
        jnp.where(slot_of[:, :, None] == slots[None, None, :], grad_gate_slot[:, None, :], 0.0),
        axis=2,
    )
    got_gates = lax.all_to_all(sent_gates, EVERY, 0, 0, tiled=True)
    grad_probs = jnp.sum(got_gates.reshape(expert_count, halves, tok_rows), axis=1).T

    act_scaled = (act_f * gate).astype(bf16)
    grad_wx = jnp.concatenate([mm_tn(n_rows, grad_gu), mm_tn(g_rows, act_scaled)], axis=1)
    grad_wx = grad_wx.astype(bf16).reshape(z_count, width // z_count, 3 * ffh)
    grad_wx = lax.all_to_all(grad_wx, "dp", 0, 0, tiled=True)
    grad_experts = (
        grad_wx.astype(f32)
        .reshape(local_experts, halves, width // z_count, 3, ffh)
        .transpose(2, 0, 3, 1, 4)
        .reshape(width // z_count, local_experts, 3 * ffn)
    )
    mixture = token_scatter(put_rows(mm_nt(act, w_down) * gate))
    output = hidden + mixture

    grad_logits = (
        probs * (grad_probs - jnp.sum(probs * grad_probs, axis=-1, keepdims=True))
    ).astype(bf16)
    grad_n2 = grad_n2 + mm_nt(grad_logits, router_w)
    router_term = mm_tn(normed_two, grad_logits)

    def norm_back(v, scale, gain, grad):
        pulled = grad * gain
        inner = jnp.mean(v * pulled, axis=-1, keepdims=True)
        return scale * pulled - v * (scale * scale * scale * inner)

    gain_two = jnp.sum(grad_n2 * hidden * scale_two, axis=0)
    grad_hidden = grad_out + norm_back(hidden, scale_two, gains[1], grad_n2)
    grad_hidden_b = grad_hidden.astype(bf16)

    pack_dh = context_gather(grad_hidden_b)
    grad_mixed = mm_nt(pack_dh, wo_all).astype(bf16)
    if aligned:
        grad_mixed = mm_nt(grad_mixed, order_o).astype(bf16)
    grad_mixed_h = grad_mixed.reshape(pack_rows, local_heads, head_width)
    grad_soft = jnp.einsum("qhd,khd->hqk", grad_mixed_h, value, preferred_element_type=f32)
    delta = jnp.sum(soft * grad_soft, axis=2, keepdims=True)
    grad_scores = (soft * (grad_soft - delta)).astype(bf16)
    grad_query = jnp.einsum("hqk,khd->qhd", grad_scores, key, preferred_element_type=f32)
    grad_key = jnp.einsum("hqk,qhd->khd", grad_scores, query, preferred_element_type=f32)
    grad_value = jnp.einsum("hqk,qhd->khd", soft_b, grad_mixed_h, preferred_element_type=f32)
    back_q, back_k = turn_back(grad_query * score_scale), turn_back(grad_key * score_scale)
    gain_q = jnp.sum(back_q * unit_q, axis=0)
    gain_k = jnp.sum(back_k * unit_k, axis=0)
    pull_q, pull_k = back_q * my_gains[0], back_k * my_gains[1]
    inner = jnp.stack([jnp.sum(raw_q * pull_q, axis=1), jnp.sum(raw_k * pull_k, axis=1)])
    inner = (lax.psum(inner, "context") / width)[:, :, None]
    grad_qkv = jnp.concatenate(
        [
            scale_qk[0] * pull_q - raw_q * (scale_qk[0] ** 3 * inner[0]),
            scale_qk[1] * pull_k - raw_k * (scale_qk[1] ** 3 * inner[1]),
            grad_value.reshape(pack_rows, cols),
        ],
        axis=1,
    ).astype(bf16)
    grad_n1 = mm(context_pull(grad_qkv, wqkv_all), order_n_t(order_n))
    grad_n1 = context_scatter(grad_n1)
    own_scale = lax.rsqrt(jnp.mean(inputs * inputs, axis=-1, keepdims=True) + epsilon)
    gain_one = jnp.sum(grad_n1 * inputs * own_scale, axis=0)
    grad_tokens = grad_hidden + norm_back(inputs, own_scale, gains[0], grad_n1)

    grad_wqkv = mm_tn(normed_one_r, grad_qkv).reshape(e_count, z_count, c_count, w_rows, 3 * cols)
    grad_wqkv = relative_scatter(grad_wqkv).astype(bf16)
    grad_wqkv = (
        lax.all_to_all(grad_wqkv, "context", 0, 0, tiled=True)
        .reshape(c_count, w_rows, 3, runs, run_cols)
        .transpose(1, 2, 3, 0, 4)
        .reshape(w_rows, 3 * width)
        .astype(f32)
    )
    grad_wo = mm_tn(mixed_r, pack_dh)
    if aligned:
        grad_wo = relative_scatter(grad_wo.reshape(e_count, z_count, w_rows, width))
    else:
        whole_wo = lax.dynamic_update_slice_in_dim(
            jnp.zeros((width, width), f32), grad_wo, me_c * cols, axis=0
        )
        grad_wo = lax.psum_scatter(
            whole_wo.astype(bf16), EVERY, scatter_dimension=0, tiled=True
        ).astype(f32)
    grad_attn = jnp.concatenate([grad_wqkv, grad_wo], axis=1)

    mine = jnp.arange(c_count)[None, None, :, None] == me_c
    gain_qk = jnp.where(mine, jnp.stack([gain_q, gain_k]).reshape(2, runs, 1, run_cols), 0.0)
    gain_rows = jnp.concatenate([jnp.stack([gain_one, gain_two]), gain_qk.reshape(2, width)])
    gain_rows = gain_rows.reshape(4, total, -1).transpose(1, 0, 2).reshape(total, -1)
    small_grads = jnp.concatenate([router_term.reshape(total, -1), gain_rows], axis=1)
    small_grads = jnp.sum(lax.all_to_all(small_grads, EVERY, 0, 0, tiled=True), axis=0)
    grad_router = small_grads[:n_router].reshape(w_router.shape)
    grad_gains = small_grads[n_router:].reshape(norm_gains.shape)
    return (output[None], grad_tokens[None], grad_attn, grad_router, grad_gains, grad_experts)


def context_pull(grad_qkv, wqkv_all):
    return mm_nt(grad_qkv, wqkv_all).astype(bf16)


def order_n_t(order_n):
    return order_n.T


def solution(mesh):
    in_specs = (
        P(("expert", "dp"), "context", None),
        P(("expert", "dp"), "context", None),
        P(EVERY, None),
        P(EVERY, None),
        P(None, EVERY),
        P("dp", ("expert", "context"), None),
        P(("expert", "dp"), None),
        P(("expert", "dp"), None),
        P(("expert", "dp"), "context", None),
    )
    out_specs = (
        P(("expert", "dp"), "context", None),
        P(("expert", "dp"), "context", None),
        P(EVERY, None),
        P(EVERY, None),
        P(None, EVERY),
        P("dp", ("expert", "context"), None),
    )
    return jax.shard_map(
        on_device, mesh=mesh, in_specs=in_specs, out_specs=out_specs, check_vma=False
    )
```

```python
import jax
import jax.numpy as jnp
from jax import lax
from jax.experimental import pallas as pl
from jax.experimental.pallas import tpu as pltpu
from jax.sharding import PartitionSpec as P

HEADS = 16
epsilon = 1e-05
rope_base = 10000.0
masked_score = -1e30
bf16 = jnp.bfloat16
f32 = jnp.float32
EVERY = ("expert", "context", "dp")


def mm(a, b):
    return jnp.dot(a, b, preferred_element_type=f32)


def mm_nt(a, b):
    return lax.dot_general(a, b, (((1,), (1,)), ((), ())), preferred_element_type=f32)


def mm_tn(a, b):
    return lax.dot_general(a, b, (((0,), (0,)), ((), ())), preferred_element_type=f32)


def swap(value, axis, bit):
    count = lax.axis_size(axis)
    return lax.ppermute(value, axis, [(i, i ^ bit) for i in range(count)])


def shift(value, axis, step):
    count = lax.axis_size(axis)
    return lax.ppermute(value, axis, [(i, (i + step) % count) for i in range(count)])


def bits_of(axis):
    count = lax.axis_size(axis)
    return [1 << i for i in range(count.bit_length() - 1)]


def locate(stored_rows, doc_lens, blk_order, blk_rows):
    block_ids = stored_rows // blk_rows
    block_hits = block_ids[:, None] == jnp.arange(blk_order.shape[0], dtype=jnp.int32)[None, :]
    placed_at = (
        jnp.sum(jnp.where(block_hits, blk_order[None, :], 0), axis=1) * blk_rows
        + stored_rows % blk_rows
    )
    doc_count = doc_lens.shape[0]
    upto = jnp.arange(doc_count)[:, None] >= jnp.arange(doc_count)[None, :]
    doc_ends = jnp.sum(jnp.where(upto, doc_lens[None, :], 0), axis=1)
    doc_ids = jnp.sum((placed_at[:, None] >= doc_ends[None, :]).astype(jnp.int32), axis=1)
    doc_hits = doc_ids[:, None] == jnp.arange(doc_count, dtype=jnp.int32)[None, :]
    doc_starts = doc_ends - doc_lens
    offset = placed_at - jnp.sum(jnp.where(doc_hits, doc_starts[None, :], 0), axis=1)
    return placed_at, doc_ids, offset


def context_gather(value):
    me = lax.axis_index("context")
    parts = [value]
    for bit in reversed(bits_of("context")):
        parts = parts + [swap(part, "context", bit) for part in parts]
    count = len(parts)
    order = []
    for r in range(count):
        source = 0
        for i, bit in enumerate(reversed(bits_of("context"))):
            if r >> i & 1:
                source |= bit
        order.append(source)
    stack = [None] * count
    for r in range(count):
        stack[order[r]] = parts[r]
    rows = []
    for target in range(count):
        rows.append(
            sum(
                jnp.where(me == target ^ m, stack[m], jnp.zeros_like(stack[m])) for m in range(count)
            )
        )
    return jnp.concatenate(rows, axis=0)


def half_step(value, axis, bit, dim):
    mine = (lax.axis_index(axis) // bit) % 2
    keep = lax.dynamic_index_in_dim(value, mine, dim, keepdims=False)
    send = lax.dynamic_index_in_dim(value, 1 - mine, dim, keepdims=False).astype(bf16)
    return keep.astype(f32) + swap(send, axis, bit).astype(f32)


def context_scatter(value):
    bits = bits_of("context")
    rows = value.shape[0] >> len(bits)
    value = value.reshape((2,) * len(bits) + (rows, value.shape[1]))
    left = list(reversed(bits))
    for bit in bits:
        dim = left.index(bit)
        value = half_step(value, "context", bit, dim)
        left.remove(bit)
    return value


def far_steps(k):
    steps = [("context", b) for b in bits_of("context")[1:]]
    steps = steps + [("expert", b) for b in bits_of("expert")]
    return steps[::-1] if k % 2 else steps


def near_step():
    return ("context", bits_of("context")[0])


def group_keys(k):
    steps = [near_step()] + far_steps(k)
    keys = []
    for i in range(1 << len(steps)):
        masks = {"expert": 0, "context": 0}
        for j, (axis, bit) in enumerate(steps):
            if i >> (len(steps) - 1 - j) & 1:
                masks[axis] |= bit
        keys.append((masks["expert"], masks["context"]))
    return keys


def token_gather(value):
    around = [value]
    for _ in range(lax.axis_size("dp") - 1):
        around.append(shift(around[-1], "dp", 1))
    groups = []
    for k, start in enumerate(around):
        held = {(0, 0): start}
        for axis, bit in far_steps(k) + [near_step()]:
            for key in list(held):
                new = (key[0] | bit, key[1]) if axis == "expert" else (key[0], key[1] | bit)
                held[new] = swap(held[key], axis, bit)
        groups.append([held[key] for key in group_keys(k)])
    return groups


def group_scatter(value, k):
    for axis, bit in [near_step()] + far_steps(k):
        half = value.shape[0] // 2
        got = swap(value[half:], axis, bit)
        value = (value[:half].astype(f32) + got.astype(f32)).astype(bf16)
    value = value[0]
    return shift(value, "dp", -k) if k else value


def around_dp(blocks):
    count = lax.axis_size("dp")
    me = lax.axis_index("dp")
    got = []
    for k in range(count):
        block = lax.dynamic_index_in_dim(blocks, (me + k) % count, 0, keepdims=False)
        got.append(shift(block, "dp", k) if k else block)
    return got


def split_kernel(experts, halves, w_ref, out_ref):
    ffh = out_ref.shape[2] // 3
    for e in range(experts):
        rows = w_ref[:, e, :].astype(bf16)
        for h in range(halves):
            for j in range(3):
                at = (j * halves + h) * ffh
                out_ref[e * halves + h, :, j * ffh : (j + 1) * ffh] = rows[:, at : at + ffh]


def split_experts(w, halves):
    rows, experts, width = w.shape
    block = 64
    return pl.pallas_call(
        lambda w_ref, out_ref: split_kernel(experts, halves, w_ref, out_ref),
        grid=(rows // block,),
        in_specs=[pl.BlockSpec((block, experts, width), lambda i: (i, 0, 0))],
        out_specs=pl.BlockSpec(
            (experts * halves, block, width // halves), lambda i: (0, i, 0)
        ),
        out_shape=jax.ShapeDtypeStruct((experts * halves, rows, width // halves), bf16),
        compiler_params=pltpu.CompilerParams(vmem_limit_bytes=32 * 2**20),
    )(w)


def join_kernel(experts, halves, me_ref, *refs):
    *parts, out_ref = refs
    count = len(parts)
    ffh = parts[0].shape[1] // 3
    me = me_ref[0]
    for t in range(count):
        e, h = divmod(t, halves)
        for j in range(3):
            piece = parts[0][:, j * ffh : (j + 1) * ffh].astype(f32)
            for k in range(1, count):
                other = parts[k][:, j * ffh : (j + 1) * ffh].astype(f32)
                piece = jnp.where((me - t - k) % count == 0, other, piece)
            at = (j * halves + h) * ffh
            out_ref[:, e, at : at + ffh] = piece


def join_experts(parts, experts, halves):
    rows, width = parts[0].shape
    block = 64
    me = lax.axis_index("dp").astype(jnp.int32).reshape(1) + len(parts)
    return pl.pallas_call(
        lambda me_ref, *refs: join_kernel(experts, halves, me_ref, *refs),
        grid_spec=pltpu.PrefetchScalarGridSpec(
            num_scalar_prefetch=1,
            grid=(rows // block,),
            in_specs=[pl.BlockSpec((block, width), lambda i, m: (i, 0)) for _ in parts],
            out_specs=pl.BlockSpec((block, experts, width * halves), lambda i, m: (i, 0, 0)),
        ),
        out_shape=jax.ShapeDtypeStruct((rows, experts, width * halves), f32),
        compiler_params=pltpu.CompilerParams(vmem_limit_bytes=32 * 2**20),
    )(me, *parts)


def relative_gather(piece):
    around = [piece]
    for _ in range(lax.axis_size("dp") - 1):
        around.append(shift(around[-1], "dp", 1))
    held = [around]
    for bit in bits_of("expert"):
        held = held + [[swap(part, "expert", bit) for part in row] for row in held]
    return held


def absolute(held, rows, shape):
    me_e, me_z = lax.axis_index("expert"), lax.axis_index("dp")
    z_count = len(held[0])
    first = shape(held[0][0])
    whole = jnp.zeros((len(held), first.shape[1], z_count) + first.shape[3:], first.dtype)
    for r, row in enumerate(held):
        for k, part in enumerate(row):
            at = (me_e ^ r, 0, (me_z - k) % z_count, 0, 0)
            whole = lax.dynamic_update_slice(whole, shape(part), at)
    return whole


def relative_scatter(value):
    me_e, me_z = lax.axis_index("expert"), lax.axis_index("dp")
    for bit in reversed(bits_of("expert")):
        value = value.reshape((value.shape[0] // 2, 2) + value.shape[1:]) if bit == 1 else value
        if bit == 1:
            value = half_step(value, "expert", 1, 1)
        else:
            value = value.reshape((2, value.shape[0] // 2) + value.shape[1:])
            value = half_step(value, "expert", bit, 0)
    value = value[0]
    z_count = lax.axis_size("dp")
    total = lax.dynamic_index_in_dim(value, me_z, 0, keepdims=False).astype(f32)
    for k in range(1, z_count):
        part = lax.dynamic_index_in_dim(value, (me_z - k) % z_count, 0, keepdims=False)
        total = total + shift(part.astype(bf16), "dp", -k).astype(f32)
    return total


def on_device(
    tokens, cotangent, w_attn, w_router, norm_gains, w_experts, lengths, block_order, routes
):
    tok_rows, width = tokens.shape[1:]
    blk_rows = tok_rows // 2
    e_count, c_count, z_count = (lax.axis_size(a) for a in EVERY)
    total = e_count * c_count * z_count
    me_e, me_c, me_z = (lax.axis_index(a) for a in EVERY)
    pack_rows = tok_rows * c_count
    pick_rows = routes[0]
    top_count = pick_rows.shape[1]
    local_experts = w_experts.shape[1]
    expert_count = local_experts * e_count * c_count
    slot_cap = tok_rows * top_count * 9 // (8 * expert_count)
    ffn = w_experts.shape[2] // 3
    halves = z_count // local_experts
    ffh = ffn // halves
    head_width = width // HEADS
    local_heads = HEADS // c_count
    cols = local_heads * head_width
    w_rows = w_attn.shape[0]
    score_scale = head_width ** (-0.5)
    block_rows = z_count * w_rows
    aligned = block_rows % head_width == 0
    head_run = block_rows // head_width if aligned else local_heads
    runs = local_heads // head_run
    run_cols = head_run * head_width

    expert_ids = jnp.arange(expert_count, dtype=jnp.int32)
    pick_hits = (pick_rows[:, :, None] == expert_ids[None, None, :]).astype(f32)
    named = jnp.sum(pick_hits, axis=1)
    earlier = jnp.arange(tok_rows)[:, None] > jnp.arange(tok_rows)[None, :]
    ranks = mm(earlier.astype(bf16), named.astype(bf16))
    rank_rows = jnp.repeat(jnp.where(named > 0, ranks, -1.0).T, halves, axis=0)
    own_row = jnp.concatenate(
        [w_router.astype(bf16).reshape(-1), norm_gains.astype(bf16).reshape(-1)]
    )
    small_sent = jnp.concatenate(
        [jnp.broadcast_to(own_row[None], (total, own_row.shape[0])), rank_rows.astype(bf16)], axis=1
    )
    small = lax.all_to_all(small_sent, EVERY, 0, 0, tiled=True)
    n_router = w_router.size
    router_w = small[:, :n_router].reshape(width, expert_count)
    gains = (
        small[:, n_router : n_router + norm_gains.size]
        .reshape(total, 4, norm_gains.shape[1])
        .transpose(1, 0, 2)
        .reshape(4, width)
        .astype(f32)
    )
    slot_of = small[:, n_router + norm_gains.size :].astype(jnp.int32)

    wqkv = (
        w_attn[:, : 3 * width]
        .astype(bf16)
        .reshape(w_rows, 3, runs, c_count, run_cols)
        .transpose(3, 0, 1, 2, 4)
        .reshape(c_count, w_rows, 3 * cols)
    )
    wqkv = lax.all_to_all(wqkv, "context", 0, 0, tiled=True).reshape(c_count * w_rows, 3 * cols)
    held = relative_gather(wqkv)
    z_done = held[0][-1]
    wqkv_all = absolute(held, c_count * w_rows, lambda v: v.reshape(1, c_count, 1, w_rows, -1))
    wqkv_all = wqkv_all.reshape(width, 3 * cols)
    wo_own = w_attn[:, 3 * width :].astype(bf16)
    if aligned:
        wo_all = absolute(relative_gather(wo_own), w_rows, lambda v: v.reshape(1, 1, 1, w_rows, -1))
        wo_all = wo_all.reshape(cols, width)
    else:
        wo_full = lax.all_gather(wo_own, EVERY, axis=0, tiled=True)
        wo_all = lax.dynamic_slice_in_dim(wo_full, me_c * cols, cols, axis=0)

    wx, _ = lax.optimization_barrier((split_experts(w_experts, halves), z_done))
    d_rows = w_experts.shape[0]
    wx_all = jnp.zeros((z_count, d_rows, 3 * ffh), bf16)
    for k, part in enumerate(around_dp(wx)):
        wx_all = lax.dynamic_update_slice(wx_all, part[None], ((me_z - k) % z_count, 0, 0))
    wx = wx_all.reshape(width, 3 * ffh)
    w_gu, w_down = wx[:, : 2 * ffh], wx[:, 2 * ffh :]

    grad_out = cotangent[0]
    inputs = tokens[0].astype(f32)
    pack_x = context_gather(tokens[0]).astype(f32)
    scale_one = lax.rsqrt(jnp.mean(pack_x * pack_x, axis=-1, keepdims=True) + epsilon)
    normed_one = (pack_x * scale_one * gains[0]).astype(bf16)
    qkv = mm(normed_one, wqkv_all)
    place, doc, offset = locate(
        jnp.arange(pack_rows, dtype=jnp.int32), lengths[0], block_order[0], blk_rows
    )
    half_width = head_width // 2
    freq = rope_base ** (-2.0 * jnp.arange(half_width, dtype=f32) / head_width)
    angle = offset.astype(f32)[:, None] * freq[None, :]
    cos_t, sin_t = jnp.cos(angle), jnp.sin(angle)
    cos_all = jnp.concatenate([cos_t, cos_t], axis=1)[:, None, :]
    sin_all = jnp.concatenate([-sin_t, sin_t], axis=1)[:, None, :]

    def turn(v):
        v = v.reshape(pack_rows, local_heads, head_width)
        return v * cos_all + jnp.roll(v, half_width, axis=2) * sin_all

    def turn_back(v):
        return (v * cos_all + jnp.roll(v * sin_all, half_width, axis=2)).reshape(pack_rows, cols)

    my_gains = lax.dynamic_index_in_dim(
        gains[2:].reshape(2, runs, c_count, run_cols), me_c, 2, keepdims=False
    ).reshape(2, cols)
    raw_q, raw_k = qkv[:, :cols], qkv[:, cols : 2 * cols]
    value = qkv[:, 2 * cols :].astype(bf16).reshape(pack_rows, local_heads, head_width)
    squares = jnp.stack([jnp.sum(raw_q * raw_q, axis=1), jnp.sum(raw_k * raw_k, axis=1)])
    scale_qk = lax.rsqrt(lax.psum(squares, "context") / width + epsilon)[:, :, None]
    unit_q, unit_k = raw_q * scale_qk[0], raw_k * scale_qk[1]
    query = turn(unit_q * my_gains[0]).astype(bf16)
    key = turn(unit_k * my_gains[1]).astype(bf16)
    scores = jnp.einsum("qhd,khd->hqk", query, key, preferred_element_type=f32) * score_scale
    allowed = (doc[:, None] == doc[None, :]) & (place[None, :] <= place[:, None])
    scores = jnp.where(allowed[None], scores, masked_score)
    top = jnp.max(scores, axis=2, keepdims=True)
    raised = jnp.exp(scores - top)
    soft = raised / jnp.sum(raised, axis=2, keepdims=True)
    soft_b = soft.astype(bf16)
    mixed = (
        jnp.einsum("hqk,khd->qhd", soft_b, value, preferred_element_type=f32)
        .reshape(pack_rows, cols)
        .astype(bf16)
    )
    hidden = inputs + context_scatter(mm(mixed, wo_all))
    scale_two = lax.rsqrt(jnp.mean(hidden * hidden, axis=-1, keepdims=True) + epsilon)
    normed_two = (hidden * scale_two * gains[1]).astype(bf16)
    logits = mm(normed_two, router_w)
    probs = jax.nn.softmax(logits, axis=-1)

    own_grad, _ = lax.optimization_barrier((grad_out.astype(bf16), z_done))
    all_grad = token_gather(own_grad)
    all_normed = token_gather(normed_two)
    gate_rows = lax.all_to_all(jnp.repeat(probs.T, halves, axis=0), EVERY, 0, 0, tiled=True)
    slots = jnp.arange(slot_cap, dtype=jnp.int32)
    sources = [
        jnp.stack(
            [
                ((me_e ^ m_e) * c_count + (me_c ^ m_c)) * z_count + (me_z - k) % z_count
                for m_e, m_c in group_keys(k)
            ]
        )
        for k in range(z_count)
    ]
    n_src = len(group_keys(0))
    n_rows, g_rows, acts, scaled, gus, puts, gate_parts, scattered = ([] for _ in range(8))
    dgate_rows = []
    for k in range(z_count):
        slot_k = slot_of[sources[k]]
        hit = slot_k[:, None, :] == slots[None, :, None]
        pick = hit.astype(bf16)
        put = (slot_k[:, :, None] == slots[None, None, :]).astype(bf16)
        gate_in = gate_rows[sources[k]]
        gate = jnp.sum(jnp.where(hit, gate_in[:, None, :], 0.0), axis=2)
        gate = gate.reshape(n_src * slot_cap, 1)

        def take_rows(rows):
            got = jnp.einsum("sct,std->scd", pick, jnp.stack(rows), preferred_element_type=f32)
            return got.astype(bf16).reshape(n_src * slot_cap, width)

        g_k = take_rows(all_grad[k])
        back = mm(g_k, w_down)
        n_k = take_rows(all_normed[k])
        gate_up = mm(n_k, w_gu)
        gate_part, up_part = gate_up[:, :ffh], gate_up[:, ffh:]
        sig = jax.nn.sigmoid(gate_part)
        silu = gate_part * sig
        act = (silu * up_part).astype(bf16)
        act_f = act.astype(f32)
        dgate = jnp.sum(act_f * back, axis=1).reshape(n_src, 1, slot_cap)
        put_hit = slot_k[:, :, None] == slots[None, None, :]
        dgate_rows.append(jnp.sum(jnp.where(put_hit, dgate, 0.0), axis=2))
        grad_act = back * gate
        grad_gu = jnp.concatenate(
            [grad_act * up_part * sig * (1.0 + gate_part * (1.0 - sig)), grad_act * silu], axis=1
        ).astype(bf16)
        grad_rows = mm_nt(grad_gu, w_gu).astype(bf16).reshape(n_src, slot_cap, width)
        grad_rows = jnp.einsum("stc,scd->std", put, grad_rows, preferred_element_type=f32)
        scattered.append(group_scatter(grad_rows.astype(bf16), k))
        n_rows.append(n_k)
        g_rows.append(g_k)
        acts.append(act)
        scaled.append((act_f * gate).astype(bf16))
        gus.append(grad_gu)
        puts.append(put)
        gate_parts.append(gate)
    grad_n2 = sum(part.astype(f32) for part in scattered)
    hits = jnp.arange(total)[:, None] == jnp.concatenate(sources)[None, :]
    sent_gates = jnp.sum(
        jnp.where(hits[:, :, None], jnp.concatenate(dgate_rows)[None], 0.0), axis=1
    )
    got_gates = lax.all_to_all(sent_gates, EVERY, 0, 0, tiled=True)
    grad_probs = jnp.sum(got_gates.reshape(expert_count, halves, tok_rows), axis=1).T

    n_all, g_all = jnp.concatenate(n_rows), jnp.concatenate(g_rows)
    grad_wx = jnp.concatenate(
        [
            mm_tn(n_all, jnp.concatenate(gus)).astype(bf16),
            mm_tn(g_all, jnp.concatenate(scaled)).astype(bf16),
        ],
        axis=1,
    )
    grad_experts = join_experts(
        around_dp(grad_wx.reshape(z_count, d_rows, 3 * ffh)), local_experts, halves
    )
    mixture = []
    for k in range(z_count):
        y = (mm_nt(acts[k], w_down) * gate_parts[k]).astype(bf16)
        y = y.reshape(n_src, slot_cap, width)
        y = jnp.einsum("stc,scd->std", puts[k], y, preferred_element_type=f32).astype(bf16)
        y, _ = lax.optimization_barrier((y, scattered[-1]))
        mixture.append(group_scatter(y, k))
    output = hidden + sum(part.astype(f32) for part in mixture)

    grad_logits = (
        probs * (grad_probs - jnp.sum(probs * grad_probs, axis=-1, keepdims=True))
    ).astype(bf16)
    grad_n2 = grad_n2 + mm_nt(grad_logits, router_w)
    router_term = mm_tn(normed_two, grad_logits)

    def norm_back(v, scale, gain, grad):
        pulled = grad * gain
        inner = jnp.mean(v * pulled, axis=-1, keepdims=True)
        return scale * pulled - v * (scale * scale * scale * inner)

    gain_two = jnp.sum(grad_n2 * hidden * scale_two, axis=0)
    grad_hidden = grad_out + norm_back(hidden, scale_two, gains[1], grad_n2)
    grad_hidden_b = grad_hidden.astype(bf16)

    pack_dh = context_gather(grad_hidden_b)
    grad_mixed = mm_nt(pack_dh, wo_all).astype(bf16)
    grad_mixed_h = grad_mixed.reshape(pack_rows, local_heads, head_width)
    grad_soft = jnp.einsum("qhd,khd->hqk", grad_mixed_h, value, preferred_element_type=f32)
    delta = jnp.sum(soft * grad_soft, axis=2, keepdims=True)
    grad_scores = (soft * (grad_soft - delta)).astype(bf16)
    grad_query = jnp.einsum("hqk,khd->qhd", grad_scores, key, preferred_element_type=f32)
    grad_key = jnp.einsum("hqk,qhd->khd", grad_scores, query, preferred_element_type=f32)
    grad_value = jnp.einsum("hqk,qhd->khd", soft_b, grad_mixed_h, preferred_element_type=f32)
    back_q, back_k = turn_back(grad_query * score_scale), turn_back(grad_key * score_scale)
    gain_q = jnp.sum(back_q * unit_q, axis=0)
    gain_k = jnp.sum(back_k * unit_k, axis=0)
    pull_q, pull_k = back_q * my_gains[0], back_k * my_gains[1]
    inner = jnp.stack([jnp.sum(raw_q * pull_q, axis=1), jnp.sum(raw_k * pull_k, axis=1)])
    inner = (lax.psum(inner, "context") / width)[:, :, None]
    grad_qkv = jnp.concatenate(
        [
            scale_qk[0] * pull_q - raw_q * (scale_qk[0] ** 3 * inner[0]),
            scale_qk[1] * pull_k - raw_k * (scale_qk[1] ** 3 * inner[1]),
            grad_value.reshape(pack_rows, cols),
        ],
        axis=1,
    ).astype(bf16)
    grad_n1 = context_scatter(mm_nt(grad_qkv, wqkv_all))
    own_scale = lax.rsqrt(jnp.mean(inputs * inputs, axis=-1, keepdims=True) + epsilon)
    gain_one = jnp.sum(grad_n1 * inputs * own_scale, axis=0)
    grad_tokens = grad_hidden + norm_back(inputs, own_scale, gains[0], grad_n1)

    grad_wqkv = mm_tn(normed_one, grad_qkv).reshape(e_count, c_count, z_count, w_rows, 3 * cols)
    grad_wqkv = relative_scatter(grad_wqkv.transpose(0, 2, 1, 3, 4)).astype(bf16)
    grad_wqkv = (
        lax.all_to_all(grad_wqkv, "context", 0, 0, tiled=True)
        .reshape(c_count, w_rows, 3, runs, run_cols)
        .transpose(1, 2, 3, 0, 4)
        .reshape(w_rows, 3 * width)
        .astype(f32)
    )
    grad_wo = mm_tn(mixed, pack_dh)
    if aligned:
        grad_wo = relative_scatter(grad_wo.reshape(e_count, z_count, w_rows, width))
    else:
        whole_wo = lax.dynamic_update_slice_in_dim(
            jnp.zeros((width, width), f32), grad_wo, me_c * cols, axis=0
        )
        grad_wo = lax.psum_scatter(
            whole_wo.astype(bf16), EVERY, scatter_dimension=0, tiled=True
        ).astype(f32)
    grad_attn = jnp.concatenate([grad_wqkv, grad_wo], axis=1)

    mine = jnp.arange(c_count)[None, None, :, None] == me_c
    gain_qk = jnp.where(mine, jnp.stack([gain_q, gain_k]).reshape(2, runs, 1, run_cols), 0.0)
    gain_rows = jnp.concatenate([jnp.stack([gain_one, gain_two]), gain_qk.reshape(2, width)])
    gain_rows = gain_rows.reshape(4, total, -1).transpose(1, 0, 2).reshape(total, -1)
    small_grads = jnp.concatenate([router_term.reshape(total, -1), gain_rows], axis=1)
    small_grads = jnp.sum(lax.all_to_all(small_grads, EVERY, 0, 0, tiled=True), axis=0)
    grad_router = small_grads[:n_router].reshape(w_router.shape)
    grad_gains = small_grads[n_router:].reshape(norm_gains.shape)
    return (output[None], grad_tokens[None], grad_attn, grad_router, grad_gains, grad_experts)


def solution(mesh):
    in_specs = (
        P(("expert", "dp"), "context", None),
        P(("expert", "dp"), "context", None),
        P(EVERY, None),
        P(EVERY, None),
        P(None, EVERY),
        P("dp", ("expert", "context"), None),
        P(("expert", "dp"), None),
        P(("expert", "dp"), None),
        P(("expert", "dp"), "context", None),
    )
    out_specs = (
        P(("expert", "dp"), "context", None),
        P(("expert", "dp"), "context", None),
        P(EVERY, None),
        P(EVERY, None),
        P(None, EVERY),
        P("dp", ("expert", "context"), None),
    )
    return jax.shard_map(
        on_device, mesh=mesh, in_specs=in_specs, out_specs=out_specs, check_vma=False
    )
```

```python
import jax
import jax.numpy as jnp
from jax import lax
from jax.experimental import pallas as pl
from jax.experimental.pallas import tpu as pltpu
from jax.sharding import PartitionSpec as P

HEADS = 16
epsilon = 1e-05
rope_base = 10000.0
masked_score = -1e30
bf16 = jnp.bfloat16
f32 = jnp.float32
EVERY = ("expert", "context", "dp")


def mm(a, b):
    return jnp.dot(a, b, preferred_element_type=f32)


def mm_nt(a, b):
    return lax.dot_general(a, b, (((1,), (1,)), ((), ())), preferred_element_type=f32)


def mm_tn(a, b):
    return lax.dot_general(a, b, (((0,), (0,)), ((), ())), preferred_element_type=f32)


def swap(value, axis, bit):
    count = lax.axis_size(axis)
    return lax.ppermute(value, axis, [(i, i ^ bit) for i in range(count)])


def shift(value, axis, step):
    count = lax.axis_size(axis)
    return lax.ppermute(value, axis, [(i, (i + step) % count) for i in range(count)])


def bits_of(axis):
    count = lax.axis_size(axis)
    return [1 << i for i in range(count.bit_length() - 1)]


def locate(stored_rows, doc_lens, blk_order, blk_rows):
    block_ids = stored_rows // blk_rows
    block_hits = block_ids[:, None] == jnp.arange(blk_order.shape[0], dtype=jnp.int32)[None, :]
    placed_at = (
        jnp.sum(jnp.where(block_hits, blk_order[None, :], 0), axis=1) * blk_rows
        + stored_rows % blk_rows
    )
    doc_count = doc_lens.shape[0]
    upto = jnp.arange(doc_count)[:, None] >= jnp.arange(doc_count)[None, :]
    doc_ends = jnp.sum(jnp.where(upto, doc_lens[None, :], 0), axis=1)
    doc_ids = jnp.sum((placed_at[:, None] >= doc_ends[None, :]).astype(jnp.int32), axis=1)
    doc_hits = doc_ids[:, None] == jnp.arange(doc_count, dtype=jnp.int32)[None, :]
    doc_starts = doc_ends - doc_lens
    offset = placed_at - jnp.sum(jnp.where(doc_hits, doc_starts[None, :], 0), axis=1)
    return placed_at, doc_ids, offset


def context_gather(value):
    me = lax.axis_index("context")
    parts = [value]
    for bit in reversed(bits_of("context")):
        parts = parts + [swap(part, "context", bit) for part in parts]
    count = len(parts)
    order = []
    for r in range(count):
        source = 0
        for i, bit in enumerate(reversed(bits_of("context"))):
            if r >> i & 1:
                source |= bit
        order.append(source)
    stack = [None] * count
    for r in range(count):
        stack[order[r]] = parts[r]
    rows = []
    for target in range(count):
        rows.append(
            sum(
                jnp.where(me == target ^ m, stack[m], jnp.zeros_like(stack[m])) for m in range(count)
            )
        )
    return jnp.concatenate(rows, axis=0)


def half_step(value, axis, bit, dim):
    mine = (lax.axis_index(axis) // bit) % 2
    keep = lax.dynamic_index_in_dim(value, mine, dim, keepdims=False)
    send = lax.dynamic_index_in_dim(value, 1 - mine, dim, keepdims=False).astype(bf16)
    return keep.astype(f32) + swap(send, axis, bit).astype(f32)


def context_scatter(value):
    bits = bits_of("context")
    rows = value.shape[0] >> len(bits)
    value = value.reshape((2,) * len(bits) + (rows, value.shape[1]))
    left = list(reversed(bits))
    for bit in bits:
        dim = left.index(bit)
        value = half_step(value, "context", bit, dim)
        left.remove(bit)
    return value


def after(value, *done):
    return lax.optimization_barrier((value,) + done)[0] if done else value


def tie(*values):
    return lax.optimization_barrier(values)


def near_step():
    return ("context", bits_of("context")[0])


def far_steps():
    steps = [("context", b) for b in bits_of("context")[1:]]
    return steps + [("expert", b) for b in bits_of("expert")]


def source_order():
    steps = [near_step()] + far_steps()
    me = {axis: lax.axis_index(axis) for axis in EVERY}
    c_count, z_count = lax.axis_size("context"), lax.axis_size("dp")
    order = []
    for i in range(1 << len(steps)):
        masks = {"expert": 0, "context": 0}
        for j, (axis, bit) in enumerate(steps):
            if i >> (len(steps) - 1 - j) & 1:
                masks[axis] |= bit
        column = (me["expert"] ^ masks["expert"]) * c_count + (me["context"] ^ masks["context"])
        order += [column * z_count + z for z in range(z_count)]
    return jnp.stack(order).astype(jnp.int32)


class Gather:
    def __init__(self, value):
        around = [value]
        for _ in range(lax.axis_size("dp") - 1):
            around.append(shift(around[-1], "dp", 1))
        far = far_steps()
        half = value.shape[1] // 2
        shape = (-1, value.shape[0], half)
        self.near, self.other, self.first = [], [], []
        for i in range(2):
            held = jnp.stack([part[:, i * half : (i + 1) * half] for part in around])
            held = held.reshape((1,) * len(far) + held.shape)
            for level, step in enumerate(far[::-1] if i else far):
                got = swap(held, *step)
                self.first += [got] if level == 0 else []
                held = jnp.concatenate([held, got], axis=far.index(step))
            self.near.append(held.reshape(shape))
            self.other.append(swap(held, *near_step()).reshape(shape))

    def order(self):
        z_count = lax.axis_size("dp")
        spots = jnp.arange(self.near[0].shape[0], dtype=jnp.int32)
        return spots // z_count * z_count + (lax.axis_index("dp") - spots) % z_count


class Scatter:
    def __init__(self, send, rows):
        self.far = far_steps()
        self.shape = (2,) * len(self.far) + (lax.axis_size("dp"), rows)
        self.got = swap(send, *near_step())

    def begin(self, keep, *done):
        far, width = self.far, keep.shape[-1]
        half = width // 2
        keep = keep.reshape(self.shape + (width,))
        got = after(self.got, *done).reshape(self.shape + (width,))
        self.states = []
        for i in range(2):
            cut = slice(i * half, (i + 1) * half)
            self.states.append((keep[..., cut], got[..., cut], far[::-1] if i else far, list(far)))

    def step(self, *done):
        sums = []
        arrived = [state[1] for state in self.states]
        arrived = after(arrived, *done) if done else arrived
        for (own, _, order, left), other in zip(self.states, arrived):
            step = order[len(order) - len(left)]
            dim = left.index(step)
            first = [slice(None)] * dim + [0]
            second = [slice(None)] * dim + [1]
            sent = own[tuple(second)].astype(f32) + other[tuple(second)].astype(f32)
            kept = own[tuple(first)].astype(f32) + other[tuple(first)].astype(f32)
            got = swap(sent.astype(bf16), *step)
            sums.append((kept.astype(bf16), got, order, left[:dim] + left[dim + 1 :]))
        self.states = sums
        return [state[1] for state in sums]

    def steps_left(self):
        return len(self.states[0][3])

    def cross(self, *done):
        blocks = jnp.concatenate(
            [
                (own.astype(f32) + got.astype(f32)).astype(bf16)
                for own, got, _, _ in self.states
            ],
            axis=-1,
        )
        return exchange(blocks, *done)


def sources_per_block(slot_cap):
    count = 1
    while count * slot_cap % 16:
        count *= 2
    return count


def take_kernel(per, slot_cap, order_ref, slot_ref, *refs):
    *rows, out_ref = refs
    places = lax.broadcasted_iota(jnp.int32, (slot_cap, slot_ref.shape[2]), 0)
    picks = [(slot_ref[j] == places).astype(f32).astype(bf16) for j in range(per)]
    at = 0
    for p in range(0, len(rows), per):
        part = [jnp.dot(picks[j], rows[p + j][0], preferred_element_type=f32) for j in range(per)]
        width = part[0].shape[1]
        out_ref[:, at : at + width] = jnp.concatenate(part).astype(bf16)
        at += width


def take_rows(parts, order, slots, slot_cap):
    count = order.shape[0]
    tokens = slots.shape[1]
    per = sources_per_block(slot_cap)
    width = sum(part.shape[2] for part in parts)

    def block_of(part, j):
        return pl.BlockSpec(
            (1, tokens, part.shape[2]), lambda i, order_ref: (order_ref[i * per + j], 0, 0)
        )

    return pl.pallas_call(
        lambda *refs: take_kernel(per, slot_cap, *refs),
        grid_spec=pltpu.PrefetchScalarGridSpec(
            num_scalar_prefetch=1,
            grid=(count // per,),
            in_specs=[pl.BlockSpec((per, 1, tokens), lambda i, order_ref: (i, 0, 0))]
            + [block_of(part, j) for part in parts for j in range(per)],
            out_specs=pl.BlockSpec((per * slot_cap, width), lambda i, order_ref: (i, 0)),
        ),
        out_shape=jax.ShapeDtypeStruct((count * slot_cap, width), bf16),
        compiler_params=pltpu.CompilerParams(vmem_limit_bytes=40 * 2**20),
    )(order, slots.reshape(count, 1, tokens), *[part for part in parts for _ in range(per)])


def put_kernel(per, slot_cap, slot_ref, rows_ref, out_ref):
    places = lax.broadcasted_iota(jnp.int32, (slot_cap, slot_ref.shape[2]), 0)
    rows = rows_ref[...].astype(f32)
    for j in range(per):
        pick = (slot_ref[j] == places).astype(f32).astype(bf16)
        part = rows[j * slot_cap : (j + 1) * slot_cap].astype(bf16)
        out_ref[j] = mm_tn(pick, part).astype(bf16)


def put_rows(rows, slots, slot_cap, first, count):
    width = rows.shape[1]
    total, tokens = slots.shape
    per = sources_per_block(slot_cap)
    skip = first // per
    return pl.pallas_call(
        lambda *refs: put_kernel(per, slot_cap, *refs),
        grid=(count // per,),
        in_specs=[
            pl.BlockSpec((per, 1, tokens), lambda i: (i + skip, 0, 0)),
            pl.BlockSpec((per * slot_cap, width), lambda i: (i + skip, 0)),
        ],
        out_specs=pl.BlockSpec((per, tokens, width), lambda i: (i, 0, 0)),
        out_shape=jax.ShapeDtypeStruct((count, tokens, width), bf16),
        compiler_params=pltpu.CompilerParams(vmem_limit_bytes=40 * 2**20),
    )(slots.reshape(total, 1, tokens), rows)


def exchange(blocks, *done):
    return lax.all_to_all(after(blocks, *done), "dp", 0, 0, tiled=True)


def split_kernel(experts, halves, w_ref, *out_refs):
    ffh = out_refs[0].shape[2]
    for e in range(experts):
        rows = w_ref[:, e, :].astype(bf16)
        for h in range(halves):
            for j in range(3):
                at = (j * halves + h) * ffh
                out_refs[j][e * halves + h] = rows[:, at : at + ffh]


def split_experts(w, halves):
    rows, experts, width = w.shape
    block, shares, ffh = 64, experts * halves, width // (3 * halves)
    return pl.pallas_call(
        lambda *refs: split_kernel(experts, halves, *refs),
        grid=(rows // block,),
        in_specs=[pl.BlockSpec((block, experts, width), lambda i: (i, 0, 0))],
        out_specs=[pl.BlockSpec((shares, block, ffh), lambda i: (0, i, 0))] * 3,
        out_shape=[jax.ShapeDtypeStruct((shares, rows, ffh), bf16)] * 3,
        compiler_params=pltpu.CompilerParams(vmem_limit_bytes=32 * 2**20),
    )(w)


def join_kernel(halves, gate_ref, up_ref, down_ref, out_ref):
    shares, _, ffh = gate_ref.shape
    for t in range(shares):
        e, h = divmod(t, halves)
        for j, ref in enumerate((gate_ref, up_ref, down_ref)):
            at = (j * halves + h) * ffh
            out_ref[:, e, at : at + ffh] = ref[t].astype(f32)


def join_experts(gate, up, down, halves):
    shares, rows, ffh = gate.shape
    block, experts, width = 64, shares // halves, 3 * ffh * halves
    return pl.pallas_call(
        lambda *refs: join_kernel(halves, *refs),
        grid=(rows // block,),
        in_specs=[pl.BlockSpec((shares, block, ffh), lambda i: (0, i, 0))] * 3,
        out_specs=pl.BlockSpec((block, experts, width), lambda i: (i, 0, 0)),
        out_shape=jax.ShapeDtypeStruct((rows, experts, width), f32),
        compiler_params=pltpu.CompilerParams(vmem_limit_bytes=32 * 2**20),
    )(gate, up, down)


def relative_scatter(value, *done, late=()):
    for bit in reversed(bits_of("expert")):
        value = value.reshape((value.shape[0] // 2, 2) + value.shape[1:]) if bit == 1 else value
        if bit == 1:
            value = half_step(value, "expert", 1, 1)
        else:
            value = value.reshape((2, value.shape[0] // 2) + value.shape[1:])
            value = half_step(value, "expert", bit, 0)
    arrived = exchange(value[0].astype(bf16), *done)
    return jnp.sum(arrived.astype(f32), axis=0), arrived


def on_device(
    tokens, cotangent, w_attn, w_router, norm_gains, w_experts, lengths, block_order, routes
):
    tok_rows, width = tokens.shape[1:]
    blk_rows = tok_rows // 2
    e_count, c_count, z_count = (lax.axis_size(a) for a in EVERY)
    total = e_count * c_count * z_count
    me_e, me_c, me_z = (lax.axis_index(a) for a in EVERY)
    pack_rows = tok_rows * c_count
    pick_rows = routes[0]
    top_count = pick_rows.shape[1]
    local_experts = w_experts.shape[1]
    expert_count = local_experts * e_count * c_count
    slot_cap = tok_rows * top_count * 9 // (8 * expert_count)
    ffn = w_experts.shape[2] // 3
    halves = z_count // local_experts
    ffh = ffn // halves
    head_width = width // HEADS
    local_heads = HEADS // c_count
    cols = local_heads * head_width
    w_rows = w_attn.shape[0]
    score_scale = head_width ** (-0.5)
    block_rows = z_count * w_rows
    aligned = block_rows % head_width == 0
    head_run = block_rows // head_width if aligned else local_heads
    runs = local_heads // head_run
    run_cols = head_run * head_width

    expert_ids = jnp.arange(expert_count, dtype=jnp.int32)
    pick_hits = (pick_rows[:, :, None] == expert_ids[None, None, :]).astype(f32)
    named = jnp.sum(pick_hits, axis=1)
    earlier = jnp.arange(tok_rows)[:, None] > jnp.arange(tok_rows)[None, :]
    ranks = mm(earlier.astype(bf16), named.astype(bf16))
    rank_rows = jnp.repeat(jnp.where(named > 0, ranks, -1.0).T, halves, axis=0)
    own_row = jnp.concatenate(
        [w_router.astype(bf16).reshape(-1), norm_gains.astype(bf16).reshape(-1)]
    )
    small_sent = jnp.concatenate(
        [jnp.broadcast_to(own_row[None], (total, own_row.shape[0])), rank_rows.astype(bf16)], axis=1
    )
    wqkv = (
        w_attn[:, : 3 * width]
        .astype(bf16)
        .reshape(w_rows, 3, runs, c_count, run_cols)
        .transpose(3, 0, 1, 2, 4)
        .reshape(c_count, w_rows, 3 * cols)
    )
    wqkv = lax.all_to_all(wqkv, "context", 0, 0, tiled=True).reshape(c_count * w_rows, 3 * cols)
    small_sent = after(small_sent, wqkv)
    small = lax.all_to_all(small_sent, EVERY, 0, 0, tiled=True)
    n_router = w_router.size
    router_w = small[:, :n_router].reshape(width, expert_count)
    gains = (
        small[:, n_router : n_router + norm_gains.size]
        .reshape(total, 4, norm_gains.shape[1])
        .transpose(1, 0, 2)
        .reshape(4, width)
        .astype(f32)
    )
    slot_of = small[:, n_router + norm_gains.size :].astype(jnp.int32)

    grad_out = cotangent[0]
    gate_blocks, up_blocks, down_blocks = split_experts(w_experts, halves)
    around = ("expert", "dp")
    wqkv_all = lax.all_gather(wqkv, around, axis=0, tiled=True)
    g_gather = Gather(grad_out.astype(bf16))
    wqkv_all = (
        wqkv_all.reshape(e_count, z_count, c_count, w_rows, 3 * cols)
        .transpose(0, 2, 1, 3, 4)
        .reshape(width, 3 * cols)
    )
    wo_own = w_attn[:, 3 * width :].astype(bf16)
    if aligned:
        wo_all = lax.all_gather(after(wo_own, wqkv_all), around, axis=0, tiled=True)
    else:
        wo_full = lax.all_gather(wo_own, EVERY, axis=0, tiled=True)
        wo_all = lax.dynamic_slice_in_dim(wo_full, me_c * cols, cols, axis=0)

    w_down = exchange(down_blocks, wqkv_all)
    w_gate = exchange(gate_blocks, w_down)
    w_up = exchange(up_blocks, w_gate)
    w_gu = jnp.concatenate([w_gate.reshape(width, ffh), w_up.reshape(width, ffh)], axis=1)

    inputs = tokens[0].astype(f32)
    pack_x = context_gather(tokens[0]).astype(f32)
    scale_one = lax.rsqrt(jnp.mean(pack_x * pack_x, axis=-1, keepdims=True) + epsilon)
    normed_one = (pack_x * scale_one * gains[0]).astype(bf16)
    qkv = mm(after(normed_one, gate_blocks, *g_gather.first), wqkv_all)
    place, doc, offset = locate(
        jnp.arange(pack_rows, dtype=jnp.int32), lengths[0], block_order[0], blk_rows
    )
    half_width = head_width // 2
    freq = rope_base ** (-2.0 * jnp.arange(half_width, dtype=f32) / head_width)
    angle = offset.astype(f32)[:, None] * freq[None, :]
    cos_t, sin_t = jnp.cos(angle), jnp.sin(angle)
    cos_all = jnp.concatenate([cos_t, cos_t], axis=1)[:, None, :]
    sin_all = jnp.concatenate([-sin_t, sin_t], axis=1)[:, None, :]

    def turn(v):
        v = v.reshape(pack_rows, local_heads, head_width)
        return v * cos_all + jnp.roll(v, half_width, axis=2) * sin_all

    def turn_back(v):
        return (v * cos_all + jnp.roll(v * sin_all, half_width, axis=2)).reshape(pack_rows, cols)

    my_gains = lax.dynamic_index_in_dim(
        gains[2:].reshape(2, runs, c_count, run_cols), me_c, 2, keepdims=False
    ).reshape(2, cols)
    raw_q, raw_k = qkv[:, :cols], qkv[:, cols : 2 * cols]
    value = qkv[:, 2 * cols :].astype(bf16).reshape(pack_rows, local_heads, head_width)
    squares = jnp.stack([jnp.sum(raw_q * raw_q, axis=1), jnp.sum(raw_k * raw_k, axis=1)])
    scale_qk = lax.rsqrt(lax.psum(squares, "context") / width + epsilon)[:, :, None]
    unit_q, unit_k = raw_q * scale_qk[0], raw_k * scale_qk[1]
    query = turn(unit_q * my_gains[0]).astype(bf16)
    key = turn(unit_k * my_gains[1]).astype(bf16)
    scores = jnp.einsum("qhd,khd->hqk", query, key, preferred_element_type=f32) * score_scale
    allowed = (doc[:, None] == doc[None, :]) & (place[None, :] <= place[:, None])
    scores = jnp.where(allowed[None], scores, masked_score)
    top = jnp.max(scores, axis=2, keepdims=True)
    raised = jnp.exp(scores - top)
    soft = raised / jnp.sum(raised, axis=2, keepdims=True)
    soft_b = after(soft.astype(bf16), w_down)
    mixed = (
        jnp.einsum("hqk,khd->qhd", soft_b, value, preferred_element_type=f32)
        .reshape(pack_rows, cols)
        .astype(bf16)
    )
    hidden = after(inputs + context_scatter(mm(mixed, wo_all)), w_gate)
    scale_two = lax.rsqrt(jnp.mean(hidden * hidden, axis=-1, keepdims=True) + epsilon)
    normed_two = (hidden * scale_two * gains[1]).astype(bf16)
    logits = mm(normed_two, router_w)
    probs = jax.nn.softmax(logits, axis=-1)

    order = source_order()
    all_normed = lax.all_gather(normed_two, EVERY, axis=0, tiled=True)
    all_normed = all_normed.reshape(total, tok_rows, width)
    gate_rows = lax.all_to_all(jnp.repeat(probs.T, halves, axis=0), EVERY, 0, 0, tiled=True)
    slots = jnp.arange(slot_cap, dtype=jnp.int32)
    slot_of = slot_of[order]
    gate_rows = gate_rows[order]
    gate = jnp.sum(
        jnp.where(slot_of[:, None, :] == slots[None, :, None], gate_rows[:, None, :], 0.0), axis=2
    ).reshape(total * slot_cap, 1)
    side = total // 2
    g_rows = jnp.concatenate(
        [
            take_rows(g_gather.near, g_gather.order(), slot_of[:side], slot_cap),
            take_rows(g_gather.other, g_gather.order(), slot_of[side:], slot_cap),
        ]
    )
    w_down = w_down.reshape(width, ffh)
    back = mm(g_rows, w_down)
    n_rows = take_rows([after(all_normed, back)], order, slot_of, slot_cap)
    gate_up = mm(n_rows, w_gu)
    gate_part, up_part = gate_up[:, :ffh], gate_up[:, ffh:]
    sig = jax.nn.sigmoid(gate_part)
    silu = gate_part * sig
    act = (silu * up_part).astype(bf16)
    act_f = act.astype(f32)
    grad_gate_slot = jnp.sum(act_f * back, axis=1).reshape(total, slot_cap)
    grad_act = back * gate
    grad_gu = jnp.concatenate(
        [grad_act * up_part * sig * (1.0 + gate_part * (1.0 - sig)), grad_act * silu], axis=1
    ).astype(bf16)
    act_scaled = (act_f * gate).astype(bf16)
    grad_wd = mm_tn(g_rows, act_scaled).astype(bf16)
    down_got = exchange(grad_wd.reshape(z_count, -1, ffh))
    hits = jnp.arange(total)[:, None] == order[None, :]
    sent_gates = jnp.sum(
        jnp.where(slot_of[:, :, None] == slots[None, None, :], grad_gate_slot[:, None, :], 0.0),
        axis=2,
    )
    sent_gates = jnp.sum(jnp.where(hits[:, :, None], sent_gates[None], 0.0), axis=1)
    got_gates = lax.all_to_all(sent_gates, EVERY, 0, 0, tiled=True)
    grad_rows = mm_nt(after(grad_gu, grad_wd), w_gu).astype(bf16)
    grad_rows, got_gates = tie(grad_rows, got_gates)
    grad_probs = jnp.sum(got_gates.reshape(expert_count, halves, tok_rows), axis=1).T
    n2_sum = Scatter(put_rows(grad_rows, slot_of, slot_cap, side, side), tok_rows)
    n2_keep = put_rows(grad_rows, slot_of, slot_cap, 0, side)
    n_late, gu_late, _ = tie(n_rows, grad_gu, n2_keep)
    grad_wg = mm_tn(n_late, gu_late[:, :ffh]).astype(bf16)
    grad_wu = mm_tn(n_late, gu_late[:, ffh:]).astype(bf16)
    n2_sum.begin(n2_keep)
    n2_spread = n2_sum.step()
    gate_got = exchange(grad_wg.reshape(z_count, -1, ffh), down_got)
    y_rows = (mm_nt(after(act, n2_sum.got), w_down) * gate).astype(bf16)
    y_sum = Scatter(put_rows(y_rows, slot_of, slot_cap, side, side), tok_rows)
    y_keep = put_rows(y_rows, slot_of, slot_cap, 0, side)
    n2_spread = n2_sum.step(down_got)
    while n2_sum.steps_left():
        n2_spread = n2_sum.step()
    n2_last = n2_sum.cross(gate_got)
    y_sum.begin(y_keep, *n2_spread)
    y_far = y_sum.step()
    n2_last = tie(n2_last, *y_far)[0]
    grad_n2 = jnp.sum(n2_last.astype(f32), axis=0)
    up_got = exchange(grad_wu.reshape(z_count, -1, ffh), n2_last)

    grad_logits = (
        probs * (grad_probs - jnp.sum(probs * grad_probs, axis=-1, keepdims=True))
    ).astype(bf16)
    grad_n2 = grad_n2 + mm_nt(grad_logits, router_w)
    router_term = mm_tn(normed_two, grad_logits)

    def norm_back(v, scale, gain, grad):
        pulled = grad * gain
        inner = jnp.mean(v * pulled, axis=-1, keepdims=True)
        return scale * pulled - v * (scale * scale * scale * inner)

    gain_two = jnp.sum(grad_n2 * hidden * scale_two, axis=0)
    grad_hidden = grad_out + norm_back(hidden, scale_two, gains[1], grad_n2)
    grad_hidden_b = grad_hidden.astype(bf16)

    pack_dh = context_gather(grad_hidden_b)
    while y_sum.steps_left():
        y_far = y_sum.step()
    pack_dh, *_ = tie(pack_dh, *y_far)
    y_last = y_sum.cross(up_got, pack_dh)
    output = hidden + jnp.sum(y_last.astype(f32), axis=0)
    grad_mixed = mm_nt(pack_dh, wo_all).astype(bf16)
    grad_mixed_h = grad_mixed.reshape(pack_rows, local_heads, head_width)
    grad_soft = jnp.einsum("qhd,khd->hqk", grad_mixed_h, value, preferred_element_type=f32)
    delta = jnp.sum(soft * grad_soft, axis=2, keepdims=True)
    grad_scores = (soft * (grad_soft - delta)).astype(bf16)
    grad_query = jnp.einsum("hqk,khd->qhd", grad_scores, key, preferred_element_type=f32)
    grad_key = jnp.einsum("hqk,qhd->khd", grad_scores, query, preferred_element_type=f32)
    grad_value = jnp.einsum("hqk,qhd->khd", soft_b, grad_mixed_h, preferred_element_type=f32)
    grad_v = grad_value.reshape(pack_rows, cols).astype(bf16)
    back_q, back_k = turn_back(grad_query * score_scale), turn_back(grad_key * score_scale)
    gain_q = jnp.sum(back_q * unit_q, axis=0)
    gain_k = jnp.sum(back_k * unit_k, axis=0)
    pull_q, pull_k = back_q * my_gains[0], back_k * my_gains[1]
    inner = jnp.stack([jnp.sum(raw_q * pull_q, axis=1), jnp.sum(raw_k * pull_k, axis=1)])
    inner = (lax.psum(inner, "context") / width)[:, :, None]
    grad_qkv = jnp.concatenate(
        [
            scale_qk[0] * pull_q - raw_q * (scale_qk[0] ** 3 * inner[0]),
            scale_qk[1] * pull_k - raw_k * (scale_qk[1] ** 3 * inner[1]),
            grad_v,
        ],
        axis=1,
    ).astype(bf16)
    grad_experts = join_experts(gate_got, up_got, down_got, halves)
    grad_n1 = context_scatter(mm_nt(grad_qkv, wqkv_all))
    own_scale = lax.rsqrt(jnp.mean(inputs * inputs, axis=-1, keepdims=True) + epsilon)
    gain_one = jnp.sum(grad_n1 * inputs * own_scale, axis=0)
    grad_tokens = grad_hidden + norm_back(inputs, own_scale, gains[0], grad_n1)


    def weight_blocks(left, right):
        blocks = mm_tn(left, right).reshape(e_count, c_count, z_count, w_rows, right.shape[1])
        return blocks.transpose(0, 2, 1, 3, 4)

    grad_v_sum, v_last = relative_scatter(weight_blocks(normed_one, grad_v), y_last)
    grad_wo = mm_tn(mixed, pack_dh)
    if aligned:
        grad_wo, last = relative_scatter(grad_wo.reshape(e_count, z_count, w_rows, width), v_last)
    else:
        whole_wo = lax.dynamic_update_slice_in_dim(
            jnp.zeros((width, width), f32), grad_wo, me_c * cols, axis=0
        )
        grad_wo = lax.psum_scatter(
            whole_wo.astype(bf16), EVERY, scatter_dimension=0, tiled=True
        ).astype(f32)
        last = v_last
    grad_qk_sum, _ = relative_scatter(weight_blocks(normed_one, grad_qkv[:, : 2 * cols]), last)
    grad_wqkv = jnp.concatenate([grad_qk_sum, grad_v_sum], axis=2).astype(bf16)
    grad_wqkv = (
        lax.all_to_all(grad_wqkv, "context", 0, 0, tiled=True)
        .reshape(c_count, w_rows, 3, runs, run_cols)
        .transpose(1, 2, 3, 0, 4)
        .reshape(w_rows, 3 * width)
        .astype(f32)
    )
    grad_attn = jnp.concatenate([grad_wqkv, grad_wo], axis=1)

    mine = jnp.arange(c_count)[None, None, :, None] == me_c
    gain_qk = jnp.where(mine, jnp.stack([gain_q, gain_k]).reshape(2, runs, 1, run_cols), 0.0)
    gain_rows = jnp.concatenate([jnp.stack([gain_one, gain_two]), gain_qk.reshape(2, width)])
    gain_rows = gain_rows.reshape(4, total, -1).transpose(1, 0, 2).reshape(total, -1)
    small_grads = jnp.concatenate([router_term.reshape(total, -1), gain_rows], axis=1)
    small_grads = jnp.sum(lax.all_to_all(small_grads, EVERY, 0, 0, tiled=True), axis=0)
    grad_router = small_grads[:n_router].reshape(w_router.shape)
    grad_gains = small_grads[n_router:].reshape(norm_gains.shape)
    return (output[None], grad_tokens[None], grad_attn, grad_router, grad_gains, grad_experts)


def solution(mesh):
    in_specs = (
        P(("expert", "dp"), "context", None),
        P(("expert", "dp"), "context", None),
        P(EVERY, None),
        P(EVERY, None),
        P(None, EVERY),
        P("dp", ("expert", "context"), None),
        P(("expert", "dp"), None),
        P(("expert", "dp"), None),
        P(("expert", "dp"), "context", None),
    )
    out_specs = (
        P(("expert", "dp"), "context", None),
        P(("expert", "dp"), "context", None),
        P(EVERY, None),
        P(EVERY, None),
        P(None, EVERY),
        P("dp", ("expert", "context"), None),
    )
    return jax.shard_map(
        on_device, mesh=mesh, in_specs=in_specs, out_specs=out_specs, check_vma=False
    )
```

```python
import jax
import jax.numpy as jnp
from jax import lax
from jax.experimental import pallas as pl
from jax.experimental.pallas import tpu as pltpu
from jax.sharding import PartitionSpec as P

HEADS = 16
epsilon = 1e-05
rope_base = 10000.0
masked_score = -1e30
bf16 = jnp.bfloat16
f32 = jnp.float32
EVERY = ("expert", "context", "dp")
QUICK = pl.CostEstimate(flops=1, bytes_accessed=1, transcendentals=0)


def mm(a, b):
    return jnp.dot(a, b, preferred_element_type=f32)


def mm_nt(a, b):
    return lax.dot_general(a, b, (((1,), (1,)), ((), ())), preferred_element_type=f32)


def mm_tn(a, b):
    return lax.dot_general(a, b, (((0,), (0,)), ((), ())), preferred_element_type=f32)


def swap(value, axis, bit):
    count = lax.axis_size(axis)
    return lax.ppermute(value, axis, [(i, i ^ bit) for i in range(count)])


def shift(value, axis, step):
    count = lax.axis_size(axis)
    return lax.ppermute(value, axis, [(i, (i + step) % count) for i in range(count)])


def bits_of(axis):
    count = lax.axis_size(axis)
    return [1 << i for i in range(count.bit_length() - 1)]


def locate(stored_rows, doc_lens, blk_order, blk_rows):
    block_ids = stored_rows // blk_rows
    block_hits = block_ids[:, None] == jnp.arange(blk_order.shape[0], dtype=jnp.int32)[None, :]
    placed_at = (
        jnp.sum(jnp.where(block_hits, blk_order[None, :], 0), axis=1) * blk_rows
        + stored_rows % blk_rows
    )
    doc_count = doc_lens.shape[0]
    upto = jnp.arange(doc_count)[:, None] >= jnp.arange(doc_count)[None, :]
    doc_ends = jnp.sum(jnp.where(upto, doc_lens[None, :], 0), axis=1)
    doc_ids = jnp.sum((placed_at[:, None] >= doc_ends[None, :]).astype(jnp.int32), axis=1)
    doc_hits = doc_ids[:, None] == jnp.arange(doc_count, dtype=jnp.int32)[None, :]
    doc_starts = doc_ends - doc_lens
    offset = placed_at - jnp.sum(jnp.where(doc_hits, doc_starts[None, :], 0), axis=1)
    return placed_at, doc_ids, offset


def context_gather(value):
    me = lax.axis_index("context")
    parts = [value]
    for bit in reversed(bits_of("context")):
        parts = parts + [swap(part, "context", bit) for part in parts]
    count = len(parts)
    order = []
    for r in range(count):
        source = 0
        for i, bit in enumerate(reversed(bits_of("context"))):
            if r >> i & 1:
                source |= bit
        order.append(source)
    stack = [None] * count
    for r in range(count):
        stack[order[r]] = parts[r]
    rows = []
    for target in range(count):
        rows.append(
            sum(
                jnp.where(me == target ^ m, stack[m], jnp.zeros_like(stack[m])) for m in range(count)
            )
        )
    return jnp.concatenate(rows, axis=0)


def half_step(value, axis, bit, dim):
    mine = (lax.axis_index(axis) // bit) % 2
    keep = lax.dynamic_index_in_dim(value, mine, dim, keepdims=False)
    send = lax.dynamic_index_in_dim(value, 1 - mine, dim, keepdims=False).astype(bf16)
    return keep.astype(f32) + swap(send, axis, bit).astype(f32)


def context_scatter(value):
    bits = bits_of("context")
    rows = value.shape[0] >> len(bits)
    value = value.reshape((2,) * len(bits) + (rows, value.shape[1]))
    left = list(reversed(bits))
    for bit in bits:
        dim = left.index(bit)
        value = half_step(value, "context", bit, dim)
        left.remove(bit)
    return value


def after(value, *done):
    return lax.optimization_barrier((value,) + done)[0] if done else value


def tie(*values):
    return lax.optimization_barrier(values)


def near_step():
    return ("context", bits_of("context")[0])


def far_steps():
    steps = [("context", b) for b in bits_of("context")[1:]]
    return steps + [("expert", b) for b in bits_of("expert")]


def source_order():
    steps = [near_step()] + far_steps()
    me = {axis: lax.axis_index(axis) for axis in EVERY}
    c_count, z_count = lax.axis_size("context"), lax.axis_size("dp")
    order = []
    for i in range(1 << len(steps)):
        masks = {"expert": 0, "context": 0}
        for j, (axis, bit) in enumerate(steps):
            if i >> (len(steps) - 1 - j) & 1:
                masks[axis] |= bit
        column = (me["expert"] ^ masks["expert"]) * c_count + (me["context"] ^ masks["context"])
        order += [column * z_count + z for z in range(z_count)]
    return jnp.stack(order).astype(jnp.int32)


class Gather:
    def __init__(self, value):
        around = [value]
        for _ in range(lax.axis_size("dp") - 1):
            around.append(shift(around[-1], "dp", 1))
        self.ring, self.around = around[-1], around
        far = far_steps()
        half = value.shape[1] // 2
        shape = (-1, value.shape[0], half)
        self.near, self.other, self.first = [], [], []
        for i in range(2):
            held = jnp.stack([part[:, i * half : (i + 1) * half] for part in around])
            held = held.reshape((1,) * len(far) + held.shape)
            for level, step in enumerate(far[::-1] if i else far):
                got = swap(held, *step)
                self.first += [got] if level == 0 else []
                held = jnp.concatenate([held, got], axis=far.index(step))
            self.near.append(held.reshape(shape))
            self.other.append(swap(held, *near_step()).reshape(shape))

    def order(self):
        z_count = lax.axis_size("dp")
        spots = jnp.arange(self.near[0].shape[0], dtype=jnp.int32)
        return spots // z_count * z_count + (lax.axis_index("dp") - spots) % z_count


class Scatter:
    def __init__(self, send, rows):
        self.far = far_steps()
        self.shape = (2,) * len(self.far) + (lax.axis_size("dp"), rows)
        self.got = swap(send, *near_step())

    def begin(self, keep, *done):
        far, width = self.far, keep.shape[-1]
        half = width // 2
        keep = keep.reshape(self.shape + (width,))
        got = after(self.got, *done).reshape(self.shape + (width,))
        self.states = []
        for i in range(2):
            cut = slice(i * half, (i + 1) * half)
            self.states.append((keep[..., cut], got[..., cut], far[::-1] if i else far, list(far)))

    def step(self, other=None):
        sums = []
        for own, got, order, left in self.states:
            step = order[len(order) - len(left)]
            dim = left.index(step)
            first = [slice(None)] * dim + [0]
            second = [slice(None)] * dim + [1]
            sent = own[tuple(second)].astype(f32) + got[tuple(second)].astype(f32)
            kept = own[tuple(first)].astype(f32) + got[tuple(first)].astype(f32)
            sums.append([kept.astype(bf16), sent.astype(bf16), step, order, left[:dim] + left[dim + 1 :]])
        if other:
            sent = other.require(*[entry[1] for entry in sums])
            for entry, new in zip(sums, sent):
                entry[1] = new
        self.states = [
            (kept, swap(sent, *step), order, left) for kept, sent, step, order, left in sums
        ]

    def require(self, *values):
        count = len(self.states)
        *got, = tie(*[state[1] for state in self.states], *values)
        self.states = [
            state[:1] + (new,) + state[2:] for state, new in zip(self.states, got[:count])
        ]
        return got[count:]

    def kept(self):
        return [state[0] for state in self.states]

    def keep(self, kept):
        self.states = [(own,) + state[1:] for own, state in zip(kept, self.states)]

    def steps_left(self):
        return len(self.states[0][3])

    def cross(self, *done):
        blocks = jnp.concatenate(
            [
                (own.astype(f32) + got.astype(f32)).astype(bf16)
                for own, got, _, _ in self.states
            ],
            axis=-1,
        )
        return exchange(blocks, *done)


def sources_per_block(slot_cap):
    count = 1
    while count * slot_cap % 16:
        count *= 2
    return count


def take_kernel(per, slot_cap, order_ref, slot_ref, *refs):
    *rows, out_ref = refs
    places = lax.broadcasted_iota(jnp.int32, (slot_cap, slot_ref.shape[2]), 0)
    picks = [(slot_ref[j] == places).astype(f32).astype(bf16) for j in range(per)]
    at = 0
    for p in range(0, len(rows), per):
        part = [jnp.dot(picks[j], rows[p + j][0], preferred_element_type=f32) for j in range(per)]
        width = part[0].shape[1]
        out_ref[:, at : at + width] = jnp.concatenate(part).astype(bf16)
        at += width


def take_rows(parts, order, slots, slot_cap):
    count = order.shape[0]
    tokens = slots.shape[1]
    per = sources_per_block(slot_cap)
    width = sum(part.shape[2] for part in parts)

    def block_of(part, j):
        return pl.BlockSpec(
            (1, tokens, part.shape[2]), lambda i, order_ref: (order_ref[i * per + j], 0, 0)
        )

    return pl.pallas_call(
        lambda *refs: take_kernel(per, slot_cap, *refs),
        grid_spec=pltpu.PrefetchScalarGridSpec(
            num_scalar_prefetch=1,
            grid=(count // per,),
            in_specs=[pl.BlockSpec((per, 1, tokens), lambda i, order_ref: (i, 0, 0))]
            + [block_of(part, j) for part in parts for j in range(per)],
            out_specs=pl.BlockSpec((per * slot_cap, width), lambda i, order_ref: (i, 0)),
        ),
        out_shape=jax.ShapeDtypeStruct((count * slot_cap, width), bf16),
        cost_estimate=QUICK,
        compiler_params=pltpu.CompilerParams(vmem_limit_bytes=40 * 2**20),
    )(order, slots.reshape(count, 1, tokens), *[part for part in parts for _ in range(per)])


def output_kernel(per, slot_cap, slot_ref, act_ref, gate_ref, w_ref, out_ref):
    places = lax.broadcasted_iota(jnp.int32, (slot_cap, slot_ref.shape[2]), 0)
    rows = mm_nt(act_ref[...], w_ref[...]) * gate_ref[...]
    for j in range(per):
        pick = (slot_ref[j] == places).astype(f32).astype(bf16)
        part = rows[j * slot_cap : (j + 1) * slot_cap].astype(bf16)
        out_ref[j] = mm_tn(pick, part).astype(bf16)


def expert_output(act, gate, w_down, slots, slot_cap, side):
    total, tokens = slots.shape
    width, ffh = w_down.shape
    per = max(sources_per_block(slot_cap), 8)
    steps = total // 2 // per
    first = side * steps

    def rows_of(columns):
        return pl.BlockSpec((per * slot_cap, columns), lambda i: (i + first, 0))

    return pl.pallas_call(
        lambda *refs: output_kernel(per, slot_cap, *refs),
        grid=(steps,),
        in_specs=[
            pl.BlockSpec((per, 1, tokens), lambda i: (i + first, 0, 0)),
            rows_of(ffh),
            rows_of(1),
            pl.BlockSpec((width, ffh), lambda i: (0, 0)),
        ],
        out_specs=pl.BlockSpec((per, tokens, width), lambda i: (i, 0, 0)),
        out_shape=jax.ShapeDtypeStruct((total // 2, tokens, width), bf16),
        cost_estimate=pl.CostEstimate(
            flops=total * slot_cap * width * (ffh + tokens),
            bytes_accessed=total * tokens * width,
            transcendentals=0,
        ),
        compiler_params=pltpu.CompilerParams(vmem_limit_bytes=48 * 2**20),
    )(slots.reshape(total, 1, tokens), act, gate, w_down)


def turn(v, cos, sin):
    return v * cos + pltpu.roll(v, v.shape[1] // 2, 1) * sin


def turn_back(v, cos, sin):
    return v * cos + pltpu.roll(v * sin, v.shape[1] // 2, 1)


def soften(query, key, score_scale, spot_ref, spot_t_ref):
    scores = mm_nt(query, key) * score_scale
    same = spot_ref[:, 0:1] == spot_t_ref[0:1, :]
    allowed = same & (spot_t_ref[1:2, :] <= spot_ref[:, 1:2])
    scores = jnp.where(allowed, scores, masked_score)
    raised = jnp.exp(scores - jnp.max(scores, axis=1, keepdims=True))
    return raised / jnp.sum(raised, axis=1, keepdims=True)


def mix_kernel(score_scale, q_ref, k_ref, v_ref, scale_ref, gain_ref, cos_ref, sin_ref, *refs):
    spot_ref, spot_t_ref, query_ref, key_ref, value_ref, mixed_ref = refs
    cos, sin = cos_ref[...], sin_ref[...]
    query = turn(q_ref[...] * scale_ref[:, 0:1] * gain_ref[0:1, :], cos, sin).astype(bf16)
    key = turn(k_ref[...] * scale_ref[:, 1:2] * gain_ref[1:2, :], cos, sin).astype(bf16)
    value = v_ref[...].astype(bf16)
    soft = soften(query, key, score_scale, spot_ref, spot_t_ref)
    query_ref[...], key_ref[...], value_ref[...] = query, key, value
    mixed_ref[...] = mm(soft.astype(bf16), value).astype(bf16)


def mix_back_kernel(score_scale, q_ref, k_ref, scale_ref, gain_ref, cos_ref, sin_ref, *refs):
    spot_ref, spot_t_ref, query_ref, key_ref, value_ref, dh_ref, wo_ref = refs[:7]
    pull_q_ref, pull_k_ref, grad_v_ref, gain_out_ref, inner_ref = refs[7:]
    cos, sin = cos_ref[...], sin_ref[...]
    query, key, value = query_ref[...], key_ref[...], value_ref[...]
    grad_mixed = mm_nt(dh_ref[...], wo_ref[...]).astype(bf16)
    soft = soften(query, key, score_scale, spot_ref, spot_t_ref)
    grad_soft = mm_nt(grad_mixed, value)
    delta = jnp.sum(soft * grad_soft, axis=1, keepdims=True)
    grad_scores = (soft * (grad_soft - delta)).astype(bf16)
    grad_v_ref[...] = mm_tn(soft.astype(bf16), grad_mixed).astype(bf16)
    inner = []
    for i, (grad, raw_ref, out_ref) in enumerate(
        (
            (mm(grad_scores, key), q_ref, pull_q_ref),
            (mm_tn(grad_scores, query), k_ref, pull_k_ref),
        )
    ):
        back = turn_back(grad * score_scale, cos, sin)
        raw, scale = raw_ref[...], scale_ref[:, i : i + 1]
        pull = back * gain_ref[i : i + 1, :]
        gain_out_ref[i : i + 1, :] = jnp.sum(back * raw * scale, axis=0, keepdims=True)
        inner.append(jnp.sum(raw * pull, axis=1, keepdims=True))
        out_ref[...] = pull
    both = jnp.concatenate(inner, axis=1)

    @pl.when(pl.program_id(0) == 0)
    def _():
        inner_ref[...] = both

    @pl.when(pl.program_id(0) > 0)
    def _():
        inner_ref[...] += both


def head_specs(rows, head_width, heads):
    def part(p):
        return pl.BlockSpec((rows, head_width), lambda h: (0, h + p * heads))

    def fixed(*shape):
        return pl.BlockSpec(shape, lambda h: (0,) * len(shape))

    gain = pl.BlockSpec((2, head_width), lambda h: (0, h))
    return part, fixed, gain


def mix(qkv, scale, gains, cos, sin, spots, heads):
    rows, head_width = cos.shape
    part, fixed, gain = head_specs(rows, head_width, heads)
    return pl.pallas_call(
        lambda *refs: mix_kernel(head_width**-0.5, *refs),
        grid=(heads,),
        in_specs=[part(0), part(1), part(2), fixed(rows, 2), gain, fixed(rows, head_width)]
        + [fixed(rows, head_width), fixed(rows, 2), fixed(2, rows)],
        out_specs=[part(0)] * 4,
        out_shape=[jax.ShapeDtypeStruct((rows, heads * head_width), bf16)] * 4,
        cost_estimate=QUICK,
        compiler_params=pltpu.CompilerParams(vmem_limit_bytes=40 * 2**20),
    )(qkv, qkv, qkv, scale, gains, cos, sin, spots, spots.T)


def mix_back(qkv, scale, gains, cos, sin, spots, heads, query, key, value, dh, wo):
    rows, head_width = cos.shape
    part, fixed, gain = head_specs(rows, head_width, heads)
    cols = heads * head_width
    return pl.pallas_call(
        lambda *refs: mix_back_kernel(head_width**-0.5, *refs),
        grid=(heads,),
        in_specs=[part(0), part(1), fixed(rows, 2), gain, fixed(rows, head_width)]
        + [fixed(rows, head_width), fixed(rows, 2), fixed(2, rows), part(0), part(0), part(0)]
        + [fixed(*dh.shape), pl.BlockSpec((head_width, wo.shape[1]), lambda h: (h, 0))],
        out_specs=[part(0), part(0), part(0), gain, fixed(rows, 2)],
        out_shape=[jax.ShapeDtypeStruct((rows, cols), f32)] * 2
        + [jax.ShapeDtypeStruct((rows, cols), bf16), jax.ShapeDtypeStruct((2, cols), f32)]
        + [jax.ShapeDtypeStruct((rows, 2), f32)],
        cost_estimate=QUICK,
        compiler_params=pltpu.CompilerParams(vmem_limit_bytes=48 * 2**20),
    )(qkv, qkv, scale, gains, cos, sin, spots, spots.T, query, key, value, dh, wo)


def expert_kernel(per, slot_cap, order_ref, slot_ref, *refs):
    xs, (w_ref, back_ref, gate_ref) = refs[:per], refs[per : per + 3]
    n_ref, act_ref, scaled_ref, gu_ref, dgate_ref, out_ref = refs[-6:]
    ffh = act_ref.shape[1]
    places = lax.broadcasted_iota(jnp.int32, (slot_cap, slot_ref.shape[2]), 0)
    picks = [(slot_ref[j] == places).astype(f32).astype(bf16) for j in range(per)]
    rows = jnp.concatenate([mm(picks[j], xs[j][0]) for j in range(per)]).astype(bf16)
    n_ref[...] = rows
    gate_up = mm(rows, w_ref[...])
    gate_part, up_part = gate_up[:, :ffh], gate_up[:, ffh:]
    sig = jax.nn.sigmoid(gate_part)
    silu = gate_part * sig
    act = (silu * up_part).astype(bf16)
    act_f = act.astype(f32)
    back, gate = back_ref[...], gate_ref[...]
    act_ref[...] = act
    scaled_ref[...] = (act_f * gate).astype(bf16)
    dgate_ref[...] = jnp.sum(act_f * back, axis=1, keepdims=True)
    grad_act = back * gate
    gu_ref[:, :ffh] = (grad_act * up_part * sig * (1.0 + gate_part * (1.0 - sig))).astype(bf16)
    gu_ref[:, ffh:] = (grad_act * silu).astype(bf16)
    grad_rows = mm_nt(gu_ref[...], w_ref[...])
    for j in range(per):
        part = grad_rows[j * slot_cap : (j + 1) * slot_cap].astype(bf16)
        out_ref[j] = mm_tn(picks[j], part).astype(bf16)


def run_expert(rows, order, slots, slot_cap, w_gu, back, gate, side, held=()):
    total, tokens, width = rows.shape
    ffh = back.shape[1]
    per = max(sources_per_block(slot_cap), 8)
    steps = total // 2 // per
    first = side * steps
    block = per * slot_cap

    def block_of(j):
        return pl.BlockSpec(
            (1, tokens, width), lambda i, order_ref: (order_ref[(i + first) * per + j], 0, 0)
        )

    def rows_of(columns):
        return pl.BlockSpec((block, columns), lambda i, order_ref: (i + first, 0))

    def whole(columns, dtype):
        return jax.ShapeDtypeStruct((total * slot_cap, columns), dtype)

    in_specs = [pl.BlockSpec((per, 1, tokens), lambda i, order_ref: (i + first, 0, 0))]
    in_specs += [block_of(j) for j in range(per)]
    in_specs += [pl.BlockSpec(w_gu.shape, lambda i, order_ref: (0, 0)), rows_of(ffh), rows_of(1)]
    aliases = {len(in_specs) + 1 + i: i for i in range(len(held))}
    in_specs += [pl.BlockSpec(memory_space=pl.ANY) for _ in held]
    return pl.pallas_call(
        lambda *refs: expert_kernel(per, slot_cap, *refs),
        grid_spec=pltpu.PrefetchScalarGridSpec(
            num_scalar_prefetch=1,
            grid=(steps,),
            in_specs=in_specs,
            out_specs=[rows_of(width), rows_of(ffh), rows_of(ffh), rows_of(2 * ffh), rows_of(1)]
            + [pl.BlockSpec((per, tokens, width), lambda i, order_ref: (i, 0, 0))],
        ),
        out_shape=[whole(width, bf16), whole(ffh, bf16), whole(ffh, bf16), whole(2 * ffh, bf16)]
        + [whole(1, f32), jax.ShapeDtypeStruct((total // 2, tokens, width), bf16)],
        input_output_aliases=aliases,
        cost_estimate=QUICK,
        compiler_params=pltpu.CompilerParams(vmem_limit_bytes=58 * 2**20),
    )(order, slots.reshape(total, 1, tokens), *([rows] * per), w_gu, back, gate, *held)


def exchange(blocks, *done):
    return lax.all_to_all(after(blocks, *done), "dp", 0, 0, tiled=True)


def split_kernel(experts, halves, w_ref, *out_refs):
    ffh = out_refs[0].shape[2]
    for e in range(experts):
        rows = w_ref[:, e, :].astype(bf16)
        for h in range(halves):
            for j in range(3):
                at = (j * halves + h) * ffh
                out_refs[j][e * halves + h] = rows[:, at : at + ffh]


def split_experts(w, halves):
    rows, experts, width = w.shape
    block, shares, ffh = 64, experts * halves, width // (3 * halves)
    return pl.pallas_call(
        lambda *refs: split_kernel(experts, halves, *refs),
        grid=(rows // block,),
        in_specs=[pl.BlockSpec((block, experts, width), lambda i: (i, 0, 0))],
        out_specs=[pl.BlockSpec((shares, block, ffh), lambda i: (0, i, 0))] * 3,
        out_shape=[jax.ShapeDtypeStruct((shares, rows, ffh), bf16)] * 3,
        cost_estimate=QUICK,
        compiler_params=pltpu.CompilerParams(vmem_limit_bytes=32 * 2**20),
    )(w)


def join_kernel(halves, gate_ref, up_ref, down_ref, out_ref):
    shares, _, ffh = gate_ref.shape
    for t in range(shares):
        e, h = divmod(t, halves)
        for j, ref in enumerate((gate_ref, up_ref, down_ref)):
            at = (j * halves + h) * ffh
            out_ref[:, e, at : at + ffh] = ref[t].astype(f32)


def join_experts(gate, up, down, halves):
    shares, rows, ffh = gate.shape
    block, experts, width = 64, shares // halves, 3 * ffh * halves
    return pl.pallas_call(
        lambda *refs: join_kernel(halves, *refs),
        grid=(rows // block,),
        in_specs=[pl.BlockSpec((shares, block, ffh), lambda i: (0, i, 0))] * 3,
        out_specs=pl.BlockSpec((block, experts, width), lambda i: (i, 0, 0)),
        out_shape=jax.ShapeDtypeStruct((rows, experts, width), f32),
        cost_estimate=QUICK,
        compiler_params=pltpu.CompilerParams(vmem_limit_bytes=32 * 2**20),
    )(gate, up, down)


def near_gather(piece):
    around = [piece]
    for _ in range(lax.axis_size("dp") - 1):
        around.append(shift(around[-1], "dp", 1))
    held = [jnp.stack(around)]
    for bit in bits_of("expert"):
        held = held + [swap(part, "expert", bit) for part in held]
    me_e, me_z = lax.axis_index("expert"), lax.axis_index("dp")
    z_count = len(around)
    whole = jnp.zeros((len(held), z_count) + piece.shape, piece.dtype)
    for r, part in enumerate(held):
        for k in range(z_count):
            at = (me_e ^ r, (me_z - k) % z_count, 0, 0)
            whole = lax.dynamic_update_slice(whole, part[None, k : k + 1], at)
    return whole.reshape(-1, piece.shape[1])


def halved(value):
    for bit in reversed(bits_of("expert")):
        if bit == 1:
            value = value.reshape((value.shape[0] // 2, 2) + value.shape[1:])
            value = half_step(value, "expert", 1, 1)
        else:
            value = value.reshape((2, value.shape[0] // 2) + value.shape[1:])
            value = half_step(value, "expert", bit, 0)
    return value[0].astype(bf16)


def sum_over_dp(blocks, *done):
    arrived = exchange(blocks, *done)
    return jnp.sum(arrived.astype(f32), axis=0), arrived


def on_device(
    tokens, cotangent, w_attn, w_router, norm_gains, w_experts, lengths, block_order, routes
):
    tok_rows, width = tokens.shape[1:]
    blk_rows = tok_rows // 2
    e_count, c_count, z_count = (lax.axis_size(a) for a in EVERY)
    total = e_count * c_count * z_count
    me_e, me_c, me_z = (lax.axis_index(a) for a in EVERY)
    pack_rows = tok_rows * c_count
    pick_rows = routes[0]
    top_count = pick_rows.shape[1]
    local_experts = w_experts.shape[1]
    expert_count = local_experts * e_count * c_count
    slot_cap = tok_rows * top_count * 9 // (8 * expert_count)
    ffn = w_experts.shape[2] // 3
    halves = z_count // local_experts
    ffh = ffn // halves
    head_width = width // HEADS
    local_heads = HEADS // c_count
    cols = local_heads * head_width
    w_rows = w_attn.shape[0]
    score_scale = head_width ** (-0.5)
    block_rows = z_count * w_rows
    aligned = block_rows % head_width == 0
    head_run = block_rows // head_width if aligned else local_heads
    runs = local_heads // head_run
    run_cols = head_run * head_width

    expert_ids = jnp.arange(expert_count, dtype=jnp.int32)
    pick_hits = (pick_rows[:, :, None] == expert_ids[None, None, :]).astype(f32)
    named = jnp.sum(pick_hits, axis=1)
    earlier = jnp.arange(tok_rows)[:, None] > jnp.arange(tok_rows)[None, :]
    ranks = mm(earlier.astype(bf16), named.astype(bf16))
    rank_rows = jnp.repeat(jnp.where(named > 0, ranks, -1.0).T, halves, axis=0)
    own_row = jnp.concatenate(
        [w_router.astype(bf16).reshape(-1), norm_gains.astype(bf16).reshape(-1)]
    )
    small_sent = jnp.concatenate(
        [jnp.broadcast_to(own_row[None], (total, own_row.shape[0])), rank_rows.astype(bf16)], axis=1
    )
    wqkv = (
        w_attn[:, : 3 * width]
        .astype(bf16)
        .reshape(w_rows, 3, runs, c_count, run_cols)
        .transpose(3, 0, 1, 2, 4)
        .reshape(c_count, w_rows, 3 * cols)
    )
    wqkv = lax.all_to_all(wqkv, "context", 0, 0, tiled=True).reshape(c_count * w_rows, 3 * cols)
    small_sent = after(small_sent, wqkv)
    small = lax.all_to_all(small_sent, EVERY, 0, 0, tiled=True)
    n_router = w_router.size
    router_w = small[:, :n_router].reshape(width, expert_count)
    gains = (
        small[:, n_router : n_router + norm_gains.size]
        .reshape(total, 4, norm_gains.shape[1])
        .transpose(1, 0, 2)
        .reshape(4, width)
        .astype(f32)
    )
    slot_of = small[:, n_router + norm_gains.size :].astype(jnp.int32)

    grad_out = cotangent[0]
    gate_blocks, up_blocks, down_blocks = split_experts(w_experts, halves)
    around = ("expert", "dp")
    wo_own = w_attn[:, 3 * width :].astype(bf16)
    g_gather = Gather(grad_out.astype(bf16))
    wqkv = after(wqkv, g_gather.around[1])
    wqkv_all = packed = lax.all_gather(wqkv, around, axis=0, tiled=True)
    if aligned:
        wo_all = near_gather(wo_own)
    else:
        wo_full = lax.all_gather(wo_own, EVERY, axis=0, tiled=True)
        wo_all = lax.dynamic_slice_in_dim(wo_full, me_c * cols, cols, axis=0)
    wqkv_all = (
        wqkv_all.reshape(e_count, z_count, c_count, w_rows, 3 * cols)
        .transpose(0, 2, 1, 3, 4)
        .reshape(width, 3 * cols)
    )

    w_down = exchange(down_blocks, packed)
    w_gate = exchange(gate_blocks, w_down)
    w_up = exchange(up_blocks, w_gate)
    w_gu = jnp.concatenate([w_gate.reshape(width, ffh), w_up.reshape(width, ffh)], axis=1)

    inputs = tokens[0].astype(f32)
    pack_x = context_gather(tokens[0]).astype(f32)
    scale_one = lax.rsqrt(jnp.mean(pack_x * pack_x, axis=-1, keepdims=True) + epsilon)
    normed_one = (pack_x * scale_one * gains[0]).astype(bf16)
    qkv = mm(after(normed_one, gate_blocks, wo_all, g_gather.ring), wqkv_all)
    place, doc, offset = locate(
        jnp.arange(pack_rows, dtype=jnp.int32), lengths[0], block_order[0], blk_rows
    )
    half_width = head_width // 2
    freq = rope_base ** (-2.0 * jnp.arange(half_width, dtype=f32) / head_width)
    angle = offset.astype(f32)[:, None] * freq[None, :]
    cos_t, sin_t = jnp.cos(angle), jnp.sin(angle)
    cos_all = jnp.concatenate([cos_t, cos_t], axis=1)
    sin_all = jnp.concatenate([-sin_t, sin_t], axis=1)
    spots = jnp.stack([doc, place], axis=1)
    my_gains = lax.dynamic_index_in_dim(
        gains[2:].reshape(2, runs, c_count, run_cols), me_c, 2, keepdims=False
    ).reshape(2, cols)
    raw_q, raw_k = qkv[:, :cols], qkv[:, cols : 2 * cols]
    squares = jnp.stack([jnp.sum(raw_q * raw_q, axis=1), jnp.sum(raw_k * raw_k, axis=1)])
    scale_qk = lax.rsqrt(lax.psum(squares, "context") / width + epsilon).T
    query, key, value, mixed = mix(qkv, scale_qk, my_gains, cos_all, sin_all, spots, local_heads)
    hidden = inputs + context_scatter(mm(after(mixed, w_down), wo_all))
    scale_two = lax.rsqrt(jnp.mean(hidden * hidden, axis=-1, keepdims=True) + epsilon)
    normed_two = (hidden * scale_two * gains[1]).astype(bf16)
    logits = mm(normed_two, router_w)
    probs = jax.nn.softmax(logits, axis=-1)

    order = source_order()
    all_normed = lax.all_gather(normed_two, EVERY, axis=0, tiled=True)
    all_normed = all_normed.reshape(total, tok_rows, width)
    gate_rows = lax.all_to_all(jnp.repeat(probs.T, halves, axis=0), EVERY, 0, 0, tiled=True)
    slots = jnp.arange(slot_cap, dtype=jnp.int32)
    slot_of = slot_of[order]
    gate_rows = gate_rows[order]
    gate = jnp.sum(
        jnp.where(slot_of[:, None, :] == slots[None, :, None], gate_rows[:, None, :], 0.0), axis=2
    ).reshape(total * slot_cap, 1)
    side = total // 2
    g_rows = jnp.concatenate(
        [
            take_rows(g_gather.near, g_gather.order(), slot_of[:side], slot_cap),
            take_rows(g_gather.other, g_gather.order(), slot_of[side:], slot_cap),
        ]
    )
    w_down = w_down.reshape(width, ffh)
    back = mm(g_rows, w_down)
    all_normed = after(all_normed, back)
    *held, n2_send = run_expert(all_normed, order, slot_of, slot_cap, w_gu, back, gate, 1)
    n2_sum = Scatter(n2_send, tok_rows)
    *held, n2_keep = run_expert(all_normed, order, slot_of, slot_cap, w_gu, back, gate, 0, held)
    n_rows, act, act_scaled, grad_gu, grad_gate_slot = held
    grad_wd = mm_tn(g_rows, act_scaled).astype(bf16)
    grad_wd, n2_sum.got, n2_keep = tie(grad_wd, n2_sum.got, n2_keep)
    hits = jnp.arange(total)[:, None] == order[None, :]
    grad_gate_slot = grad_gate_slot.reshape(total, 1, slot_cap)
    sent_gates = jnp.sum(
        jnp.where(slot_of[:, :, None] == slots[None, None, :], grad_gate_slot, 0.0), axis=2
    )
    sent_gates = jnp.sum(jnp.where(hits[:, :, None], sent_gates[None], 0.0), axis=1)
    got_gates = lax.all_to_all(sent_gates, EVERY, 0, 0, tiled=True)
    grad_wd, got_gates = tie(grad_wd, got_gates)
    grad_probs = jnp.sum(got_gates.reshape(expert_count, halves, tok_rows), axis=1).T
    down_got = exchange(grad_wd.reshape(z_count, -1, ffh))
    n2_sum.begin(n2_keep)
    n2_sum.step()
    n_late, down_got = tie(n_rows, down_got)
    grad_wg = mm_tn(n_late, grad_gu[:, :ffh]).astype(bf16)
    gate_got = exchange(grad_wg.reshape(z_count, -1, ffh))
    act, n_late = n2_sum.require(act, n_late)
    act, grad_wg = tie(act, grad_wg)
    y_sum = Scatter(expert_output(act, gate, w_down, slot_of, slot_cap, 1), tok_rows)
    y_keep = expert_output(act, gate, w_down, slot_of, slot_cap, 0)
    n_late, y_keep = tie(n_late, y_keep)
    grad_wu = mm_tn(n_late, grad_gu[:, ffh:]).astype(bf16)
    while n2_sum.steps_left():
        n2_sum.step()
    y_sum.begin(y_keep)
    y_sum.step(n2_sum)
    n2_last = n2_sum.cross(gate_got)
    n2_last, grad_wu = y_sum.require(n2_last, grad_wu)
    grad_n2 = jnp.sum(n2_last.astype(f32), axis=0)
    up_got = exchange(grad_wu.reshape(z_count, -1, ffh), n2_last)

    grad_logits = (
        probs * (grad_probs - jnp.sum(probs * grad_probs, axis=-1, keepdims=True))
    ).astype(bf16)
    grad_n2 = grad_n2 + mm_nt(grad_logits, router_w)
    router_term = mm_tn(normed_two, grad_logits)

    def norm_back(v, scale, gain, grad):
        pulled = grad * gain
        inner = jnp.mean(v * pulled, axis=-1, keepdims=True)
        return scale * pulled - v * (scale * scale * scale * inner)

    gain_two = jnp.sum(grad_n2 * hidden * scale_two, axis=0)
    grad_hidden = grad_out + norm_back(hidden, scale_two, gains[1], grad_n2)
    grad_hidden_b = grad_hidden.astype(bf16)

    pack_dh = context_gather(grad_hidden_b)
    while y_sum.steps_left():
        y_sum.step()
    pull_q, pull_k, grad_v, gain_qk, inner = mix_back(
        qkv, scale_qk, my_gains, cos_all, sin_all, spots, local_heads, query, key, value, pack_dh, wo_all
    )
    def weight_blocks(left, right):
        return mm_tn(left, right).reshape(e_count, c_count, z_count, w_rows, right.shape[1])

    grad_wo = mm_tn(mixed, pack_dh)
    if aligned:
        wo_send = halved(grad_wo.reshape(e_count, z_count, w_rows, width))
    v_send = halved(weight_blocks(normed_one, grad_v)).transpose(1, 0, 2, 3)
    (inner,) = y_sum.require(inner)
    inner = lax.psum(inner.T, "context").T / width
    grad_qkv = jnp.concatenate(
        [
            scale_qk[:, 0:1] * pull_q - raw_q * (scale_qk[:, 0:1] ** 3 * inner[:, 0:1]),
            scale_qk[:, 1:2] * pull_k - raw_k * (scale_qk[:, 1:2] ** 3 * inner[:, 1:2]),
        ],
        axis=1,
    ).astype(bf16)
    grad_qkv = jnp.concatenate([grad_qkv, grad_v], axis=1)
    grad_experts = join_experts(gate_got, up_got, down_got, halves)
    qk_blocks = weight_blocks(normed_one, grad_qkv[:, : 2 * cols])
    grad_qkv, qk_blocks = tie(grad_qkv, qk_blocks)
    if aligned:
        grad_qkv, wo_send = tie(grad_qkv, wo_send)
    grad_qkv, v_send = tie(grad_qkv, v_send)
    y_last = y_sum.cross(up_got)
    output = hidden + jnp.sum(y_last.astype(f32), axis=0)
    grad_n1 = context_scatter(mm_nt(grad_qkv, wqkv_all))
    own_scale = lax.rsqrt(jnp.mean(inputs * inputs, axis=-1, keepdims=True) + epsilon)
    gain_one = jnp.sum(grad_n1 * inputs * own_scale, axis=0)
    grad_tokens = grad_hidden + norm_back(inputs, own_scale, gains[0], grad_n1)


    if aligned:
        grad_wo, last = sum_over_dp(wo_send, y_last)
    else:
        whole_wo = lax.dynamic_update_slice_in_dim(
            jnp.zeros((width, width), f32), grad_wo, me_c * cols, axis=0
        )
        grad_wo = lax.psum_scatter(
            whole_wo.astype(bf16), EVERY, scatter_dimension=0, tiled=True
        ).astype(f32)
        last = y_last
    grad_v_sum, last = sum_over_dp(v_send, last)
    grad_qk_sum, _ = sum_over_dp(halved(qk_blocks).transpose(1, 0, 2, 3), last)
    grad_wqkv = jnp.concatenate([grad_qk_sum, grad_v_sum], axis=2).astype(bf16)
    grad_wqkv = (
        lax.all_to_all(grad_wqkv, "context", 0, 0, tiled=True)
        .reshape(c_count, w_rows, 3, runs, run_cols)
        .transpose(1, 2, 3, 0, 4)
        .reshape(w_rows, 3 * width)
        .astype(f32)
    )
    grad_attn = jnp.concatenate([grad_wqkv, grad_wo], axis=1)

    mine = jnp.arange(c_count)[None, None, :, None] == me_c
    gain_qk = jnp.where(mine, gain_qk.reshape(2, runs, 1, run_cols), 0.0)
    gain_rows = jnp.concatenate([jnp.stack([gain_one, gain_two]), gain_qk.reshape(2, width)])
    gain_rows = gain_rows.reshape(4, total, -1).transpose(1, 0, 2).reshape(total, -1)
    small_grads = jnp.concatenate([router_term.reshape(total, -1), gain_rows], axis=1)
    small_grads = jnp.sum(lax.all_to_all(small_grads, EVERY, 0, 0, tiled=True), axis=0)
    grad_router = small_grads[:n_router].reshape(w_router.shape)
    grad_gains = small_grads[n_router:].reshape(norm_gains.shape)
    return (output[None], grad_tokens[None], grad_attn, grad_router, grad_gains, grad_experts)


def solution(mesh):
    in_specs = (
        P(("expert", "dp"), "context", None),
        P(("expert", "dp"), "context", None),
        P(EVERY, None),
        P(EVERY, None),
        P(None, EVERY),
        P("dp", ("expert", "context"), None),
        P(("expert", "dp"), None),
        P(("expert", "dp"), None),
        P(("expert", "dp"), "context", None),
    )
    out_specs = (
        P(("expert", "dp"), "context", None),
        P(("expert", "dp"), "context", None),
        P(EVERY, None),
        P(EVERY, None),
        P(None, EVERY),
        P("dp", ("expert", "context"), None),
    )
    return jax.shard_map(
        on_device, mesh=mesh, in_specs=in_specs, out_specs=out_specs, check_vma=False
    )
```

```python
import jax
import jax.numpy as jnp
from jax import lax
from jax.experimental import pallas as pl
from jax.experimental.pallas import tpu as pltpu
from jax.sharding import PartitionSpec as P

HEADS = 16
epsilon = 1e-05
rope_base = 10000.0
masked_score = -1e30
bf16 = jnp.bfloat16
f32 = jnp.float32
EVERY = ("expert", "context", "dp")
QUICK = pl.CostEstimate(flops=1, bytes_accessed=1, transcendentals=0)


def mm(a, b):
    return jnp.dot(a, b, preferred_element_type=f32)


def mm_nt(a, b):
    return lax.dot_general(a, b, (((1,), (1,)), ((), ())), preferred_element_type=f32)


def mm_tn(a, b):
    return lax.dot_general(a, b, (((0,), (0,)), ((), ())), preferred_element_type=f32)


def swap(value, axis, bit):
    count = lax.axis_size(axis)
    return lax.ppermute(value, axis, [(i, i ^ bit) for i in range(count)])


def shift(value, axis, step):
    count = lax.axis_size(axis)
    return lax.ppermute(value, axis, [(i, (i + step) % count) for i in range(count)])


def bits_of(axis):
    count = lax.axis_size(axis)
    return [1 << i for i in range(count.bit_length() - 1)]


def locate(stored_rows, doc_lens, blk_order, blk_rows):
    block_ids = stored_rows // blk_rows
    block_hits = block_ids[:, None] == jnp.arange(blk_order.shape[0], dtype=jnp.int32)[None, :]
    placed_at = (
        jnp.sum(jnp.where(block_hits, blk_order[None, :], 0), axis=1) * blk_rows
        + stored_rows % blk_rows
    )
    doc_count = doc_lens.shape[0]
    upto = jnp.arange(doc_count)[:, None] >= jnp.arange(doc_count)[None, :]
    doc_ends = jnp.sum(jnp.where(upto, doc_lens[None, :], 0), axis=1)
    doc_ids = jnp.sum((placed_at[:, None] >= doc_ends[None, :]).astype(jnp.int32), axis=1)
    doc_hits = doc_ids[:, None] == jnp.arange(doc_count, dtype=jnp.int32)[None, :]
    doc_starts = doc_ends - doc_lens
    offset = placed_at - jnp.sum(jnp.where(doc_hits, doc_starts[None, :], 0), axis=1)
    return placed_at, doc_ids, offset


def context_gather(value):
    me = lax.axis_index("context")
    parts = [value]
    for bit in reversed(bits_of("context")):
        parts = parts + [swap(part, "context", bit) for part in parts]
    count = len(parts)
    order = []
    for r in range(count):
        source = 0
        for i, bit in enumerate(reversed(bits_of("context"))):
            if r >> i & 1:
                source |= bit
        order.append(source)
    stack = [None] * count
    for r in range(count):
        stack[order[r]] = parts[r]
    rows = []
    for target in range(count):
        rows.append(
            sum(
                jnp.where(me == target ^ m, stack[m], jnp.zeros_like(stack[m])) for m in range(count)
            )
        )
    return jnp.concatenate(rows, axis=0)


def half_step(value, axis, bit, dim):
    mine = (lax.axis_index(axis) // bit) % 2
    keep = lax.dynamic_index_in_dim(value, mine, dim, keepdims=False)
    send = lax.dynamic_index_in_dim(value, 1 - mine, dim, keepdims=False).astype(bf16)
    return keep.astype(f32) + swap(send, axis, bit).astype(f32)


def context_scatter(value):
    bits = bits_of("context")
    rows = value.shape[0] >> len(bits)
    value = value.reshape((2,) * len(bits) + (rows, value.shape[1]))
    left = list(reversed(bits))
    for bit in bits:
        dim = left.index(bit)
        value = half_step(value, "context", bit, dim)
        left.remove(bit)
    return value


def after(value, *done):
    return lax.optimization_barrier((value,) + done)[0] if done else value


def tie(*values):
    return lax.optimization_barrier(values)


def near_step():
    return ("context", bits_of("context")[0])


def far_steps():
    steps = [("context", b) for b in bits_of("context")[1:]]
    return steps + [("expert", b) for b in bits_of("expert")]


def source_order():
    steps = [near_step()] + far_steps()
    me = {axis: lax.axis_index(axis) for axis in EVERY}
    c_count, z_count = lax.axis_size("context"), lax.axis_size("dp")
    order = []
    for i in range(1 << len(steps)):
        masks = {"expert": 0, "context": 0}
        for j, (axis, bit) in enumerate(steps):
            if i >> (len(steps) - 1 - j) & 1:
                masks[axis] |= bit
        column = (me["expert"] ^ masks["expert"]) * c_count + (me["context"] ^ masks["context"])
        order += [column * z_count + z for z in range(z_count)]
    return jnp.stack(order).astype(jnp.int32)


class Gather:
    def __init__(self, value):
        around = [value]
        for _ in range(lax.axis_size("dp") - 1):
            around.append(shift(around[-1], "dp", 1))
        self.ring, self.around = around[-1], around
        far = far_steps()
        half = value.shape[1] // 2
        shape = (-1, value.shape[0], half)
        self.near = []
        for i in range(2):
            held = jnp.stack([part[:, i * half : (i + 1) * half] for part in around])
            held = held.reshape((1,) * len(far) + held.shape)
            for step in far[::-1] if i else far:
                held = jnp.concatenate([held, swap(held, *step)], axis=far.index(step))
            self.near.append(held.reshape(shape))

    def others(self, *done):
        return [swap(after(held, *done), *near_step()) for held in self.near]

    def order(self):
        z_count = lax.axis_size("dp")
        spots = jnp.arange(self.near[0].shape[0], dtype=jnp.int32)
        return spots // z_count * z_count + (lax.axis_index("dp") - spots) % z_count


class Scatter:
    def __init__(self, send, rows):
        self.far = far_steps()
        self.shape = (2,) * len(self.far) + (lax.axis_size("dp"), rows)
        self.got = swap(send, *near_step())

    def begin(self, keep, *done):
        far, width = self.far, keep.shape[-1]
        half = width // 2
        keep = keep.reshape(self.shape + (width,))
        got = after(self.got, *done).reshape(self.shape + (width,))
        self.states = []
        for i in range(2):
            cut = slice(i * half, (i + 1) * half)
            self.states.append((keep[..., cut], got[..., cut], far[::-1] if i else far, list(far)))

    def step(self, other=None):
        sums = []
        for own, got, order, left in self.states:
            step = order[len(order) - len(left)]
            dim = left.index(step)
            first = [slice(None)] * dim + [0]
            second = [slice(None)] * dim + [1]
            sent = own[tuple(second)].astype(f32) + got[tuple(second)].astype(f32)
            kept = own[tuple(first)].astype(f32) + got[tuple(first)].astype(f32)
            sums.append([kept.astype(bf16), sent.astype(bf16), step, order, left[:dim] + left[dim + 1 :]])
        if other:
            sent = other.require(*[entry[1] for entry in sums])
            for entry, new in zip(sums, sent):
                entry[1] = new
        self.states = [
            (kept, swap(sent, *step), order, left) for kept, sent, step, order, left in sums
        ]

    def require(self, *values):
        count = len(self.states)
        *got, = tie(*[state[1] for state in self.states], *values)
        self.states = [
            state[:1] + (new,) + state[2:] for state, new in zip(self.states, got[:count])
        ]
        return got[count:]

    def kept(self):
        return [state[0] for state in self.states]

    def keep(self, kept):
        self.states = [(own,) + state[1:] for own, state in zip(kept, self.states)]

    def steps_left(self):
        return len(self.states[0][3])

    def cross(self, *done):
        blocks = jnp.concatenate(
            [
                (own.astype(f32) + got.astype(f32)).astype(bf16)
                for own, got, _, _ in self.states
            ],
            axis=-1,
        )
        return exchange(blocks, *done)


def sources_per_block(slot_cap):
    count = 1
    while count * slot_cap % 16:
        count *= 2
    return count


def take_kernel(per, slot_cap, order_ref, slot_ref, *refs):
    *rows, out_ref = refs
    places = lax.broadcasted_iota(jnp.int32, (slot_cap, slot_ref.shape[2]), 0)
    picks = [(slot_ref[j] == places).astype(f32).astype(bf16) for j in range(per)]
    at = 0
    for p in range(0, len(rows), per):
        part = [jnp.dot(picks[j], rows[p + j][0], preferred_element_type=f32) for j in range(per)]
        width = part[0].shape[1]
        out_ref[:, at : at + width] = jnp.concatenate(part).astype(bf16)
        at += width


def take_rows(parts, order, slots, slot_cap):
    count = order.shape[0]
    tokens = slots.shape[1]
    per = sources_per_block(slot_cap)
    width = sum(part.shape[2] for part in parts)

    def block_of(part, j):
        return pl.BlockSpec(
            (1, tokens, part.shape[2]), lambda i, order_ref: (order_ref[i * per + j], 0, 0)
        )

    return pl.pallas_call(
        lambda *refs: take_kernel(per, slot_cap, *refs),
        grid_spec=pltpu.PrefetchScalarGridSpec(
            num_scalar_prefetch=1,
            grid=(count // per,),
            in_specs=[pl.BlockSpec((per, 1, tokens), lambda i, order_ref: (i, 0, 0))]
            + [block_of(part, j) for part in parts for j in range(per)],
            out_specs=pl.BlockSpec((per * slot_cap, width), lambda i, order_ref: (i, 0)),
        ),
        out_shape=jax.ShapeDtypeStruct((count * slot_cap, width), bf16),
        cost_estimate=QUICK,
        compiler_params=pltpu.CompilerParams(vmem_limit_bytes=40 * 2**20),
    )(order, slots.reshape(count, 1, tokens), *[part for part in parts for _ in range(per)])


def output_kernel(per, slot_cap, slot_ref, act_ref, gate_ref, w_ref, out_ref):
    places = lax.broadcasted_iota(jnp.int32, (slot_cap, slot_ref.shape[2]), 0)
    rows = mm_nt(act_ref[...], w_ref[...]) * gate_ref[...]
    for j in range(per):
        pick = (slot_ref[j] == places).astype(f32).astype(bf16)
        part = rows[j * slot_cap : (j + 1) * slot_cap].astype(bf16)
        out_ref[j] = mm_tn(pick, part).astype(bf16)


def expert_output(act, gate, w_down, slots, slot_cap, side):
    total, tokens = slots.shape
    width, ffh = w_down.shape
    per = max(sources_per_block(slot_cap), 8)
    steps = total // 2 // per
    first = side * steps

    def rows_of(columns):
        return pl.BlockSpec((per * slot_cap, columns), lambda i: (i + first, 0))

    return pl.pallas_call(
        lambda *refs: output_kernel(per, slot_cap, *refs),
        grid=(steps,),
        in_specs=[
            pl.BlockSpec((per, 1, tokens), lambda i: (i + first, 0, 0)),
            rows_of(ffh),
            rows_of(1),
            pl.BlockSpec((width, ffh), lambda i: (0, 0)),
        ],
        out_specs=pl.BlockSpec((per, tokens, width), lambda i: (i, 0, 0)),
        out_shape=jax.ShapeDtypeStruct((total // 2, tokens, width), bf16),
        cost_estimate=pl.CostEstimate(
            flops=total * slot_cap * width * (ffh + tokens),
            bytes_accessed=total * tokens * width,
            transcendentals=0,
        ),
        compiler_params=pltpu.CompilerParams(vmem_limit_bytes=48 * 2**20),
    )(slots.reshape(total, 1, tokens), act, gate, w_down)


def turn(v, cos, sin):
    return v * cos + pltpu.roll(v, v.shape[1] // 2, 1) * sin


def turn_back(v, cos, sin):
    return v * cos + pltpu.roll(v * sin, v.shape[1] // 2, 1)


def soften(query, key, score_scale, spot_ref, spot_t_ref):
    scores = mm_nt(query, key) * score_scale
    same = spot_ref[:, 0:1] == spot_t_ref[0:1, :]
    allowed = same & (spot_t_ref[1:2, :] <= spot_ref[:, 1:2])
    scores = jnp.where(allowed, scores, masked_score)
    raised = jnp.exp(scores - jnp.max(scores, axis=1, keepdims=True))
    return raised / jnp.sum(raised, axis=1, keepdims=True)


def mix_kernel(score_scale, q_ref, k_ref, v_ref, scale_ref, gain_ref, cos_ref, sin_ref, *refs):
    spot_ref, spot_t_ref, query_ref, key_ref, value_ref, mixed_ref = refs
    cos, sin = cos_ref[...], sin_ref[...]
    query = turn(q_ref[...] * scale_ref[:, 0:1] * gain_ref[0:1, :], cos, sin).astype(bf16)
    key = turn(k_ref[...] * scale_ref[:, 1:2] * gain_ref[1:2, :], cos, sin).astype(bf16)
    value = v_ref[...].astype(bf16)
    soft = soften(query, key, score_scale, spot_ref, spot_t_ref)
    query_ref[...], key_ref[...], value_ref[...] = query, key, value
    mixed_ref[...] = mm(soft.astype(bf16), value).astype(bf16)


def mix_back_kernel(score_scale, q_ref, k_ref, scale_ref, gain_ref, cos_ref, sin_ref, *refs):
    spot_ref, spot_t_ref, query_ref, key_ref, value_ref, dh_ref, wo_ref = refs[:7]
    pull_q_ref, pull_k_ref, grad_v_ref, gain_out_ref, inner_ref = refs[7:]
    cos, sin = cos_ref[...], sin_ref[...]
    query, key, value = query_ref[...], key_ref[...], value_ref[...]
    grad_mixed = mm_nt(dh_ref[...], wo_ref[...]).astype(bf16)
    soft = soften(query, key, score_scale, spot_ref, spot_t_ref)
    grad_soft = mm_nt(grad_mixed, value)
    delta = jnp.sum(soft * grad_soft, axis=1, keepdims=True)
    grad_scores = (soft * (grad_soft - delta)).astype(bf16)
    grad_v_ref[...] = mm_tn(soft.astype(bf16), grad_mixed).astype(bf16)
    inner = []
    for i, (grad, raw_ref, out_ref) in enumerate(
        (
            (mm(grad_scores, key), q_ref, pull_q_ref),
            (mm_tn(grad_scores, query), k_ref, pull_k_ref),
        )
    ):
        back = turn_back(grad * score_scale, cos, sin)
        raw, scale = raw_ref[...], scale_ref[:, i : i + 1]
        pull = back * gain_ref[i : i + 1, :]
        gain_out_ref[i : i + 1, :] = jnp.sum(back * raw * scale, axis=0, keepdims=True)
        inner.append(jnp.sum(raw * pull, axis=1, keepdims=True))
        out_ref[...] = pull
    both = jnp.concatenate(inner, axis=1)

    @pl.when(pl.program_id(0) == 0)
    def _():
        inner_ref[...] = both

    @pl.when(pl.program_id(0) > 0)
    def _():
        inner_ref[...] += both


def head_specs(rows, head_width, heads):
    def part(p):
        return pl.BlockSpec((rows, head_width), lambda h: (0, h + p * heads))

    def fixed(*shape):
        return pl.BlockSpec(shape, lambda h: (0,) * len(shape))

    gain = pl.BlockSpec((2, head_width), lambda h: (0, h))
    return part, fixed, gain


def mix(qkv, scale, gains, cos, sin, spots, heads):
    rows, head_width = cos.shape
    part, fixed, gain = head_specs(rows, head_width, heads)
    return pl.pallas_call(
        lambda *refs: mix_kernel(head_width**-0.5, *refs),
        grid=(heads,),
        in_specs=[part(0), part(1), part(2), fixed(rows, 2), gain, fixed(rows, head_width)]
        + [fixed(rows, head_width), fixed(rows, 2), fixed(2, rows)],
        out_specs=[part(0)] * 4,
        out_shape=[jax.ShapeDtypeStruct((rows, heads * head_width), bf16)] * 4,
        cost_estimate=QUICK,
        compiler_params=pltpu.CompilerParams(vmem_limit_bytes=40 * 2**20),
    )(qkv, qkv, qkv, scale, gains, cos, sin, spots, spots.T)


def mix_back(qkv, scale, gains, cos, sin, spots, heads, query, key, value, dh, wo):
    rows, head_width = cos.shape
    part, fixed, gain = head_specs(rows, head_width, heads)
    cols = heads * head_width
    return pl.pallas_call(
        lambda *refs: mix_back_kernel(head_width**-0.5, *refs),
        grid=(heads,),
        in_specs=[part(0), part(1), fixed(rows, 2), gain, fixed(rows, head_width)]
        + [fixed(rows, head_width), fixed(rows, 2), fixed(2, rows), part(0), part(0), part(0)]
        + [fixed(*dh.shape), pl.BlockSpec((head_width, wo.shape[1]), lambda h: (h, 0))],
        out_specs=[part(0), part(0), part(0), gain, fixed(rows, 2)],
        out_shape=[jax.ShapeDtypeStruct((rows, cols), f32)] * 2
        + [jax.ShapeDtypeStruct((rows, cols), bf16), jax.ShapeDtypeStruct((2, cols), f32)]
        + [jax.ShapeDtypeStruct((rows, 2), f32)],
        cost_estimate=QUICK,
        compiler_params=pltpu.CompilerParams(vmem_limit_bytes=48 * 2**20),
    )(qkv, qkv, scale, gains, cos, sin, spots, spots.T, query, key, value, dh, wo)


def expert_kernel(per, slot_cap, order_ref, slot_ref, *refs):
    xs, (wg_ref, wu_ref, back_ref, gate_ref) = refs[:per], refs[per : per + 4]
    n_ref, act_ref, scaled_ref, gu_ref, dgate_ref, out_ref = refs[-6:]
    ffh = act_ref.shape[1]
    places = lax.broadcasted_iota(jnp.int32, (slot_cap, slot_ref.shape[2]), 0)
    picks = [(slot_ref[j] == places).astype(f32).astype(bf16) for j in range(per)]
    rows = jnp.concatenate([mm(picks[j], xs[j][0]) for j in range(per)]).astype(bf16)
    n_ref[...] = rows
    gate_part, up_part = mm(rows, wg_ref[...]), mm(rows, wu_ref[...])
    sig = jax.nn.sigmoid(gate_part)
    silu = gate_part * sig
    act = (silu * up_part).astype(bf16)
    act_f = act.astype(f32)
    back, gate = back_ref[...], gate_ref[...]
    act_ref[...] = act
    scaled_ref[...] = (act_f * gate).astype(bf16)
    dgate_ref[...] = jnp.sum(act_f * back, axis=1, keepdims=True)
    grad_act = back * gate
    grad_gate = (grad_act * up_part * sig * (1.0 + gate_part * (1.0 - sig))).astype(bf16)
    grad_up = (grad_act * silu).astype(bf16)
    gu_ref[:, :ffh] = grad_gate
    gu_ref[:, ffh:] = grad_up
    grad_rows = mm_nt(grad_gate, wg_ref[...]) + mm_nt(grad_up, wu_ref[...])
    for j in range(per):
        part = grad_rows[j * slot_cap : (j + 1) * slot_cap].astype(bf16)
        out_ref[j] = mm_tn(picks[j], part).astype(bf16)


def run_expert(rows, order, slots, slot_cap, w_gate, w_up, back, gate, side, held=()):
    total, tokens, width = rows.shape
    ffh = back.shape[1]
    per = max(sources_per_block(slot_cap), 8)
    steps = total // 2 // per
    first = side * steps
    block = per * slot_cap

    def block_of(j):
        return pl.BlockSpec(
            (1, tokens, width), lambda i, order_ref: (order_ref[(i + first) * per + j], 0, 0)
        )

    def rows_of(columns):
        return pl.BlockSpec((block, columns), lambda i, order_ref: (i + first, 0))

    def whole(columns, dtype):
        return jax.ShapeDtypeStruct((total * slot_cap, columns), dtype)

    in_specs = [pl.BlockSpec((per, 1, tokens), lambda i, order_ref: (i + first, 0, 0))]
    in_specs += [block_of(j) for j in range(per)]
    in_specs += [pl.BlockSpec(w_gate.shape, lambda i, order_ref: (0, 0))] * 2
    in_specs += [rows_of(ffh), rows_of(1)]
    aliases = {len(in_specs) + 1 + i: i for i in range(len(held))}
    in_specs += [pl.BlockSpec(memory_space=pl.ANY) for _ in held]
    return pl.pallas_call(
        lambda *refs: expert_kernel(per, slot_cap, *refs),
        grid_spec=pltpu.PrefetchScalarGridSpec(
            num_scalar_prefetch=1,
            grid=(steps,),
            in_specs=in_specs,
            out_specs=[rows_of(width), rows_of(ffh), rows_of(ffh), rows_of(2 * ffh), rows_of(1)]
            + [pl.BlockSpec((per, tokens, width), lambda i, order_ref: (i, 0, 0))],
        ),
        out_shape=[whole(width, bf16), whole(ffh, bf16), whole(ffh, bf16), whole(2 * ffh, bf16)]
        + [whole(1, f32), jax.ShapeDtypeStruct((total // 2, tokens, width), bf16)],
        input_output_aliases=aliases,
        cost_estimate=QUICK,
        compiler_params=pltpu.CompilerParams(vmem_limit_bytes=58 * 2**20),
    )(order, slots.reshape(total, 1, tokens), *([rows] * per), w_gate, w_up, back, gate, *held)


def exchange(blocks, *done):
    return lax.all_to_all(after(blocks, *done), "dp", 0, 0, tiled=True)


def split_kernel(experts, halves, w_ref, *out_refs):
    ffh = out_refs[0].shape[2]
    for e in range(experts):
        rows = w_ref[:, e, :].astype(bf16)
        for h in range(halves):
            for j in range(3):
                at = (j * halves + h) * ffh
                out_refs[j][e * halves + h] = rows[:, at : at + ffh]


def split_experts(w, halves):
    rows, experts, width = w.shape
    block, shares, ffh = 64, experts * halves, width // (3 * halves)
    return pl.pallas_call(
        lambda *refs: split_kernel(experts, halves, *refs),
        grid=(rows // block,),
        in_specs=[pl.BlockSpec((block, experts, width), lambda i: (i, 0, 0))],
        out_specs=[pl.BlockSpec((shares, block, ffh), lambda i: (0, i, 0))] * 3,
        out_shape=[jax.ShapeDtypeStruct((shares, rows, ffh), bf16)] * 3,
        cost_estimate=QUICK,
        compiler_params=pltpu.CompilerParams(vmem_limit_bytes=32 * 2**20),
    )(w)


def join_kernel(halves, gate_ref, up_ref, down_ref, out_ref):
    shares, _, ffh = gate_ref.shape
    for t in range(shares):
        e, h = divmod(t, halves)
        for j, ref in enumerate((gate_ref, up_ref, down_ref)):
            at = (j * halves + h) * ffh
            out_ref[:, e, at : at + ffh] = ref[t].astype(f32)


def join_experts(gate, up, down, halves):
    shares, rows, ffh = gate.shape
    block, experts, width = 64, shares // halves, 3 * ffh * halves
    return pl.pallas_call(
        lambda *refs: join_kernel(halves, *refs),
        grid=(rows // block,),
        in_specs=[pl.BlockSpec((shares, block, ffh), lambda i: (0, i, 0))] * 3,
        out_specs=pl.BlockSpec((block, experts, width), lambda i: (i, 0, 0)),
        out_shape=jax.ShapeDtypeStruct((rows, experts, width), f32),
        cost_estimate=QUICK,
        compiler_params=pltpu.CompilerParams(vmem_limit_bytes=32 * 2**20),
    )(gate, up, down)


def near_gather(piece):
    around = [piece]
    for _ in range(lax.axis_size("dp") - 1):
        around.append(shift(around[-1], "dp", 1))
    held = [jnp.stack(around)]
    for bit in bits_of("expert"):
        held = held + [swap(part, "expert", bit) for part in held]
    me_e, me_z = lax.axis_index("expert"), lax.axis_index("dp")
    z_count = len(around)
    whole = jnp.zeros((len(held), z_count) + piece.shape, piece.dtype)
    for r, part in enumerate(held):
        for k in range(z_count):
            at = (me_e ^ r, (me_z - k) % z_count, 0, 0)
            whole = lax.dynamic_update_slice(whole, part[None, k : k + 1], at)
    return whole.reshape(-1, piece.shape[1])


def halved(value):
    for bit in reversed(bits_of("expert")):
        if bit == 1:
            value = value.reshape((value.shape[0] // 2, 2) + value.shape[1:])
            value = half_step(value, "expert", 1, 1)
        else:
            value = value.reshape((2, value.shape[0] // 2) + value.shape[1:])
            value = half_step(value, "expert", bit, 0)
    return value[0].astype(bf16)


def sum_over_dp(blocks, *done):
    arrived = exchange(blocks, *done)
    return jnp.sum(arrived.astype(f32), axis=0), arrived


def on_device(
    tokens, cotangent, w_attn, w_router, norm_gains, w_experts, lengths, block_order, routes
):
    tok_rows, width = tokens.shape[1:]
    blk_rows = tok_rows // 2
    e_count, c_count, z_count = (lax.axis_size(a) for a in EVERY)
    total = e_count * c_count * z_count
    me_e, me_c, me_z = (lax.axis_index(a) for a in EVERY)
    pack_rows = tok_rows * c_count
    pick_rows = routes[0]
    top_count = pick_rows.shape[1]
    local_experts = w_experts.shape[1]
    expert_count = local_experts * e_count * c_count
    slot_cap = tok_rows * top_count * 9 // (8 * expert_count)
    ffn = w_experts.shape[2] // 3
    halves = z_count // local_experts
    ffh = ffn // halves
    head_width = width // HEADS
    local_heads = HEADS // c_count
    cols = local_heads * head_width
    w_rows = w_attn.shape[0]
    score_scale = head_width ** (-0.5)
    block_rows = z_count * w_rows
    aligned = block_rows % head_width == 0
    head_run = block_rows // head_width if aligned else local_heads
    runs = local_heads // head_run
    run_cols = head_run * head_width

    expert_ids = jnp.arange(expert_count, dtype=jnp.int32)
    pick_hits = (pick_rows[:, :, None] == expert_ids[None, None, :]).astype(f32)
    named = jnp.sum(pick_hits, axis=1)
    earlier = jnp.arange(tok_rows)[:, None] > jnp.arange(tok_rows)[None, :]
    ranks = mm(earlier.astype(bf16), named.astype(bf16))
    rank_rows = jnp.repeat(jnp.where(named > 0, ranks, -1.0).T, halves, axis=0)
    own_row = jnp.concatenate(
        [w_router.astype(bf16).reshape(-1), norm_gains.astype(bf16).reshape(-1)]
    )
    small_sent = jnp.concatenate(
        [jnp.broadcast_to(own_row[None], (total, own_row.shape[0])), rank_rows.astype(bf16)], axis=1
    )
    wqkv = (
        w_attn[:, : 3 * width]
        .astype(bf16)
        .reshape(w_rows, 3, runs, c_count, run_cols)
        .transpose(3, 0, 1, 2, 4)
        .reshape(c_count, w_rows, 3 * cols)
    )
    wqkv = lax.all_to_all(wqkv, "context", 0, 0, tiled=True).reshape(c_count * w_rows, 3 * cols)
    small_sent = after(small_sent, wqkv)
    small = lax.all_to_all(small_sent, EVERY, 0, 0, tiled=True)
    n_router = w_router.size
    router_w = small[:, :n_router].reshape(width, expert_count)
    gains = (
        small[:, n_router : n_router + norm_gains.size]
        .reshape(total, 4, norm_gains.shape[1])
        .transpose(1, 0, 2)
        .reshape(4, width)
        .astype(f32)
    )
    slot_of = small[:, n_router + norm_gains.size :].astype(jnp.int32)

    grad_out = cotangent[0]
    gate_blocks, up_blocks, down_blocks = split_experts(w_experts, halves)
    around = ("expert", "dp")
    wo_own = w_attn[:, 3 * width :].astype(bf16)
    g_gather = Gather(grad_out.astype(bf16))
    wqkv = after(wqkv, g_gather.around[1])
    wqkv_all = packed = lax.all_gather(wqkv, around, axis=0, tiled=True)
    if aligned:
        wo_all = near_gather(wo_own)
    else:
        wo_full = lax.all_gather(wo_own, EVERY, axis=0, tiled=True)
        wo_all = lax.dynamic_slice_in_dim(wo_full, me_c * cols, cols, axis=0)
    wqkv_all = (
        wqkv_all.reshape(e_count, z_count, c_count, w_rows, 3 * cols)
        .transpose(0, 2, 1, 3, 4)
        .reshape(width, 3 * cols)
    )

    w_down = exchange(down_blocks, packed)
    w_gate = exchange(gate_blocks, w_down)
    w_up = exchange(up_blocks, w_gate)
    w_gate_all, w_up_all = w_gate.reshape(width, ffh), w_up.reshape(width, ffh)

    inputs = tokens[0].astype(f32)
    pack_x = context_gather(tokens[0]).astype(f32)
    scale_one = lax.rsqrt(jnp.mean(pack_x * pack_x, axis=-1, keepdims=True) + epsilon)
    normed_one = (pack_x * scale_one * gains[0]).astype(bf16)
    qkv = mm(after(normed_one, gate_blocks, wo_all, g_gather.ring), wqkv_all)
    place, doc, offset = locate(
        jnp.arange(pack_rows, dtype=jnp.int32), lengths[0], block_order[0], blk_rows
    )
    half_width = head_width // 2
    freq = rope_base ** (-2.0 * jnp.arange(half_width, dtype=f32) / head_width)
    angle = offset.astype(f32)[:, None] * freq[None, :]
    cos_t, sin_t = jnp.cos(angle), jnp.sin(angle)
    cos_all = jnp.concatenate([cos_t, cos_t], axis=1)
    sin_all = jnp.concatenate([-sin_t, sin_t], axis=1)
    spots = jnp.stack([doc, place], axis=1)
    my_gains = lax.dynamic_index_in_dim(
        gains[2:].reshape(2, runs, c_count, run_cols), me_c, 2, keepdims=False
    ).reshape(2, cols)
    raw_q, raw_k = qkv[:, :cols], qkv[:, cols : 2 * cols]
    squares = jnp.stack([jnp.sum(raw_q * raw_q, axis=1), jnp.sum(raw_k * raw_k, axis=1)])
    scale_qk = lax.rsqrt(lax.psum(squares, "context") / width + epsilon).T
    query, key, value, mixed = mix(qkv, scale_qk, my_gains, cos_all, sin_all, spots, local_heads)
    hidden = inputs + context_scatter(mm(after(mixed, w_down), wo_all))
    scale_two = lax.rsqrt(jnp.mean(hidden * hidden, axis=-1, keepdims=True) + epsilon)
    normed_two = (hidden * scale_two * gains[1]).astype(bf16)
    logits = mm(normed_two, router_w)
    probs = jax.nn.softmax(logits, axis=-1)

    order = source_order()
    all_normed = lax.all_gather(normed_two, EVERY, axis=0, tiled=True)
    all_normed = all_normed.reshape(total, tok_rows, width)
    gate_rows = lax.all_to_all(jnp.repeat(probs.T, halves, axis=0), EVERY, 0, 0, tiled=True)
    slots = jnp.arange(slot_cap, dtype=jnp.int32)
    slot_of = slot_of[order]
    gate_rows = gate_rows[order]
    gate = jnp.sum(
        jnp.where(slot_of[:, None, :] == slots[None, :, None], gate_rows[:, None, :], 0.0), axis=2
    ).reshape(total * slot_cap, 1)
    side = total // 2
    g_rows = jnp.concatenate(
        [
            take_rows(g_gather.near, g_gather.order(), slot_of[:side], slot_cap),
            take_rows(g_gather.others(w_gate), g_gather.order(), slot_of[side:], slot_cap),
        ]
    )
    w_down = w_down.reshape(width, ffh)
    back = mm(g_rows, w_down)
    all_normed = after(all_normed, back)
    *held, n2_send = run_expert(all_normed, order, slot_of, slot_cap, w_gate_all, w_up_all, back, gate, 1)
    n2_sum = Scatter(n2_send, tok_rows)
    *held, n2_keep = run_expert(all_normed, order, slot_of, slot_cap, w_gate_all, w_up_all, back, gate, 0, held)
    n_rows, act, act_scaled, grad_gu, grad_gate_slot = held
    grad_wd = mm_tn(g_rows, act_scaled).astype(bf16)
    grad_wd, n2_sum.got, n2_keep = tie(grad_wd, n2_sum.got, n2_keep)
    hits = jnp.arange(total)[:, None] == order[None, :]
    grad_gate_slot = grad_gate_slot.reshape(total, 1, slot_cap)
    sent_gates = jnp.sum(
        jnp.where(slot_of[:, :, None] == slots[None, None, :], grad_gate_slot, 0.0), axis=2
    )
    sent_gates = jnp.sum(jnp.where(hits[:, :, None], sent_gates[None], 0.0), axis=1)
    got_gates = lax.all_to_all(sent_gates, EVERY, 0, 0, tiled=True)
    grad_wd, got_gates = tie(grad_wd, got_gates)
    grad_probs = jnp.sum(got_gates.reshape(expert_count, halves, tok_rows), axis=1).T
    down_got = exchange(grad_wd.reshape(z_count, -1, ffh))
    n2_sum.begin(n2_keep)
    n2_sum.step()
    n_late, down_got = tie(n_rows, down_got)
    grad_wg = mm_tn(n_late, grad_gu[:, :ffh]).astype(bf16)
    gate_got = exchange(grad_wg.reshape(z_count, -1, ffh))
    act, n_late = n2_sum.require(act, n_late)
    act, grad_wg = tie(act, grad_wg)
    y_sum = Scatter(expert_output(act, gate, w_down, slot_of, slot_cap, 1), tok_rows)
    y_keep = expert_output(act, gate, w_down, slot_of, slot_cap, 0)
    n_late, y_keep = tie(n_late, y_keep)
    grad_wu = mm_tn(n_late, grad_gu[:, ffh:]).astype(bf16)
    while n2_sum.steps_left():
        n2_sum.step()
    y_sum.begin(y_keep)
    y_sum.step(n2_sum)
    n2_last = n2_sum.cross(gate_got)
    n2_last, grad_wu = y_sum.require(n2_last, grad_wu)
    grad_n2 = jnp.sum(n2_last.astype(f32), axis=0)
    up_got = exchange(grad_wu.reshape(z_count, -1, ffh), n2_last)

    grad_logits = (
        probs * (grad_probs - jnp.sum(probs * grad_probs, axis=-1, keepdims=True))
    ).astype(bf16)
    grad_n2 = grad_n2 + mm_nt(grad_logits, router_w)
    router_term = mm_tn(normed_two, grad_logits)

    def norm_back(v, scale, gain, grad):
        pulled = grad * gain
        inner = jnp.mean(v * pulled, axis=-1, keepdims=True)
        return scale * pulled - v * (scale * scale * scale * inner)

    gain_two = jnp.sum(grad_n2 * hidden * scale_two, axis=0)
    grad_hidden = grad_out + norm_back(hidden, scale_two, gains[1], grad_n2)
    grad_hidden_b = grad_hidden.astype(bf16)

    pack_dh = context_gather(grad_hidden_b)
    while y_sum.steps_left():
        y_sum.step()
    pull_q, pull_k, grad_v, gain_qk, inner = mix_back(
        qkv, scale_qk, my_gains, cos_all, sin_all, spots, local_heads, query, key, value, pack_dh, wo_all
    )
    def weight_blocks(left, right):
        return mm_tn(left, right).reshape(e_count, c_count, z_count, w_rows, right.shape[1])

    grad_wo = mm_tn(mixed, pack_dh)
    if aligned:
        wo_send = halved(grad_wo.reshape(e_count, z_count, w_rows, width))
    v_send = halved(weight_blocks(normed_one, grad_v)).transpose(1, 0, 2, 3)
    (inner,) = y_sum.require(inner)
    inner = lax.psum(inner.T, "context")
    if aligned:
        inner, v_send, wo_send = tie(inner, v_send, wo_send)
    inner = inner.T / width
    grad_qkv = jnp.concatenate(
        [
            scale_qk[:, 0:1] * pull_q - raw_q * (scale_qk[:, 0:1] ** 3 * inner[:, 0:1]),
            scale_qk[:, 1:2] * pull_k - raw_k * (scale_qk[:, 1:2] ** 3 * inner[:, 1:2]),
        ],
        axis=1,
    ).astype(bf16)
    grad_qkv = jnp.concatenate([grad_qkv, grad_v], axis=1)
    grad_experts = join_experts(gate_got, up_got, down_got, halves)
    qk_blocks = weight_blocks(normed_one, grad_qkv[:, : 2 * cols])
    grad_qkv, qk_blocks = tie(grad_qkv, qk_blocks)
    y_last = y_sum.cross(up_got)
    output = hidden + jnp.sum(y_last.astype(f32), axis=0)
    grad_n1 = context_scatter(mm_nt(grad_qkv, wqkv_all))
    own_scale = lax.rsqrt(jnp.mean(inputs * inputs, axis=-1, keepdims=True) + epsilon)
    gain_one = jnp.sum(grad_n1 * inputs * own_scale, axis=0)
    grad_tokens = grad_hidden + norm_back(inputs, own_scale, gains[0], grad_n1)


    if aligned:
        grad_wo, last = sum_over_dp(wo_send, y_last)
    else:
        whole_wo = lax.dynamic_update_slice_in_dim(
            jnp.zeros((width, width), f32), grad_wo, me_c * cols, axis=0
        )
        grad_wo = lax.psum_scatter(
            whole_wo.astype(bf16), EVERY, scatter_dimension=0, tiled=True
        ).astype(f32)
        last = y_last
    grad_v_sum, last = sum_over_dp(v_send, last)
    grad_qk_sum, _ = sum_over_dp(halved(qk_blocks).transpose(1, 0, 2, 3), last)
    grad_wqkv = jnp.concatenate([grad_qk_sum, grad_v_sum], axis=2).astype(bf16)
    grad_wqkv = (
        lax.all_to_all(grad_wqkv, "context", 0, 0, tiled=True)
        .reshape(c_count, w_rows, 3, runs, run_cols)
        .transpose(1, 2, 3, 0, 4)
        .reshape(w_rows, 3 * width)
        .astype(f32)
    )
    grad_attn = jnp.concatenate([grad_wqkv, grad_wo], axis=1)

    mine = jnp.arange(c_count)[None, None, :, None] == me_c
    gain_qk = jnp.where(mine, gain_qk.reshape(2, runs, 1, run_cols), 0.0)
    gain_rows = jnp.concatenate([jnp.stack([gain_one, gain_two]), gain_qk.reshape(2, width)])
    gain_rows = gain_rows.reshape(4, total, -1).transpose(1, 0, 2).reshape(total, -1)
    small_grads = jnp.concatenate([router_term.reshape(total, -1), gain_rows], axis=1)
    small_grads = jnp.sum(lax.all_to_all(small_grads, EVERY, 0, 0, tiled=True), axis=0)
    grad_router = small_grads[:n_router].reshape(w_router.shape)
    grad_gains = small_grads[n_router:].reshape(norm_gains.shape)
    return (output[None], grad_tokens[None], grad_attn, grad_router, grad_gains, grad_experts)


def solution(mesh):
    in_specs = (
        P(("expert", "dp"), "context", None),
        P(("expert", "dp"), "context", None),
        P(EVERY, None),
        P(EVERY, None),
        P(None, EVERY),
        P("dp", ("expert", "context"), None),
        P(("expert", "dp"), None),
        P(("expert", "dp"), None),
        P(("expert", "dp"), "context", None),
    )
    out_specs = (
        P(("expert", "dp"), "context", None),
        P(("expert", "dp"), "context", None),
        P(EVERY, None),
        P(EVERY, None),
        P(None, EVERY),
        P("dp", ("expert", "context"), None),
    )
    return jax.shard_map(
        on_device, mesh=mesh, in_specs=in_specs, out_specs=out_specs, check_vma=False
    )
```

```python
import jax
import jax.numpy as jnp
from jax import lax
from jax.experimental import pallas as pl
from jax.experimental.pallas import tpu as pltpu
from jax.sharding import PartitionSpec as P

HEADS = 16
epsilon = 1e-05
rope_base = 10000.0
masked_score = -1e30
bf16 = jnp.bfloat16
f32 = jnp.float32
EVERY = ("expert", "context", "dp")
QUICK = pl.CostEstimate(flops=1, bytes_accessed=1, transcendentals=0)


def mm(a, b):
    return jnp.dot(a, b, preferred_element_type=f32)


def mm_nt(a, b):
    return lax.dot_general(a, b, (((1,), (1,)), ((), ())), preferred_element_type=f32)


def mm_tn(a, b):
    return lax.dot_general(a, b, (((0,), (0,)), ((), ())), preferred_element_type=f32)


def swap(value, axis, bit):
    count = lax.axis_size(axis)
    return lax.ppermute(value, axis, [(i, i ^ bit) for i in range(count)])


def shift(value, axis, step):
    count = lax.axis_size(axis)
    return lax.ppermute(value, axis, [(i, (i + step) % count) for i in range(count)])


def bits_of(axis):
    count = lax.axis_size(axis)
    return [1 << i for i in range(count.bit_length() - 1)]


def locate(stored_rows, doc_lens, blk_order, blk_rows):
    block_ids = stored_rows // blk_rows
    block_hits = block_ids[:, None] == jnp.arange(blk_order.shape[0], dtype=jnp.int32)[None, :]
    placed_at = (
        jnp.sum(jnp.where(block_hits, blk_order[None, :], 0), axis=1) * blk_rows
        + stored_rows % blk_rows
    )
    doc_count = doc_lens.shape[0]
    upto = jnp.arange(doc_count)[:, None] >= jnp.arange(doc_count)[None, :]
    doc_ends = jnp.sum(jnp.where(upto, doc_lens[None, :], 0), axis=1)
    doc_ids = jnp.sum((placed_at[:, None] >= doc_ends[None, :]).astype(jnp.int32), axis=1)
    doc_hits = doc_ids[:, None] == jnp.arange(doc_count, dtype=jnp.int32)[None, :]
    doc_starts = doc_ends - doc_lens
    offset = placed_at - jnp.sum(jnp.where(doc_hits, doc_starts[None, :], 0), axis=1)
    return placed_at, doc_ids, offset


def context_gather(value):
    me = lax.axis_index("context")
    parts = [value]
    for bit in reversed(bits_of("context")):
        parts = parts + [swap(part, "context", bit) for part in parts]
    count = len(parts)
    order = []
    for r in range(count):
        source = 0
        for i, bit in enumerate(reversed(bits_of("context"))):
            if r >> i & 1:
                source |= bit
        order.append(source)
    stack = [None] * count
    for r in range(count):
        stack[order[r]] = parts[r]
    rows = []
    for target in range(count):
        rows.append(
            sum(
                jnp.where(me == target ^ m, stack[m], jnp.zeros_like(stack[m])) for m in range(count)
            )
        )
    return jnp.concatenate(rows, axis=0)


def context_sum(value):
    return jnp.sum(lax.all_gather(value, "context"), axis=0)


def half_step(value, axis, bit, dim):
    mine = (lax.axis_index(axis) // bit) % 2
    keep = lax.dynamic_index_in_dim(value, mine, dim, keepdims=False)
    send = lax.dynamic_index_in_dim(value, 1 - mine, dim, keepdims=False).astype(bf16)
    return keep.astype(f32) + swap(send, axis, bit).astype(f32)


def context_scatter(value):
    bits = bits_of("context")
    rows = value.shape[0] >> len(bits)
    value = value.reshape((2,) * len(bits) + (rows, value.shape[1]))
    left = list(reversed(bits))
    for bit in bits:
        dim = left.index(bit)
        value = half_step(value, "context", bit, dim)
        left.remove(bit)
    return value


def after(value, *done):
    return lax.optimization_barrier((value,) + done)[0] if done else value


def tie(*values):
    return lax.optimization_barrier(values)


def near_step():
    return ("context", bits_of("context")[0])


def far_steps():
    steps = [("context", b) for b in bits_of("context")[1:]]
    return steps + [("expert", b) for b in bits_of("expert")]


def source_order():
    steps = [near_step()] + far_steps()
    me = {axis: lax.axis_index(axis) for axis in EVERY}
    c_count, z_count = lax.axis_size("context"), lax.axis_size("dp")
    order = []
    for i in range(1 << len(steps)):
        masks = {"expert": 0, "context": 0}
        for j, (axis, bit) in enumerate(steps):
            if i >> (len(steps) - 1 - j) & 1:
                masks[axis] |= bit
        column = (me["expert"] ^ masks["expert"]) * c_count + (me["context"] ^ masks["context"])
        order += [column * z_count + z for z in range(z_count)]
    return jnp.stack(order).astype(jnp.int32)


class Gather:
    def __init__(self, value):
        around = [value]
        for _ in range(lax.axis_size("dp") - 1):
            around.append(shift(around[-1], "dp", 1))
        self.ring, self.around = around[-1], around
        far = far_steps()
        half = value.shape[1] // 2
        shape = (-1, value.shape[0], half)
        self.near = []
        for i in range(2):
            held = jnp.stack([part[:, i * half : (i + 1) * half] for part in around])
            held = held.reshape((1,) * len(far) + held.shape)
            for step in far[::-1] if i else far:
                held = jnp.concatenate([held, swap(held, *step)], axis=far.index(step))
            self.near.append(held.reshape(shape))

    def others(self, *done):
        return [swap(after(held, *done), *near_step()) for held in self.near]

    def order(self):
        z_count = lax.axis_size("dp")
        spots = jnp.arange(self.near[0].shape[0], dtype=jnp.int32)
        return spots // z_count * z_count + (lax.axis_index("dp") - spots) % z_count


class Scatter:
    def __init__(self, send, rows):
        self.far = far_steps()
        self.shape = (2,) * len(self.far) + (lax.axis_size("dp"), rows)
        self.got = swap(send, *near_step())

    def begin(self, keep, *done):
        far, width = self.far, keep.shape[-1]
        half = width // 2
        keep = keep.reshape(self.shape + (width,))
        got = after(self.got, *done).reshape(self.shape + (width,))
        self.states = []
        for i in range(2):
            cut = slice(i * half, (i + 1) * half)
            self.states.append((keep[..., cut], got[..., cut], far[::-1] if i else far, list(far)))

    def step(self, other=None):
        sums = []
        for own, got, order, left in self.states:
            step = order[len(order) - len(left)]
            dim = left.index(step)
            first = [slice(None)] * dim + [0]
            second = [slice(None)] * dim + [1]
            sent = own[tuple(second)].astype(f32) + got[tuple(second)].astype(f32)
            kept = own[tuple(first)].astype(f32) + got[tuple(first)].astype(f32)
            sums.append([kept.astype(bf16), sent.astype(bf16), step, order, left[:dim] + left[dim + 1 :]])
        if other:
            sent = other.require(*[entry[1] for entry in sums])
            for entry, new in zip(sums, sent):
                entry[1] = new
        self.states = [
            (kept, swap(sent, *step), order, left) for kept, sent, step, order, left in sums
        ]

    def require(self, *values):
        count = len(self.states)
        *got, = tie(*[state[1] for state in self.states], *values)
        self.states = [
            state[:1] + (new,) + state[2:] for state, new in zip(self.states, got[:count])
        ]
        return got[count:]

    def kept(self):
        return [state[0] for state in self.states]

    def keep(self, kept):
        self.states = [(own,) + state[1:] for own, state in zip(kept, self.states)]

    def steps_left(self):
        return len(self.states[0][3])

    def cross(self, *done):
        blocks = jnp.concatenate(
            [
                (own.astype(f32) + got.astype(f32)).astype(bf16)
                for own, got, _, _ in self.states
            ],
            axis=-1,
        )
        return exchange(blocks, *done)


def sources_per_block(slot_cap):
    count = 1
    while count * slot_cap % 16:
        count *= 2
    return count


def take_kernel(per, slot_cap, order_ref, slot_ref, *refs):
    *rows, out_ref = refs
    places = lax.broadcasted_iota(jnp.int32, (slot_cap, slot_ref.shape[2]), 0)
    picks = [(slot_ref[j] == places).astype(f32).astype(bf16) for j in range(per)]
    at = 0
    for p in range(0, len(rows), per):
        part = [jnp.dot(picks[j], rows[p + j][0], preferred_element_type=f32) for j in range(per)]
        width = part[0].shape[1]
        out_ref[:, at : at + width] = jnp.concatenate(part).astype(bf16)
        at += width


def take_rows(parts, order, slots, slot_cap):
    count = order.shape[0]
    tokens = slots.shape[1]
    per = sources_per_block(slot_cap)
    width = sum(part.shape[2] for part in parts)

    def block_of(part, j):
        return pl.BlockSpec(
            (1, tokens, part.shape[2]), lambda i, order_ref: (order_ref[i * per + j], 0, 0)
        )

    return pl.pallas_call(
        lambda *refs: take_kernel(per, slot_cap, *refs),
        grid_spec=pltpu.PrefetchScalarGridSpec(
            num_scalar_prefetch=1,
            grid=(count // per,),
            in_specs=[pl.BlockSpec((per, 1, tokens), lambda i, order_ref: (i, 0, 0))]
            + [block_of(part, j) for part in parts for j in range(per)],
            out_specs=pl.BlockSpec((per * slot_cap, width), lambda i, order_ref: (i, 0)),
        ),
        out_shape=jax.ShapeDtypeStruct((count * slot_cap, width), bf16),
        cost_estimate=QUICK,
        compiler_params=pltpu.CompilerParams(vmem_limit_bytes=40 * 2**20),
    )(order, slots.reshape(count, 1, tokens), *[part for part in parts for _ in range(per)])


def output_kernel(per, slot_cap, slot_ref, act_ref, gate_ref, w_ref, out_ref):
    places = lax.broadcasted_iota(jnp.int32, (slot_cap, slot_ref.shape[2]), 0)
    rows = mm_nt(act_ref[...], w_ref[...]) * gate_ref[...]
    for j in range(per):
        pick = (slot_ref[j] == places).astype(f32).astype(bf16)
        part = rows[j * slot_cap : (j + 1) * slot_cap].astype(bf16)
        out_ref[j] = mm_tn(pick, part).astype(bf16)


def expert_output(act, gate, w_down, slots, slot_cap, side):
    total, tokens = slots.shape
    width, ffh = w_down.shape
    per = max(sources_per_block(slot_cap), 8)
    steps = total // 2 // per
    first = side * steps

    def rows_of(columns):
        return pl.BlockSpec((per * slot_cap, columns), lambda i: (i + first, 0))

    return pl.pallas_call(
        lambda *refs: output_kernel(per, slot_cap, *refs),
        grid=(steps,),
        in_specs=[
            pl.BlockSpec((per, 1, tokens), lambda i: (i + first, 0, 0)),
            rows_of(ffh),
            rows_of(1),
            pl.BlockSpec((width, ffh), lambda i: (0, 0)),
        ],
        out_specs=pl.BlockSpec((per, tokens, width), lambda i: (i, 0, 0)),
        out_shape=jax.ShapeDtypeStruct((total // 2, tokens, width), bf16),
        cost_estimate=pl.CostEstimate(
            flops=total * slot_cap * width * (ffh + tokens),
            bytes_accessed=total * tokens * width,
            transcendentals=0,
        ),
        compiler_params=pltpu.CompilerParams(vmem_limit_bytes=48 * 2**20),
    )(slots.reshape(total, 1, tokens), act, gate, w_down)


def turn(v, cos, sin):
    return v * cos + pltpu.roll(v, v.shape[1] // 2, 1) * sin


def turn_back(v, cos, sin):
    return v * cos + pltpu.roll(v * sin, v.shape[1] // 2, 1)


def soften(query, key, score_scale, spot_ref, spot_t_ref):
    scores = mm_nt(query, key) * score_scale
    same = spot_ref[:, 0:1] == spot_t_ref[0:1, :]
    allowed = same & (spot_t_ref[1:2, :] <= spot_ref[:, 1:2])
    scores = jnp.where(allowed, scores, masked_score)
    raised = jnp.exp(scores - jnp.max(scores, axis=1, keepdims=True))
    return raised / jnp.sum(raised, axis=1, keepdims=True)


def mix_kernel(score_scale, q_ref, k_ref, v_ref, scale_ref, gain_ref, cos_ref, sin_ref, *refs):
    spot_ref, spot_t_ref, query_ref, key_ref, value_ref, mixed_ref = refs
    cos, sin = cos_ref[...], sin_ref[...]
    query = turn(q_ref[...] * scale_ref[:, 0:1] * gain_ref[0:1, :], cos, sin).astype(bf16)
    key = turn(k_ref[...] * scale_ref[:, 1:2] * gain_ref[1:2, :], cos, sin).astype(bf16)
    value = v_ref[...].astype(bf16)
    soft = soften(query, key, score_scale, spot_ref, spot_t_ref)
    query_ref[...], key_ref[...], value_ref[...] = query, key, value
    mixed_ref[...] = mm(soft.astype(bf16), value).astype(bf16)


def mix_back_kernel(score_scale, q_ref, k_ref, scale_ref, gain_ref, cos_ref, sin_ref, *refs):
    spot_ref, spot_t_ref, query_ref, key_ref, value_ref, dh_ref, wo_ref = refs[:7]
    pull_q_ref, pull_k_ref, grad_v_ref, gain_out_ref, inner_ref = refs[7:]
    cos, sin = cos_ref[...], sin_ref[...]
    query, key, value = query_ref[...], key_ref[...], value_ref[...]
    grad_mixed = mm_nt(dh_ref[...], wo_ref[...]).astype(bf16)
    soft = soften(query, key, score_scale, spot_ref, spot_t_ref)
    grad_soft = mm_nt(grad_mixed, value)
    delta = jnp.sum(soft * grad_soft, axis=1, keepdims=True)
    grad_scores = (soft * (grad_soft - delta)).astype(bf16)
    grad_v_ref[...] = mm_tn(soft.astype(bf16), grad_mixed).astype(bf16)
    inner = []
    for i, (grad, raw_ref, out_ref) in enumerate(
        (
            (mm(grad_scores, key), q_ref, pull_q_ref),
            (mm_tn(grad_scores, query), k_ref, pull_k_ref),
        )
    ):
        back = turn_back(grad * score_scale, cos, sin)
        raw, scale = raw_ref[...], scale_ref[:, i : i + 1]
        pull = back * gain_ref[i : i + 1, :]
        gain_out_ref[i : i + 1, :] = jnp.sum(back * raw * scale, axis=0, keepdims=True)
        inner.append(jnp.sum(raw * pull, axis=1, keepdims=True))
        out_ref[...] = pull
    both = jnp.concatenate(inner, axis=1)

    @pl.when(pl.program_id(0) == 0)
    def _():
        inner_ref[...] = both

    @pl.when(pl.program_id(0) > 0)
    def _():
        inner_ref[...] += both


def head_specs(rows, head_width, heads):
    def part(p):
        return pl.BlockSpec((rows, head_width), lambda h: (0, h + p * heads))

    def fixed(*shape):
        return pl.BlockSpec(shape, lambda h: (0,) * len(shape))

    gain = pl.BlockSpec((2, head_width), lambda h: (0, h))
    return part, fixed, gain


def mix(qkv, scale, gains, cos, sin, spots, heads):
    rows, head_width = cos.shape
    part, fixed, gain = head_specs(rows, head_width, heads)
    return pl.pallas_call(
        lambda *refs: mix_kernel(head_width**-0.5, *refs),
        grid=(heads,),
        in_specs=[part(0), part(1), part(2), fixed(rows, 2), gain, fixed(rows, head_width)]
        + [fixed(rows, head_width), fixed(rows, 2), fixed(2, rows)],
        out_specs=[part(0)] * 4,
        out_shape=[jax.ShapeDtypeStruct((rows, heads * head_width), bf16)] * 4,
        cost_estimate=QUICK,
        compiler_params=pltpu.CompilerParams(vmem_limit_bytes=40 * 2**20),
    )(qkv, qkv, qkv, scale, gains, cos, sin, spots, spots.T)


def mix_back(qkv, scale, gains, cos, sin, spots, heads, query, key, value, dh, wo):
    rows, head_width = cos.shape
    part, fixed, gain = head_specs(rows, head_width, heads)
    cols = heads * head_width
    return pl.pallas_call(
        lambda *refs: mix_back_kernel(head_width**-0.5, *refs),
        grid=(heads,),
        in_specs=[part(0), part(1), fixed(rows, 2), gain, fixed(rows, head_width)]
        + [fixed(rows, head_width), fixed(rows, 2), fixed(2, rows), part(0), part(0), part(0)]
        + [fixed(*dh.shape), pl.BlockSpec((head_width, wo.shape[1]), lambda h: (h, 0))],
        out_specs=[part(0), part(0), part(0), gain, fixed(rows, 2)],
        out_shape=[jax.ShapeDtypeStruct((rows, cols), f32)] * 2
        + [jax.ShapeDtypeStruct((rows, cols), bf16), jax.ShapeDtypeStruct((2, cols), f32)]
        + [jax.ShapeDtypeStruct((rows, 2), f32)],
        cost_estimate=QUICK,
        compiler_params=pltpu.CompilerParams(vmem_limit_bytes=48 * 2**20),
    )(qkv, qkv, scale, gains, cos, sin, spots, spots.T, query, key, value, dh, wo)


def expert_kernel(per, slot_cap, order_ref, slot_ref, *refs):
    xs, (wg_ref, wu_ref, back_ref, gate_ref) = refs[:per], refs[per : per + 4]
    n_ref, act_ref, scaled_ref, gu_ref, dgate_ref, out_ref = refs[-6:]
    ffh = act_ref.shape[1]
    places = lax.broadcasted_iota(jnp.int32, (slot_cap, slot_ref.shape[2]), 0)
    picks = [(slot_ref[j] == places).astype(f32).astype(bf16) for j in range(per)]
    rows = jnp.concatenate([mm(picks[j], xs[j][0]) for j in range(per)]).astype(bf16)
    n_ref[...] = rows
    gate_part, up_part = mm(rows, wg_ref[...]), mm(rows, wu_ref[...])
    sig = jax.nn.sigmoid(gate_part)
    silu = gate_part * sig
    act = (silu * up_part).astype(bf16)
    act_f = act.astype(f32)
    back, gate = back_ref[...], gate_ref[...]
    act_ref[...] = act
    scaled_ref[...] = (act_f * gate).astype(bf16)
    dgate_ref[...] = jnp.sum(act_f * back, axis=1, keepdims=True)
    grad_act = back * gate
    grad_gate = (grad_act * up_part * sig * (1.0 + gate_part * (1.0 - sig))).astype(bf16)
    grad_up = (grad_act * silu).astype(bf16)
    gu_ref[:, :ffh] = grad_gate
    gu_ref[:, ffh:] = grad_up
    grad_rows = mm_nt(grad_gate, wg_ref[...]) + mm_nt(grad_up, wu_ref[...])
    for j in range(per):
        part = grad_rows[j * slot_cap : (j + 1) * slot_cap].astype(bf16)
        out_ref[j] = mm_tn(picks[j], part).astype(bf16)


def run_expert(rows, order, slots, slot_cap, w_gate, w_up, back, gate, side, held=()):
    total, tokens, width = rows.shape
    ffh = back.shape[1]
    per = max(sources_per_block(slot_cap), 8)
    steps = total // 2 // per
    first = side * steps
    block = per * slot_cap

    def block_of(j):
        return pl.BlockSpec(
            (1, tokens, width), lambda i, order_ref: (order_ref[(i + first) * per + j], 0, 0)
        )

    def rows_of(columns):
        return pl.BlockSpec((block, columns), lambda i, order_ref: (i + first, 0))

    def whole(columns, dtype):
        return jax.ShapeDtypeStruct((total * slot_cap, columns), dtype)

    in_specs = [pl.BlockSpec((per, 1, tokens), lambda i, order_ref: (i + first, 0, 0))]
    in_specs += [block_of(j) for j in range(per)]
    in_specs += [pl.BlockSpec(w_gate.shape, lambda i, order_ref: (0, 0))] * 2
    in_specs += [rows_of(ffh), rows_of(1)]
    aliases = {len(in_specs) + 1 + i: i for i in range(len(held))}
    in_specs += [pl.BlockSpec(memory_space=pl.ANY) for _ in held]
    return pl.pallas_call(
        lambda *refs: expert_kernel(per, slot_cap, *refs),
        grid_spec=pltpu.PrefetchScalarGridSpec(
            num_scalar_prefetch=1,
            grid=(steps,),
            in_specs=in_specs,
            out_specs=[rows_of(width), rows_of(ffh), rows_of(ffh), rows_of(2 * ffh), rows_of(1)]
            + [pl.BlockSpec((per, tokens, width), lambda i, order_ref: (i, 0, 0))],
        ),
        out_shape=[whole(width, bf16), whole(ffh, bf16), whole(ffh, bf16), whole(2 * ffh, bf16)]
        + [whole(1, f32), jax.ShapeDtypeStruct((total // 2, tokens, width), bf16)],
        input_output_aliases=aliases,
        cost_estimate=QUICK,
        compiler_params=pltpu.CompilerParams(vmem_limit_bytes=58 * 2**20),
    )(order, slots.reshape(total, 1, tokens), *([rows] * per), w_gate, w_up, back, gate, *held)


def exchange(blocks, *done):
    return lax.all_to_all(after(blocks, *done), "dp", 0, 0, tiled=True)


def split_kernel(experts, halves, w_ref, *out_refs):
    ffh = out_refs[0].shape[2]
    for e in range(experts):
        rows = w_ref[:, e, :].astype(bf16)
        for h in range(halves):
            for j in range(3):
                at = (j * halves + h) * ffh
                out_refs[j][e * halves + h] = rows[:, at : at + ffh]


def split_experts(w, halves):
    rows, experts, width = w.shape
    block, shares, ffh = 64, experts * halves, width // (3 * halves)
    return pl.pallas_call(
        lambda *refs: split_kernel(experts, halves, *refs),
        grid=(rows // block,),
        in_specs=[pl.BlockSpec((block, experts, width), lambda i: (i, 0, 0))],
        out_specs=[pl.BlockSpec((shares, block, ffh), lambda i: (0, i, 0))] * 3,
        out_shape=[jax.ShapeDtypeStruct((shares, rows, ffh), bf16)] * 3,
        cost_estimate=QUICK,
        compiler_params=pltpu.CompilerParams(vmem_limit_bytes=32 * 2**20),
    )(w)


def join_kernel(halves, gate_ref, up_ref, down_ref, out_ref):
    shares, _, ffh = gate_ref.shape
    for t in range(shares):
        e, h = divmod(t, halves)
        for j, ref in enumerate((gate_ref, up_ref, down_ref)):
            at = (j * halves + h) * ffh
            out_ref[:, e, at : at + ffh] = ref[t].astype(f32)


def join_experts(gate, up, down, halves):
    shares, rows, ffh = gate.shape
    block, experts, width = 64, shares // halves, 3 * ffh * halves
    return pl.pallas_call(
        lambda *refs: join_kernel(halves, *refs),
        grid=(rows // block,),
        in_specs=[pl.BlockSpec((shares, block, ffh), lambda i: (0, i, 0))] * 3,
        out_specs=pl.BlockSpec((block, experts, width), lambda i: (i, 0, 0)),
        out_shape=jax.ShapeDtypeStruct((rows, experts, width), f32),
        cost_estimate=QUICK,
        compiler_params=pltpu.CompilerParams(vmem_limit_bytes=32 * 2**20),
    )(gate, up, down)


def near_gather(piece):
    around = [piece]
    for _ in range(lax.axis_size("dp") - 1):
        around.append(shift(around[-1], "dp", 1))
    held = [jnp.stack(around)]
    for bit in bits_of("expert"):
        held = held + [swap(part, "expert", bit) for part in held]
    me_e, me_z = lax.axis_index("expert"), lax.axis_index("dp")
    z_count = len(around)
    whole = jnp.zeros((len(held), z_count) + piece.shape, piece.dtype)
    for r, part in enumerate(held):
        for k in range(z_count):
            at = (me_e ^ r, (me_z - k) % z_count, 0, 0)
            whole = lax.dynamic_update_slice(whole, part[None, k : k + 1], at)
    return whole.reshape(-1, piece.shape[1])


def halved(value):
    for bit in reversed(bits_of("expert")):
        if bit == 1:
            value = value.reshape((value.shape[0] // 2, 2) + value.shape[1:])
            value = half_step(value, "expert", 1, 1)
        else:
            value = value.reshape((2, value.shape[0] // 2) + value.shape[1:])
            value = half_step(value, "expert", bit, 0)
    return value[0].astype(bf16)


def sum_over_dp(blocks, *done):
    arrived = exchange(blocks, *done)
    return jnp.sum(arrived.astype(f32), axis=0), arrived


def on_device(
    tokens, cotangent, w_attn, w_router, norm_gains, w_experts, lengths, block_order, routes
):
    tok_rows, width = tokens.shape[1:]
    blk_rows = tok_rows // 2
    e_count, c_count, z_count = (lax.axis_size(a) for a in EVERY)
    total = e_count * c_count * z_count
    me_e, me_c, me_z = (lax.axis_index(a) for a in EVERY)
    pack_rows = tok_rows * c_count
    pick_rows = routes[0]
    top_count = pick_rows.shape[1]
    local_experts = w_experts.shape[1]
    expert_count = local_experts * e_count * c_count
    slot_cap = tok_rows * top_count * 9 // (8 * expert_count)
    ffn = w_experts.shape[2] // 3
    halves = z_count // local_experts
    ffh = ffn // halves
    head_width = width // HEADS
    local_heads = HEADS // c_count
    cols = local_heads * head_width
    w_rows = w_attn.shape[0]
    score_scale = head_width ** (-0.5)
    block_rows = z_count * w_rows
    aligned = block_rows % head_width == 0
    head_run = block_rows // head_width if aligned else local_heads
    runs = local_heads // head_run
    run_cols = head_run * head_width

    expert_ids = jnp.arange(expert_count, dtype=jnp.int32)
    pick_hits = (pick_rows[:, :, None] == expert_ids[None, None, :]).astype(f32)
    named = jnp.sum(pick_hits, axis=1)
    earlier = jnp.arange(tok_rows)[:, None] > jnp.arange(tok_rows)[None, :]
    ranks = mm(earlier.astype(bf16), named.astype(bf16))
    rank_rows = jnp.repeat(jnp.where(named > 0, ranks, -1.0).T, halves, axis=0)
    own_row = jnp.concatenate(
        [w_router.astype(bf16).reshape(-1), norm_gains.astype(bf16).reshape(-1)]
    )
    small_sent = jnp.concatenate(
        [jnp.broadcast_to(own_row[None], (total, own_row.shape[0])), rank_rows.astype(bf16)], axis=1
    )
    wqkv = (
        w_attn[:, : 3 * width]
        .astype(bf16)
        .reshape(w_rows, 3, runs, c_count, run_cols)
        .transpose(3, 0, 1, 2, 4)
        .reshape(c_count, w_rows, 3 * cols)
    )
    wqkv = lax.all_to_all(wqkv, "context", 0, 0, tiled=True).reshape(c_count * w_rows, 3 * cols)
    small_sent = after(small_sent, wqkv)
    small = lax.all_to_all(small_sent, EVERY, 0, 0, tiled=True)
    n_router = w_router.size
    router_w = small[:, :n_router].reshape(width, expert_count)
    gains = (
        small[:, n_router : n_router + norm_gains.size]
        .reshape(total, 4, norm_gains.shape[1])
        .transpose(1, 0, 2)
        .reshape(4, width)
        .astype(f32)
    )
    slot_of = small[:, n_router + norm_gains.size :].astype(jnp.int32)

    grad_out = cotangent[0]
    gate_blocks, up_blocks, down_blocks = split_experts(w_experts, halves)
    around = ("expert", "dp")
    wo_own = w_attn[:, 3 * width :].astype(bf16)
    g_gather = Gather(grad_out.astype(bf16))
    wqkv = after(wqkv, g_gather.around[1])
    wqkv_all = packed = lax.all_gather(wqkv, around, axis=0, tiled=True)
    if aligned:
        wo_all = near_gather(wo_own)
    else:
        wo_full = lax.all_gather(wo_own, EVERY, axis=0, tiled=True)
        wo_all = lax.dynamic_slice_in_dim(wo_full, me_c * cols, cols, axis=0)
    wqkv_all = (
        wqkv_all.reshape(e_count, z_count, c_count, w_rows, 3 * cols)
        .transpose(0, 2, 1, 3, 4)
        .reshape(width, 3 * cols)
    )

    w_down = exchange(down_blocks, packed)
    w_gate = exchange(gate_blocks, w_down)
    w_up = exchange(up_blocks, w_gate)
    w_gate_all, w_up_all = w_gate.reshape(width, ffh), w_up.reshape(width, ffh)

    inputs = tokens[0].astype(f32)
    pack_x = context_gather(tokens[0]).astype(f32)
    scale_one = lax.rsqrt(jnp.mean(pack_x * pack_x, axis=-1, keepdims=True) + epsilon)
    normed_one = (pack_x * scale_one * gains[0]).astype(bf16)
    qkv = mm(after(normed_one, gate_blocks, wo_all, g_gather.ring), wqkv_all)
    place, doc, offset = locate(
        jnp.arange(pack_rows, dtype=jnp.int32), lengths[0], block_order[0], blk_rows
    )
    half_width = head_width // 2
    freq = rope_base ** (-2.0 * jnp.arange(half_width, dtype=f32) / head_width)
    angle = offset.astype(f32)[:, None] * freq[None, :]
    cos_t, sin_t = jnp.cos(angle), jnp.sin(angle)
    cos_all = jnp.concatenate([cos_t, cos_t], axis=1)
    sin_all = jnp.concatenate([-sin_t, sin_t], axis=1)
    spots = jnp.stack([doc, place], axis=1)
    my_gains = lax.dynamic_index_in_dim(
        gains[2:].reshape(2, runs, c_count, run_cols), me_c, 2, keepdims=False
    ).reshape(2, cols)
    raw_q, raw_k = qkv[:, :cols], qkv[:, cols : 2 * cols]
    squares = jnp.stack([jnp.sum(raw_q * raw_q, axis=1), jnp.sum(raw_k * raw_k, axis=1)])
    scale_qk = lax.rsqrt(context_sum(squares) / width + epsilon).T
    query, key, value, mixed = mix(qkv, scale_qk, my_gains, cos_all, sin_all, spots, local_heads)
    hidden = after(inputs + context_scatter(mm(mixed, wo_all)), w_down)
    scale_two = lax.rsqrt(jnp.mean(hidden * hidden, axis=-1, keepdims=True) + epsilon)
    normed_two = (hidden * scale_two * gains[1]).astype(bf16)
    logits = mm(normed_two, router_w)
    probs = jax.nn.softmax(logits, axis=-1)

    order = source_order()
    all_normed = lax.all_gather(normed_two, EVERY, axis=0, tiled=True)
    all_normed = all_normed.reshape(total, tok_rows, width)
    gate_rows = lax.all_to_all(jnp.repeat(probs.T, halves, axis=0), EVERY, 0, 0, tiled=True)
    slots = jnp.arange(slot_cap, dtype=jnp.int32)
    slot_of = slot_of[order]
    gate_rows = gate_rows[order]
    gate = jnp.sum(
        jnp.where(slot_of[:, None, :] == slots[None, :, None], gate_rows[:, None, :], 0.0), axis=2
    ).reshape(total * slot_cap, 1)
    side = total // 2
    g_rows = jnp.concatenate(
        [
            take_rows(g_gather.near, g_gather.order(), slot_of[:side], slot_cap),
            take_rows(g_gather.others(w_gate), g_gather.order(), slot_of[side:], slot_cap),
        ]
    )
    w_down = w_down.reshape(width, ffh)
    back = mm(g_rows, w_down)
    all_normed = after(all_normed, back)
    *held, n2_send = run_expert(all_normed, order, slot_of, slot_cap, w_gate_all, w_up_all, back, gate, 1)
    n2_sum = Scatter(n2_send, tok_rows)
    *held, n2_keep = run_expert(all_normed, order, slot_of, slot_cap, w_gate_all, w_up_all, back, gate, 0, held)
    n_rows, act, act_scaled, grad_gu, grad_gate_slot = held
    grad_wd = mm_tn(g_rows, act_scaled).astype(bf16)
    grad_wd, n2_sum.got, n2_keep = tie(grad_wd, n2_sum.got, n2_keep)
    hits = jnp.arange(total)[:, None] == order[None, :]
    grad_gate_slot = grad_gate_slot.reshape(total, 1, slot_cap)
    sent_gates = jnp.sum(
        jnp.where(slot_of[:, :, None] == slots[None, None, :], grad_gate_slot, 0.0), axis=2
    )
    sent_gates = jnp.sum(jnp.where(hits[:, :, None], sent_gates[None], 0.0), axis=1)
    got_gates = lax.all_to_all(sent_gates, EVERY, 0, 0, tiled=True)
    grad_wd, got_gates, act = tie(grad_wd, got_gates, act)
    grad_probs = jnp.sum(got_gates.reshape(expert_count, halves, tok_rows), axis=1).T
    down_got = exchange(grad_wd.reshape(z_count, -1, ffh))
    n2_sum.begin(n2_keep)
    n2_sum.step()
    n_late, down_got = tie(n_rows, down_got)
    grad_wg = mm_tn(n_late, grad_gu[:, :ffh]).astype(bf16)
    gate_got = exchange(grad_wg.reshape(z_count, -1, ffh))
    (n_late,) = n2_sum.require(n_late)
    y_sum = Scatter(expert_output(act, gate, w_down, slot_of, slot_cap, 1), tok_rows)
    y_keep = expert_output(act, gate, w_down, slot_of, slot_cap, 0)
    n_late, y_keep = tie(n_late, y_keep)
    grad_wu = mm_tn(n_late, grad_gu[:, ffh:]).astype(bf16)
    while n2_sum.steps_left():
        n2_sum.step()
    y_sum.begin(y_keep)
    y_sum.step(n2_sum)
    n2_last = n2_sum.cross(gate_got)
    n2_last, grad_wu = y_sum.require(n2_last, grad_wu)
    grad_n2 = jnp.sum(n2_last.astype(f32), axis=0)
    up_got = exchange(grad_wu.reshape(z_count, -1, ffh), n2_last)

    grad_logits = (
        probs * (grad_probs - jnp.sum(probs * grad_probs, axis=-1, keepdims=True))
    ).astype(bf16)
    grad_n2 = grad_n2 + mm_nt(grad_logits, router_w)
    router_term = mm_tn(normed_two, grad_logits)

    def norm_back(v, scale, gain, grad):
        pulled = grad * gain
        inner = jnp.mean(v * pulled, axis=-1, keepdims=True)
        return scale * pulled - v * (scale * scale * scale * inner)

    gain_two = jnp.sum(grad_n2 * hidden * scale_two, axis=0)
    grad_hidden = grad_out + norm_back(hidden, scale_two, gains[1], grad_n2)
    grad_hidden_b = grad_hidden.astype(bf16)

    pack_dh = context_gather(grad_hidden_b)
    while y_sum.steps_left():
        y_sum.step()
    pull_q, pull_k, grad_v, gain_qk, inner = mix_back(
        qkv, scale_qk, my_gains, cos_all, sin_all, spots, local_heads, query, key, value, pack_dh, wo_all
    )
    def weight_blocks(left, right):
        return mm_tn(left, right).reshape(e_count, c_count, z_count, w_rows, right.shape[1])

    grad_wo = mm_tn(mixed, pack_dh)
    if aligned:
        wo_send = halved(grad_wo.reshape(e_count, z_count, w_rows, width))
    v_send = halved(weight_blocks(normed_one, grad_v)).transpose(1, 0, 2, 3)
    (inner,) = y_sum.require(inner)
    inner = context_sum(inner.T)
    if aligned:
        inner, v_send, wo_send = tie(inner, v_send, wo_send)
    inner = inner.T / width
    grad_qkv = jnp.concatenate(
        [
            scale_qk[:, 0:1] * pull_q - raw_q * (scale_qk[:, 0:1] ** 3 * inner[:, 0:1]),
            scale_qk[:, 1:2] * pull_k - raw_k * (scale_qk[:, 1:2] ** 3 * inner[:, 1:2]),
        ],
        axis=1,
    ).astype(bf16)
    grad_qkv = jnp.concatenate([grad_qkv, grad_v], axis=1)
    grad_experts = join_experts(gate_got, up_got, down_got, halves)
    qk_blocks = weight_blocks(normed_one, grad_qkv[:, : 2 * cols])
    grad_qkv, qk_blocks = tie(grad_qkv, qk_blocks)
    y_last = y_sum.cross(up_got)
    output = hidden + jnp.sum(y_last.astype(f32), axis=0)
    grad_n1 = context_scatter(mm_nt(grad_qkv, wqkv_all))
    own_scale = lax.rsqrt(jnp.mean(inputs * inputs, axis=-1, keepdims=True) + epsilon)
    gain_one = jnp.sum(grad_n1 * inputs * own_scale, axis=0)
    grad_tokens = grad_hidden + norm_back(inputs, own_scale, gains[0], grad_n1)


    if aligned:
        grad_wo, last = sum_over_dp(wo_send, y_last)
    else:
        whole_wo = lax.dynamic_update_slice_in_dim(
            jnp.zeros((width, width), f32), grad_wo, me_c * cols, axis=0
        )
        grad_wo = lax.psum_scatter(
            whole_wo.astype(bf16), EVERY, scatter_dimension=0, tiled=True
        ).astype(f32)
        last = y_last
    grad_v_sum, last = sum_over_dp(v_send, last)
    grad_qk_sum, _ = sum_over_dp(halved(qk_blocks).transpose(1, 0, 2, 3), last)
    grad_wqkv = jnp.concatenate([grad_qk_sum, grad_v_sum], axis=2).astype(bf16)
    grad_wqkv = (
        lax.all_to_all(grad_wqkv, "context", 0, 0, tiled=True)
        .reshape(c_count, w_rows, 3, runs, run_cols)
        .transpose(1, 2, 3, 0, 4)
        .reshape(w_rows, 3 * width)
        .astype(f32)
    )
    grad_attn = jnp.concatenate([grad_wqkv, grad_wo], axis=1)

    mine = jnp.arange(c_count)[None, None, :, None] == me_c
    gain_qk = jnp.where(mine, gain_qk.reshape(2, runs, 1, run_cols), 0.0)
    gain_rows = jnp.concatenate([jnp.stack([gain_one, gain_two]), gain_qk.reshape(2, width)])
    gain_rows = gain_rows.reshape(4, total, -1).transpose(1, 0, 2).reshape(total, -1)
    small_grads = jnp.concatenate([router_term.reshape(total, -1), gain_rows], axis=1)
    small_grads = jnp.sum(lax.all_to_all(small_grads, EVERY, 0, 0, tiled=True), axis=0)
    grad_router = small_grads[:n_router].reshape(w_router.shape)
    grad_gains = small_grads[n_router:].reshape(norm_gains.shape)
    return (output[None], grad_tokens[None], grad_attn, grad_router, grad_gains, grad_experts)


def solution(mesh):
    in_specs = (
        P(("expert", "dp"), "context", None),
        P(("expert", "dp"), "context", None),
        P(EVERY, None),
        P(EVERY, None),
        P(None, EVERY),
        P("dp", ("expert", "context"), None),
        P(("expert", "dp"), None),
        P(("expert", "dp"), None),
        P(("expert", "dp"), "context", None),
    )
    out_specs = (
        P(("expert", "dp"), "context", None),
        P(("expert", "dp"), "context", None),
        P(EVERY, None),
        P(EVERY, None),
        P(None, EVERY),
        P("dp", ("expert", "context"), None),
    )
    return jax.shard_map(
        on_device, mesh=mesh, in_specs=in_specs, out_specs=out_specs, check_vma=False
    )
```

```python
import jax
import jax.numpy as jnp
from jax import lax
from jax.experimental import pallas as pl
from jax.experimental.pallas import tpu as pltpu
from jax.sharding import PartitionSpec as P

HEADS = 16
epsilon = 1e-05
rope_base = 10000.0
masked_score = -1e30
bf16 = jnp.bfloat16
f32 = jnp.float32
EVERY = ("expert", "context", "dp")
QUICK = pl.CostEstimate(flops=1, bytes_accessed=1, transcendentals=0)


def mm(a, b):
    return jnp.dot(a, b, preferred_element_type=f32)


def mm_nt(a, b):
    return lax.dot_general(a, b, (((1,), (1,)), ((), ())), preferred_element_type=f32)


def mm_tn(a, b):
    return lax.dot_general(a, b, (((0,), (0,)), ((), ())), preferred_element_type=f32)


def swap(value, axis, bit):
    count = lax.axis_size(axis)
    return lax.ppermute(value, axis, [(i, i ^ bit) for i in range(count)])


def shift(value, axis, step):
    count = lax.axis_size(axis)
    return lax.ppermute(value, axis, [(i, (i + step) % count) for i in range(count)])


def bits_of(axis):
    count = lax.axis_size(axis)
    return [1 << i for i in range(count.bit_length() - 1)]


def locate(stored_rows, doc_lens, blk_order, blk_rows):
    block_ids = stored_rows // blk_rows
    block_hits = block_ids[:, None] == jnp.arange(blk_order.shape[0], dtype=jnp.int32)[None, :]
    placed_at = (
        jnp.sum(jnp.where(block_hits, blk_order[None, :], 0), axis=1) * blk_rows
        + stored_rows % blk_rows
    )
    doc_count = doc_lens.shape[0]
    upto = jnp.arange(doc_count)[:, None] >= jnp.arange(doc_count)[None, :]
    doc_ends = jnp.sum(jnp.where(upto, doc_lens[None, :], 0), axis=1)
    doc_ids = jnp.sum((placed_at[:, None] >= doc_ends[None, :]).astype(jnp.int32), axis=1)
    doc_hits = doc_ids[:, None] == jnp.arange(doc_count, dtype=jnp.int32)[None, :]
    doc_starts = doc_ends - doc_lens
    offset = placed_at - jnp.sum(jnp.where(doc_hits, doc_starts[None, :], 0), axis=1)
    return placed_at, doc_ids, offset


def context_gather(value):
    me = lax.axis_index("context")
    parts = [value]
    for bit in reversed(bits_of("context")):
        parts = parts + [swap(part, "context", bit) for part in parts]
    count = len(parts)
    order = []
    for r in range(count):
        source = 0
        for i, bit in enumerate(reversed(bits_of("context"))):
            if r >> i & 1:
                source |= bit
        order.append(source)
    stack = [None] * count
    for r in range(count):
        stack[order[r]] = parts[r]
    rows = []
    for target in range(count):
        rows.append(
            sum(
                jnp.where(me == target ^ m, stack[m], jnp.zeros_like(stack[m])) for m in range(count)
            )
        )
    return jnp.concatenate(rows, axis=0)


def context_sum(value):
    return jnp.sum(lax.all_gather(value, "context"), axis=0)


def half_step(value, axis, bit, dim):
    mine = (lax.axis_index(axis) // bit) % 2
    keep = lax.dynamic_index_in_dim(value, mine, dim, keepdims=False)
    send = lax.dynamic_index_in_dim(value, 1 - mine, dim, keepdims=False).astype(bf16)
    return keep.astype(f32) + swap(send, axis, bit).astype(f32)


def context_scatter(value):
    bits = bits_of("context")
    rows = value.shape[0] >> len(bits)
    value = value.reshape((2,) * len(bits) + (rows, value.shape[1]))
    left = list(reversed(bits))
    for bit in bits:
        dim = left.index(bit)
        value = half_step(value, "context", bit, dim)
        left.remove(bit)
    return value


def after(value, *done):
    return lax.optimization_barrier((value,) + done)[0] if done else value


def tie(*values):
    return lax.optimization_barrier(values)


def near_step():
    return ("context", bits_of("context")[0])


def far_steps():
    steps = [("context", b) for b in bits_of("context")[1:]]
    return steps + [("expert", b) for b in bits_of("expert")]


def source_order():
    steps = [near_step()] + far_steps()
    me = {axis: lax.axis_index(axis) for axis in EVERY}
    c_count, z_count = lax.axis_size("context"), lax.axis_size("dp")
    order = []
    for i in range(1 << len(steps)):
        masks = {"expert": 0, "context": 0}
        for j, (axis, bit) in enumerate(steps):
            if i >> (len(steps) - 1 - j) & 1:
                masks[axis] |= bit
        column = (me["expert"] ^ masks["expert"]) * c_count + (me["context"] ^ masks["context"])
        order += [column * z_count + z for z in range(z_count)]
    return jnp.stack(order).astype(jnp.int32)


class Gather:
    def __init__(self, value):
        around = [value]
        for _ in range(lax.axis_size("dp") - 1):
            around.append(shift(around[-1], "dp", 1))
        self.ring, self.around = around[-1], around
        self.half = value.shape[1] // 2

    def spread(self, done):
        far, half = far_steps(), self.half
        shape = (-1, self.ring.shape[0], half)
        self.near = []
        for i in range(2):
            held = jnp.stack([part[:, i * half : (i + 1) * half] for part in self.around])
            held = held.reshape((1,) * len(far) + held.shape)
            for level, step in enumerate(far[::-1] if i else far):
                got = swap(held, *step)
                if i and level == len(far) - 1:
                    got = after(got, done)
                held = jnp.concatenate([held, got], axis=far.index(step))
            self.near.append(held.reshape(shape))

    def others(self, *done):
        return [swap(after(held, *done), *near_step()) for held in self.near]

    def order(self):
        z_count = lax.axis_size("dp")
        spots = jnp.arange(self.near[0].shape[0], dtype=jnp.int32)
        return spots // z_count * z_count + (lax.axis_index("dp") - spots) % z_count


class Scatter:
    def __init__(self, send, rows):
        self.far = far_steps()
        self.shape = (2,) * len(self.far) + (lax.axis_size("dp"), rows)
        self.got = swap(send, *near_step())

    def begin(self, keep, *done):
        far, width = self.far, keep.shape[-1]
        half = width // 2
        keep = keep.reshape(self.shape + (width,))
        got = after(self.got, *done).reshape(self.shape + (width,))
        self.states = []
        for i in range(2):
            cut = slice(i * half, (i + 1) * half)
            self.states.append((keep[..., cut], got[..., cut], far[::-1] if i else far, list(far)))

    def step(self, other=None):
        sums = []
        for own, got, order, left in self.states:
            step = order[len(order) - len(left)]
            dim = left.index(step)
            first = [slice(None)] * dim + [0]
            second = [slice(None)] * dim + [1]
            sent = own[tuple(second)].astype(f32) + got[tuple(second)].astype(f32)
            kept = own[tuple(first)].astype(f32) + got[tuple(first)].astype(f32)
            sums.append([kept.astype(bf16), sent.astype(bf16), step, order, left[:dim] + left[dim + 1 :]])
        if other:
            sent = other.require(*[entry[1] for entry in sums])
            for entry, new in zip(sums, sent):
                entry[1] = new
        self.states = [
            (kept, swap(sent, *step), order, left) for kept, sent, step, order, left in sums
        ]

    def require(self, *values):
        count = len(self.states)
        *got, = tie(*[state[1] for state in self.states], *values)
        self.states = [
            state[:1] + (new,) + state[2:] for state, new in zip(self.states, got[:count])
        ]
        return got[count:]

    def kept(self):
        return [state[0] for state in self.states]

    def keep(self, kept):
        self.states = [(own,) + state[1:] for own, state in zip(kept, self.states)]

    def steps_left(self):
        return len(self.states[0][3])

    def cross(self, *done):
        blocks = jnp.concatenate(
            [
                (own.astype(f32) + got.astype(f32)).astype(bf16)
                for own, got, _, _ in self.states
            ],
            axis=-1,
        )
        return exchange(blocks, *done)


def sources_per_block(slot_cap):
    count = 1
    while count * slot_cap % 16:
        count *= 2
    return count


def take_kernel(per, slot_cap, order_ref, slot_ref, *refs):
    *rows, out_ref = refs
    places = lax.broadcasted_iota(jnp.int32, (slot_cap, slot_ref.shape[2]), 0)
    picks = [(slot_ref[j] == places).astype(f32).astype(bf16) for j in range(per)]
    at = 0
    for p in range(0, len(rows), per):
        part = [jnp.dot(picks[j], rows[p + j][0], preferred_element_type=f32) for j in range(per)]
        width = part[0].shape[1]
        out_ref[:, at : at + width] = jnp.concatenate(part).astype(bf16)
        at += width


def take_rows(parts, order, slots, slot_cap):
    count = order.shape[0]
    tokens = slots.shape[1]
    per = sources_per_block(slot_cap)
    width = sum(part.shape[2] for part in parts)

    def block_of(part, j):
        return pl.BlockSpec(
            (1, tokens, part.shape[2]), lambda i, order_ref: (order_ref[i * per + j], 0, 0)
        )

    return pl.pallas_call(
        lambda *refs: take_kernel(per, slot_cap, *refs),
        grid_spec=pltpu.PrefetchScalarGridSpec(
            num_scalar_prefetch=1,
            grid=(count // per,),
            in_specs=[pl.BlockSpec((per, 1, tokens), lambda i, order_ref: (i, 0, 0))]
            + [block_of(part, j) for part in parts for j in range(per)],
            out_specs=pl.BlockSpec((per * slot_cap, width), lambda i, order_ref: (i, 0)),
        ),
        out_shape=jax.ShapeDtypeStruct((count * slot_cap, width), bf16),
        cost_estimate=QUICK,
        compiler_params=pltpu.CompilerParams(vmem_limit_bytes=40 * 2**20),
    )(order, slots.reshape(count, 1, tokens), *[part for part in parts for _ in range(per)])


def output_kernel(per, slot_cap, slot_ref, act_ref, gate_ref, w_ref, out_ref):
    places = lax.broadcasted_iota(jnp.int32, (slot_cap, slot_ref.shape[2]), 0)
    rows = mm_nt(act_ref[...], w_ref[...]) * gate_ref[...]
    for j in range(per):
        pick = (slot_ref[j] == places).astype(f32).astype(bf16)
        part = rows[j * slot_cap : (j + 1) * slot_cap].astype(bf16)
        out_ref[j] = mm_tn(pick, part).astype(bf16)


def expert_output(act, gate, w_down, slots, slot_cap, side):
    total, tokens = slots.shape
    width, ffh = w_down.shape
    per = max(sources_per_block(slot_cap), 8)
    steps = total // 2 // per
    first = side * steps

    def rows_of(columns):
        return pl.BlockSpec((per * slot_cap, columns), lambda i: (i + first, 0))

    return pl.pallas_call(
        lambda *refs: output_kernel(per, slot_cap, *refs),
        grid=(steps,),
        in_specs=[
            pl.BlockSpec((per, 1, tokens), lambda i: (i + first, 0, 0)),
            rows_of(ffh),
            rows_of(1),
            pl.BlockSpec((width, ffh), lambda i: (0, 0)),
        ],
        out_specs=pl.BlockSpec((per, tokens, width), lambda i: (i, 0, 0)),
        out_shape=jax.ShapeDtypeStruct((total // 2, tokens, width), bf16),
        cost_estimate=pl.CostEstimate(
            flops=total * slot_cap * width * (ffh + tokens),
            bytes_accessed=total * tokens * width,
            transcendentals=0,
        ),
        compiler_params=pltpu.CompilerParams(vmem_limit_bytes=48 * 2**20),
    )(slots.reshape(total, 1, tokens), act, gate, w_down)


def turn(v, cos, sin):
    return v * cos + pltpu.roll(v, v.shape[1] // 2, 1) * sin


def turn_back(v, cos, sin):
    return v * cos + pltpu.roll(v * sin, v.shape[1] // 2, 1)


def soften(query, key, score_scale, spot_ref, spot_t_ref):
    scores = mm_nt(query, key) * score_scale
    same = spot_ref[:, 0:1] == spot_t_ref[0:1, :]
    allowed = same & (spot_t_ref[1:2, :] <= spot_ref[:, 1:2])
    scores = jnp.where(allowed, scores, masked_score)
    raised = jnp.exp(scores - jnp.max(scores, axis=1, keepdims=True))
    return raised / jnp.sum(raised, axis=1, keepdims=True)


def mix_kernel(score_scale, q_ref, k_ref, v_ref, scale_ref, gain_ref, cos_ref, sin_ref, *refs):
    spot_ref, spot_t_ref, query_ref, key_ref, value_ref, mixed_ref = refs
    cos, sin = cos_ref[...], sin_ref[...]
    query = turn(q_ref[...] * scale_ref[:, 0:1] * gain_ref[0:1, :], cos, sin).astype(bf16)
    key = turn(k_ref[...] * scale_ref[:, 1:2] * gain_ref[1:2, :], cos, sin).astype(bf16)
    value = v_ref[...].astype(bf16)
    soft = soften(query, key, score_scale, spot_ref, spot_t_ref)
    query_ref[...], key_ref[...], value_ref[...] = query, key, value
    mixed_ref[...] = mm(soft.astype(bf16), value).astype(bf16)


def mix_back_kernel(score_scale, q_ref, k_ref, scale_ref, gain_ref, cos_ref, sin_ref, *refs):
    spot_ref, spot_t_ref, query_ref, key_ref, value_ref, dh_ref, wo_ref = refs[:7]
    pull_q_ref, pull_k_ref, grad_v_ref, gain_out_ref, inner_ref = refs[7:]
    cos, sin = cos_ref[...], sin_ref[...]
    query, key, value = query_ref[...], key_ref[...], value_ref[...]
    grad_mixed = mm_nt(dh_ref[...], wo_ref[...]).astype(bf16)
    soft = soften(query, key, score_scale, spot_ref, spot_t_ref)
    grad_soft = mm_nt(grad_mixed, value)
    delta = jnp.sum(soft * grad_soft, axis=1, keepdims=True)
    grad_scores = (soft * (grad_soft - delta)).astype(bf16)
    grad_v_ref[...] = mm_tn(soft.astype(bf16), grad_mixed).astype(bf16)
    inner = []
    for i, (grad, raw_ref, out_ref) in enumerate(
        (
            (mm(grad_scores, key), q_ref, pull_q_ref),
            (mm_tn(grad_scores, query), k_ref, pull_k_ref),
        )
    ):
        back = turn_back(grad * score_scale, cos, sin)
        raw, scale = raw_ref[...], scale_ref[:, i : i + 1]
        pull = back * gain_ref[i : i + 1, :]
        gain_out_ref[i : i + 1, :] = jnp.sum(back * raw * scale, axis=0, keepdims=True)
        inner.append(jnp.sum(raw * pull, axis=1, keepdims=True))
        out_ref[...] = pull
    both = jnp.concatenate(inner, axis=1)

    @pl.when(pl.program_id(0) == 0)
    def _():
        inner_ref[...] = both

    @pl.when(pl.program_id(0) > 0)
    def _():
        inner_ref[...] += both


def head_specs(rows, head_width, heads):
    def part(p):
        return pl.BlockSpec((rows, head_width), lambda h: (0, h + p * heads))

    def fixed(*shape):
        return pl.BlockSpec(shape, lambda h: (0,) * len(shape))

    gain = pl.BlockSpec((2, head_width), lambda h: (0, h))
    return part, fixed, gain


def mix(qkv, scale, gains, cos, sin, spots, heads):
    rows, head_width = cos.shape
    part, fixed, gain = head_specs(rows, head_width, heads)
    return pl.pallas_call(
        lambda *refs: mix_kernel(head_width**-0.5, *refs),
        grid=(heads,),
        in_specs=[part(0), part(1), part(2), fixed(rows, 2), gain, fixed(rows, head_width)]
        + [fixed(rows, head_width), fixed(rows, 2), fixed(2, rows)],
        out_specs=[part(0)] * 4,
        out_shape=[jax.ShapeDtypeStruct((rows, heads * head_width), bf16)] * 4,
        cost_estimate=QUICK,
        compiler_params=pltpu.CompilerParams(vmem_limit_bytes=40 * 2**20),
    )(qkv, qkv, qkv, scale, gains, cos, sin, spots, spots.T)


def mix_back(qkv, scale, gains, cos, sin, spots, heads, query, key, value, dh, wo):
    rows, head_width = cos.shape
    part, fixed, gain = head_specs(rows, head_width, heads)
    cols = heads * head_width
    return pl.pallas_call(
        lambda *refs: mix_back_kernel(head_width**-0.5, *refs),
        grid=(heads,),
        in_specs=[part(0), part(1), fixed(rows, 2), gain, fixed(rows, head_width)]
        + [fixed(rows, head_width), fixed(rows, 2), fixed(2, rows), part(0), part(0), part(0)]
        + [fixed(*dh.shape), pl.BlockSpec((head_width, wo.shape[1]), lambda h: (h, 0))],
        out_specs=[part(0), part(0), part(0), gain, fixed(rows, 2)],
        out_shape=[jax.ShapeDtypeStruct((rows, cols), f32)] * 2
        + [jax.ShapeDtypeStruct((rows, cols), bf16), jax.ShapeDtypeStruct((2, cols), f32)]
        + [jax.ShapeDtypeStruct((rows, 2), f32)],
        cost_estimate=QUICK,
        compiler_params=pltpu.CompilerParams(vmem_limit_bytes=48 * 2**20),
    )(qkv, qkv, scale, gains, cos, sin, spots, spots.T, query, key, value, dh, wo)


def expert_kernel(per, slot_cap, order_ref, slot_ref, *refs):
    xs, (wg_ref, wu_ref, back_ref, gate_ref) = refs[:per], refs[per : per + 4]
    n_ref, act_ref, scaled_ref, gu_ref, dgate_ref, out_ref = refs[-6:]
    ffh = act_ref.shape[1]
    places = lax.broadcasted_iota(jnp.int32, (slot_cap, slot_ref.shape[2]), 0)
    picks = [(slot_ref[j] == places).astype(f32).astype(bf16) for j in range(per)]
    rows = jnp.concatenate([mm(picks[j], xs[j][0]) for j in range(per)]).astype(bf16)
    n_ref[...] = rows
    gate_part, up_part = mm(rows, wg_ref[...]), mm(rows, wu_ref[...])
    sig = jax.nn.sigmoid(gate_part)
    silu = gate_part * sig
    act = (silu * up_part).astype(bf16)
    act_f = act.astype(f32)
    back, gate = back_ref[...], gate_ref[...]
    act_ref[...] = act
    scaled_ref[...] = (act_f * gate).astype(bf16)
    dgate_ref[...] = jnp.sum(act_f * back, axis=1, keepdims=True)
    grad_act = back * gate
    grad_gate = (grad_act * up_part * sig * (1.0 + gate_part * (1.0 - sig))).astype(bf16)
    grad_up = (grad_act * silu).astype(bf16)
    gu_ref[:, :ffh] = grad_gate
    gu_ref[:, ffh:] = grad_up
    grad_rows = mm_nt(grad_gate, wg_ref[...]) + mm_nt(grad_up, wu_ref[...])
    for j in range(per):
        part = grad_rows[j * slot_cap : (j + 1) * slot_cap].astype(bf16)
        out_ref[j] = mm_tn(picks[j], part).astype(bf16)


def run_expert(rows, order, slots, slot_cap, w_gate, w_up, back, gate, side, held=()):
    total, tokens, width = rows.shape
    ffh = back.shape[1]
    per = max(sources_per_block(slot_cap), 8)
    steps = total // 2 // per
    first = side * steps
    block = per * slot_cap

    def block_of(j):
        return pl.BlockSpec(
            (1, tokens, width), lambda i, order_ref: (order_ref[(i + first) * per + j], 0, 0)
        )

    def rows_of(columns):
        return pl.BlockSpec((block, columns), lambda i, order_ref: (i + first, 0))

    def whole(columns, dtype):
        return jax.ShapeDtypeStruct((total * slot_cap, columns), dtype)

    in_specs = [pl.BlockSpec((per, 1, tokens), lambda i, order_ref: (i + first, 0, 0))]
    in_specs += [block_of(j) for j in range(per)]
    in_specs += [pl.BlockSpec(w_gate.shape, lambda i, order_ref: (0, 0))] * 2
    in_specs += [rows_of(ffh), rows_of(1)]
    aliases = {len(in_specs) + 1 + i: i for i in range(len(held))}
    in_specs += [pl.BlockSpec(memory_space=pl.ANY) for _ in held]
    return pl.pallas_call(
        lambda *refs: expert_kernel(per, slot_cap, *refs),
        grid_spec=pltpu.PrefetchScalarGridSpec(
            num_scalar_prefetch=1,
            grid=(steps,),
            in_specs=in_specs,
            out_specs=[rows_of(width), rows_of(ffh), rows_of(ffh), rows_of(2 * ffh), rows_of(1)]
            + [pl.BlockSpec((per, tokens, width), lambda i, order_ref: (i, 0, 0))],
        ),
        out_shape=[whole(width, bf16), whole(ffh, bf16), whole(ffh, bf16), whole(2 * ffh, bf16)]
        + [whole(1, f32), jax.ShapeDtypeStruct((total // 2, tokens, width), bf16)],
        input_output_aliases=aliases,
        cost_estimate=QUICK,
        compiler_params=pltpu.CompilerParams(vmem_limit_bytes=58 * 2**20),
    )(order, slots.reshape(total, 1, tokens), *([rows] * per), w_gate, w_up, back, gate, *held)


def exchange(blocks, *done):
    return lax.all_to_all(after(blocks, *done), "dp", 0, 0, tiled=True)


def split_kernel(experts, halves, w_ref, *out_refs):
    ffh = out_refs[0].shape[2]
    for e in range(experts):
        rows = w_ref[:, e, :].astype(bf16)
        for h in range(halves):
            for j in range(3):
                at = (j * halves + h) * ffh
                out_refs[j][e * halves + h] = rows[:, at : at + ffh]


def split_experts(w, halves):
    rows, experts, width = w.shape
    block, shares, ffh = 64, experts * halves, width // (3 * halves)
    return pl.pallas_call(
        lambda *refs: split_kernel(experts, halves, *refs),
        grid=(rows // block,),
        in_specs=[pl.BlockSpec((block, experts, width), lambda i: (i, 0, 0))],
        out_specs=[pl.BlockSpec((shares, block, ffh), lambda i: (0, i, 0))] * 3,
        out_shape=[jax.ShapeDtypeStruct((shares, rows, ffh), bf16)] * 3,
        cost_estimate=QUICK,
        compiler_params=pltpu.CompilerParams(vmem_limit_bytes=32 * 2**20),
    )(w)


def join_kernel(halves, gate_ref, up_ref, down_ref, out_ref):
    shares, _, ffh = gate_ref.shape
    for t in range(shares):
        e, h = divmod(t, halves)
        for j, ref in enumerate((gate_ref, up_ref, down_ref)):
            at = (j * halves + h) * ffh
            out_ref[:, e, at : at + ffh] = ref[t].astype(f32)


def join_experts(gate, up, down, halves):
    shares, rows, ffh = gate.shape
    block, experts, width = 64, shares // halves, 3 * ffh * halves
    return pl.pallas_call(
        lambda *refs: join_kernel(halves, *refs),
        grid=(rows // block,),
        in_specs=[pl.BlockSpec((shares, block, ffh), lambda i: (0, i, 0))] * 3,
        out_specs=pl.BlockSpec((block, experts, width), lambda i: (i, 0, 0)),
        out_shape=jax.ShapeDtypeStruct((rows, experts, width), f32),
        cost_estimate=QUICK,
        compiler_params=pltpu.CompilerParams(vmem_limit_bytes=32 * 2**20),
    )(gate, up, down)


def near_gather(piece):
    around = [piece]
    for _ in range(lax.axis_size("dp") - 1):
        around.append(shift(around[-1], "dp", 1))
    held = [jnp.stack(around)]
    for bit in bits_of("expert"):
        held = held + [swap(part, "expert", bit) for part in held]
    me_e, me_z = lax.axis_index("expert"), lax.axis_index("dp")
    z_count = len(around)
    whole = jnp.zeros((len(held), z_count) + piece.shape, piece.dtype)
    for r, part in enumerate(held):
        for k in range(z_count):
            at = (me_e ^ r, (me_z - k) % z_count, 0, 0)
            whole = lax.dynamic_update_slice(whole, part[None, k : k + 1], at)
    return whole.reshape(-1, piece.shape[1])


def halved(value):
    for bit in reversed(bits_of("expert")):
        if bit == 1:
            value = value.reshape((value.shape[0] // 2, 2) + value.shape[1:])
            value = half_step(value, "expert", 1, 1)
        else:
            value = value.reshape((2, value.shape[0] // 2) + value.shape[1:])
            value = half_step(value, "expert", bit, 0)
    return value[0].astype(bf16)


def sum_over_dp(blocks, *done):
    arrived = exchange(blocks, *done)
    return jnp.sum(arrived.astype(f32), axis=0), arrived


def on_device(
    tokens, cotangent, w_attn, w_router, norm_gains, w_experts, lengths, block_order, routes
):
    tok_rows, width = tokens.shape[1:]
    blk_rows = tok_rows // 2
    e_count, c_count, z_count = (lax.axis_size(a) for a in EVERY)
    total = e_count * c_count * z_count
    me_e, me_c, me_z = (lax.axis_index(a) for a in EVERY)
    pack_rows = tok_rows * c_count
    pick_rows = routes[0]
    top_count = pick_rows.shape[1]
    local_experts = w_experts.shape[1]
    expert_count = local_experts * e_count * c_count
    slot_cap = tok_rows * top_count * 9 // (8 * expert_count)
    ffn = w_experts.shape[2] // 3
    halves = z_count // local_experts
    ffh = ffn // halves
    head_width = width // HEADS
    local_heads = HEADS // c_count
    cols = local_heads * head_width
    w_rows = w_attn.shape[0]
    score_scale = head_width ** (-0.5)
    block_rows = z_count * w_rows
    aligned = block_rows % head_width == 0
    head_run = block_rows // head_width if aligned else local_heads
    runs = local_heads // head_run
    run_cols = head_run * head_width

    expert_ids = jnp.arange(expert_count, dtype=jnp.int32)
    pick_hits = (pick_rows[:, :, None] == expert_ids[None, None, :]).astype(f32)
    named = jnp.sum(pick_hits, axis=1)
    earlier = jnp.arange(tok_rows)[:, None] > jnp.arange(tok_rows)[None, :]
    ranks = mm(earlier.astype(bf16), named.astype(bf16))
    rank_rows = jnp.repeat(jnp.where(named > 0, ranks, -1.0).T, halves, axis=0)
    own_row = jnp.concatenate(
        [w_router.astype(bf16).reshape(-1), norm_gains.astype(bf16).reshape(-1)]
    )
    small_sent = jnp.concatenate(
        [jnp.broadcast_to(own_row[None], (total, own_row.shape[0])), rank_rows.astype(bf16)], axis=1
    )
    wqkv = (
        w_attn[:, : 3 * width]
        .astype(bf16)
        .reshape(w_rows, 3, runs, c_count, run_cols)
        .transpose(3, 0, 1, 2, 4)
        .reshape(c_count, w_rows, 3 * cols)
    )
    wqkv = lax.all_to_all(wqkv, "context", 0, 0, tiled=True).reshape(c_count * w_rows, 3 * cols)
    small_sent = after(small_sent, wqkv)
    small = lax.all_to_all(small_sent, EVERY, 0, 0, tiled=True)
    n_router = w_router.size
    router_w = small[:, :n_router].reshape(width, expert_count)
    gains = (
        small[:, n_router : n_router + norm_gains.size]
        .reshape(total, 4, norm_gains.shape[1])
        .transpose(1, 0, 2)
        .reshape(4, width)
        .astype(f32)
    )
    slot_of = small[:, n_router + norm_gains.size :].astype(jnp.int32)

    grad_out = cotangent[0]
    gate_blocks, up_blocks, down_blocks = split_experts(w_experts, halves)
    around = ("expert", "dp")
    wo_own = w_attn[:, 3 * width :].astype(bf16)
    g_gather = Gather(grad_out.astype(bf16))
    wqkv = after(wqkv, g_gather.around[1])
    wqkv_all = packed = lax.all_gather(wqkv, around, axis=0, tiled=True)
    if aligned:
        wo_all = near_gather(wo_own)
    else:
        wo_full = lax.all_gather(wo_own, EVERY, axis=0, tiled=True)
        wo_all = lax.dynamic_slice_in_dim(wo_full, me_c * cols, cols, axis=0)
    wqkv_all = (
        wqkv_all.reshape(e_count, z_count, c_count, w_rows, 3 * cols)
        .transpose(0, 2, 1, 3, 4)
        .reshape(width, 3 * cols)
    )

    w_down = exchange(down_blocks, packed)
    w_gate = exchange(gate_blocks, w_down)
    w_up = exchange(up_blocks, w_gate)
    g_gather.spread(w_gate)
    w_gate_all, w_up_all = w_gate.reshape(width, ffh), w_up.reshape(width, ffh)

    inputs = tokens[0].astype(f32)
    pack_x = context_gather(tokens[0]).astype(f32)
    scale_one = lax.rsqrt(jnp.mean(pack_x * pack_x, axis=-1, keepdims=True) + epsilon)
    normed_one = (pack_x * scale_one * gains[0]).astype(bf16)
    qkv = mm(after(normed_one, gate_blocks, wo_all, g_gather.ring), wqkv_all)
    place, doc, offset = locate(
        jnp.arange(pack_rows, dtype=jnp.int32), lengths[0], block_order[0], blk_rows
    )
    half_width = head_width // 2
    freq = rope_base ** (-2.0 * jnp.arange(half_width, dtype=f32) / head_width)
    angle = offset.astype(f32)[:, None] * freq[None, :]
    cos_t, sin_t = jnp.cos(angle), jnp.sin(angle)
    cos_all = jnp.concatenate([cos_t, cos_t], axis=1)
    sin_all = jnp.concatenate([-sin_t, sin_t], axis=1)
    spots = jnp.stack([doc, place], axis=1)
    my_gains = lax.dynamic_index_in_dim(
        gains[2:].reshape(2, runs, c_count, run_cols), me_c, 2, keepdims=False
    ).reshape(2, cols)
    raw_q, raw_k = qkv[:, :cols], qkv[:, cols : 2 * cols]
    squares = jnp.stack([jnp.sum(raw_q * raw_q, axis=1), jnp.sum(raw_k * raw_k, axis=1)])
    scale_qk = lax.rsqrt(context_sum(squares) / width + epsilon).T
    query, key, value, mixed = mix(qkv, scale_qk, my_gains, cos_all, sin_all, spots, local_heads)
    hidden = after(inputs + context_scatter(mm(mixed, wo_all)), w_down)
    scale_two = lax.rsqrt(jnp.mean(hidden * hidden, axis=-1, keepdims=True) + epsilon)
    normed_two = (hidden * scale_two * gains[1]).astype(bf16)
    logits = mm(normed_two, router_w)
    probs = jax.nn.softmax(logits, axis=-1)

    order = source_order()
    all_normed = lax.all_gather(normed_two, EVERY, axis=0, tiled=True)
    all_normed = all_normed.reshape(total, tok_rows, width)
    gate_rows = lax.all_to_all(jnp.repeat(probs.T, halves, axis=0), EVERY, 0, 0, tiled=True)
    slots = jnp.arange(slot_cap, dtype=jnp.int32)
    slot_of = slot_of[order]
    gate_rows = gate_rows[order]
    gate = jnp.sum(
        jnp.where(slot_of[:, None, :] == slots[None, :, None], gate_rows[:, None, :], 0.0), axis=2
    ).reshape(total * slot_cap, 1)
    side = total // 2
    g_rows = jnp.concatenate(
        [
            take_rows(g_gather.near, g_gather.order(), slot_of[:side], slot_cap),
            take_rows(g_gather.others(w_gate), g_gather.order(), slot_of[side:], slot_cap),
        ]
    )
    w_down = w_down.reshape(width, ffh)
    back = mm(g_rows, w_down)
    all_normed = after(all_normed, back)
    *held, n2_send = run_expert(all_normed, order, slot_of, slot_cap, w_gate_all, w_up_all, back, gate, 1)
    n2_sum = Scatter(n2_send, tok_rows)
    *held, n2_keep = run_expert(all_normed, order, slot_of, slot_cap, w_gate_all, w_up_all, back, gate, 0, held)
    n_rows, act, act_scaled, grad_gu, grad_gate_slot = held
    grad_wd = mm_tn(g_rows, act_scaled).astype(bf16)
    grad_wd, n2_sum.got, n2_keep = tie(grad_wd, n2_sum.got, n2_keep)
    hits = jnp.arange(total)[:, None] == order[None, :]
    grad_gate_slot = grad_gate_slot.reshape(total, 1, slot_cap)
    sent_gates = jnp.sum(
        jnp.where(slot_of[:, :, None] == slots[None, None, :], grad_gate_slot, 0.0), axis=2
    )
    sent_gates = jnp.sum(jnp.where(hits[:, :, None], sent_gates[None], 0.0), axis=1)
    got_gates = lax.all_to_all(sent_gates, EVERY, 0, 0, tiled=True)
    grad_wd, got_gates, act = tie(grad_wd, got_gates, act)
    grad_probs = jnp.sum(got_gates.reshape(expert_count, halves, tok_rows), axis=1).T
    down_got = exchange(grad_wd.reshape(z_count, -1, ffh))
    n2_sum.begin(n2_keep)
    n2_sum.step()
    n_late, down_got = tie(n_rows, down_got)
    grad_wg = mm_tn(n_late, grad_gu[:, :ffh]).astype(bf16)
    gate_got = exchange(grad_wg.reshape(z_count, -1, ffh))
    (n_late,) = n2_sum.require(n_late)
    y_sum = Scatter(expert_output(act, gate, w_down, slot_of, slot_cap, 1), tok_rows)
    y_keep = expert_output(act, gate, w_down, slot_of, slot_cap, 0)
    n_late, y_keep = tie(n_late, y_keep)
    grad_wu = mm_tn(n_late, grad_gu[:, ffh:]).astype(bf16)
    while n2_sum.steps_left():
        n2_sum.step()
    y_sum.begin(y_keep)
    y_sum.step(n2_sum)
    n2_last = n2_sum.cross(gate_got)
    n2_last, grad_wu = y_sum.require(n2_last, grad_wu)
    grad_n2 = jnp.sum(n2_last.astype(f32), axis=0)
    up_got = exchange(grad_wu.reshape(z_count, -1, ffh), n2_last)

    grad_logits = (
        probs * (grad_probs - jnp.sum(probs * grad_probs, axis=-1, keepdims=True))
    ).astype(bf16)
    grad_n2 = grad_n2 + mm_nt(grad_logits, router_w)
    router_term = mm_tn(normed_two, grad_logits)

    def norm_back(v, scale, gain, grad):
        pulled = grad * gain
        inner = jnp.mean(v * pulled, axis=-1, keepdims=True)
        return scale * pulled - v * (scale * scale * scale * inner)

    gain_two = jnp.sum(grad_n2 * hidden * scale_two, axis=0)
    grad_hidden = grad_out + norm_back(hidden, scale_two, gains[1], grad_n2)
    grad_hidden_b = grad_hidden.astype(bf16)

    pack_dh = context_gather(grad_hidden_b)
    while y_sum.steps_left():
        y_sum.step()
    pull_q, pull_k, grad_v, gain_qk, inner = mix_back(
        qkv, scale_qk, my_gains, cos_all, sin_all, spots, local_heads, query, key, value, pack_dh, wo_all
    )
    def weight_blocks(left, right):
        return mm_tn(left, right).reshape(e_count, c_count, z_count, w_rows, right.shape[1])

    grad_wo = mm_tn(mixed, pack_dh)
    if aligned:
        wo_send = halved(grad_wo.reshape(e_count, z_count, w_rows, width))
    v_send = halved(weight_blocks(normed_one, grad_v)).transpose(1, 0, 2, 3)
    (inner,) = y_sum.require(inner)
    inner = context_sum(inner.T)
    if aligned:
        inner, v_send, wo_send = tie(inner, v_send, wo_send)
    inner = inner.T / width
    grad_qkv = jnp.concatenate(
        [
            scale_qk[:, 0:1] * pull_q - raw_q * (scale_qk[:, 0:1] ** 3 * inner[:, 0:1]),
            scale_qk[:, 1:2] * pull_k - raw_k * (scale_qk[:, 1:2] ** 3 * inner[:, 1:2]),
        ],
        axis=1,
    ).astype(bf16)
    grad_qkv = jnp.concatenate([grad_qkv, grad_v], axis=1)
    grad_experts = join_experts(gate_got, up_got, down_got, halves)
    qk_blocks = weight_blocks(normed_one, grad_qkv[:, : 2 * cols])
    grad_qkv, qk_blocks = tie(grad_qkv, qk_blocks)
    y_last = y_sum.cross(up_got)
    output = hidden + jnp.sum(y_last.astype(f32), axis=0)
    grad_n1 = context_scatter(mm_nt(grad_qkv, wqkv_all))
    own_scale = lax.rsqrt(jnp.mean(inputs * inputs, axis=-1, keepdims=True) + epsilon)
    gain_one = jnp.sum(grad_n1 * inputs * own_scale, axis=0)
    grad_tokens = grad_hidden + norm_back(inputs, own_scale, gains[0], grad_n1)


    if aligned:
        grad_wo, last = sum_over_dp(wo_send, y_last)
    else:
        whole_wo = lax.dynamic_update_slice_in_dim(
            jnp.zeros((width, width), f32), grad_wo, me_c * cols, axis=0
        )
        grad_wo = lax.psum_scatter(
            whole_wo.astype(bf16), EVERY, scatter_dimension=0, tiled=True
        ).astype(f32)
        last = y_last
    grad_v_sum, last = sum_over_dp(v_send, last)
    grad_qk_sum, _ = sum_over_dp(halved(qk_blocks).transpose(1, 0, 2, 3), last)
    grad_wqkv = jnp.concatenate([grad_qk_sum, grad_v_sum], axis=2).astype(bf16)
    grad_wqkv = (
        lax.all_to_all(grad_wqkv, "context", 0, 0, tiled=True)
        .reshape(c_count, w_rows, 3, runs, run_cols)
        .transpose(1, 2, 3, 0, 4)
        .reshape(w_rows, 3 * width)
        .astype(f32)
    )
    grad_attn = jnp.concatenate([grad_wqkv, grad_wo], axis=1)

    mine = jnp.arange(c_count)[None, None, :, None] == me_c
    gain_qk = jnp.where(mine, gain_qk.reshape(2, runs, 1, run_cols), 0.0)
    gain_rows = jnp.concatenate([jnp.stack([gain_one, gain_two]), gain_qk.reshape(2, width)])
    gain_rows = gain_rows.reshape(4, total, -1).transpose(1, 0, 2).reshape(total, -1)
    small_grads = jnp.concatenate([router_term.reshape(total, -1), gain_rows], axis=1)
    small_grads = jnp.sum(lax.all_to_all(small_grads, EVERY, 0, 0, tiled=True), axis=0)
    grad_router = small_grads[:n_router].reshape(w_router.shape)
    grad_gains = small_grads[n_router:].reshape(norm_gains.shape)
    return (output[None], grad_tokens[None], grad_attn, grad_router, grad_gains, grad_experts)


def solution(mesh):
    in_specs = (
        P(("expert", "dp"), "context", None),
        P(("expert", "dp"), "context", None),
        P(EVERY, None),
        P(EVERY, None),
        P(None, EVERY),
        P("dp", ("expert", "context"), None),
        P(("expert", "dp"), None),
        P(("expert", "dp"), None),
        P(("expert", "dp"), "context", None),
    )
    out_specs = (
        P(("expert", "dp"), "context", None),
        P(("expert", "dp"), "context", None),
        P(EVERY, None),
        P(EVERY, None),
        P(None, EVERY),
        P("dp", ("expert", "context"), None),
    )
    return jax.shard_map(
        on_device, mesh=mesh, in_specs=in_specs, out_specs=out_specs, check_vma=False
    )
```
